32 devices in a mesh: hst: 8 (over z, x), doc: 4 (over y, core).
Axes of the slice: x: 2, y: 2, z: 4, core: 2. Of those that a mesh axis runs over, the one named last changes fastest.
Arguments:
- docs: bfloat16 [262144, 768], P(('hst', 'doc')), may hold values from -400 to 400, as said below
- w_in: bfloat16 [768, 256], replicated, may hold values from -0.21875 to 0.21875
- w_out: bfloat16 [256, 64], replicated, may hold values from -0.375 to 0.375
- doc_host: int32 [262144], P(('hst', 'doc')), may hold values from 0 to 2047
- tiles: bfloat16 [2048, 128, 128], P(('hst', 'doc')), may hold values from 0 to 10, as said below
- dst_block: int32 [2048], P(('hst', 'doc')), may hold values from 0 to 15
- src_block: int32 [2048], P(('hst', 'doc')), may hold values from 0 to 127
- tile_count: int32 [32], P(('hst', 'doc')), may hold values from 1 to 64, as said below
- teleport: int32 [16384], P('hst'), may hold values 0 or 1
Outputs:
- scores: float32 [16384, 64], P(('hst', 'doc'))
The draws below stay inside these ranges and needn't reach their ends.
Inputs may be any that keep to these rules, and one draw needn't show every extreme that they name: `docs`: embeddings stay in the stated range. `tiles`: link weights are nonnegative. `tile_count`: some device uses all 64 slots.
All inputs are finite; a program needn't handle non-finite values. No bound on the sum of `teleport` on one device may be relied on, other than what follows from the above.
Results may differ from the reference program's by a relative error of at most 0.00066.
Values may be sent and summed in bfloat16 or wider, within the bound.
No kernel may reach another device: no remote copies, remote signals or barrier semaphores. Data moves between devices by JAX's collectives and lax.ppermute only.
A program may use at most 128 MiB of HBM per device.

```python
import math
import jax
import jax.numpy as jnp
import numpy as np
from jax import lax

D = 768
HID = 256
TOPICS = 64
DOC_DEV = 8192
HOST_DEV = 2048
BLOCK = 128
TILE_DEV = 64
HOPS = 3
DOCS = 262144
HOSTS = 16384
BLK_PART = 16
NBLK = 128
TILES = 2048
N_HST = 8
N_DOC = 4
DEVICES = 32


def draw_docs(key, part):
    first = jax.random.fold_in(key, 0)
    values = jnp.clip(jax.random.normal(first, (DOCS, D)), -5.0, 5.0)
    return values.astype(jnp.bfloat16)


def draw_tiles(key, part):
    value_key = jax.random.fold_in(key, 11)
    values = jax.random.uniform(value_key, (TILES, BLOCK, BLOCK), minval=0.0, maxval=1.0)
    low_end = 0.5
    high_end = 2.0
    exponent = 0.4
    row_level = jnp.exp(jax.random.uniform(jax.random.fold_in(key, 12), (TILES, BLOCK, 1), minval=jnp.log(low_end), maxval=jnp.log(high_end)))
    col_level = jnp.exp(jax.random.uniform(jax.random.fold_in(key, 13), (TILES, 1, BLOCK), minval=jnp.log(low_end), maxval=jnp.log(high_end)))
    chance = jnp.clip(row_level * col_level * 0.125, 0.0, 0.5)
    weight = jnp.maximum(values / chance, 0.01) ** (-exponent)
    weak_pick = jax.random.uniform(jax.random.fold_in(key, 14), (BLOCK,)) < 0.0625
    forced = jax.random.randint(jax.random.fold_in(key, 15), (), 0, BLOCK)
    weak_cols = jnp.logical_or(weak_pick, jnp.arange(BLOCK) == forced)
    damping = jnp.where(weak_cols, 0.001, 1.0)
    result_tiles = jnp.where(values < chance, weight, 0.0) * damping[None, None, :]
    return result_tiles.astype(jnp.bfloat16)


def draw_tile_count(key, part):
    counts = jax.random.randint(key, (DEVICES,), 1, TILE_DEV + 1)
    where = jax.random.randint(jax.random.fold_in(key, 1), (), 0, DEVICES)
    return counts.at[where].set(TILE_DEV).astype(jnp.int32)


def with_ends(result, rng, least, high):
    dims = result.shape
    spot = [jax.random.randint(jax.random.fold_in(rng, axis), (), 0, dims[axis]) for axis in range(len(dims))]
    result = result.at[tuple(spot)].set(least)
    longest = dims.index(max(dims))
    spot[longest] = (spot[longest] + 1) % dims[longest]
    return result.at[tuple(spot)].set(high)


def rank_table(number_of, lean):
    portions = [(1 << 20) // math.isqrt(grade ** lean) + 1 for grade in range(1, number_of + 1)]
    deviation = 1 + sum(portions) // (1 << 30)
    return np.cumsum(np.array([max(1, weight // deviation) for weight in portions]))


def ranked(own_key, dims, amount, slope):
    table = rank_table(amount, slope)
    lot = jax.random.randint(jax.random.fold_in(own_key, 1), dims, 0, int(table[amount - 1]))
    grade = jnp.searchsorted(jnp.asarray(table, jnp.int32), lot, side="right")
    return jax.random.permutation(jax.random.fold_in(own_key, 2), amount)[grade].astype(jnp.int32)


def scatter_about(rng, shape, width, limit, dtype=jnp.bfloat16):
    drawn = jax.random.normal(rng, shape, jnp.float32) * width
    return jnp.minimum(jnp.maximum(drawn, -limit), limit).astype(dtype)


def setup_inputs(seed: int = 0) -> dict:
    splits = jax.random.split(jax.random.key(seed), 10)
    docs = draw_docs(jax.random.fold_in(splits[9], 71), 0)
    w_in = scatter_about(splits[1], (D, HID), D ** -0.5, 0.21875)
    w_out = scatter_about(splits[2], (HID, TOPICS), HID ** -0.5, 0.375)
    doc_host = with_ends(ranked(splits[3], (DOCS,), HOST_DEV, 2), jax.random.fold_in(splits[3], 3), 0, HOST_DEV - 1).astype(jnp.int32)
    tiles = draw_tiles(jax.random.fold_in(splits[9], 71), 0)
    dst_block = with_ends(jax.random.randint(splits[5], (TILES,), 0, BLK_PART), jax.random.fold_in(splits[5], 1), 0, BLK_PART - 1).astype(jnp.int32)
    src_block = with_ends(jax.random.randint(splits[6], (TILES,), 0, NBLK), jax.random.fold_in(splits[6], 1), 0, NBLK - 1).astype(jnp.int32)
    tile_count = draw_tile_count(jax.random.fold_in(splits[9], 71), 0)
    teleport = with_ends((jax.random.randint(splits[8], (HOSTS,), 0, 4) < 1).astype(jnp.int32), jax.random.fold_in(splits[8], 1), 0, 1)
    return {"docs": docs, "w_in": w_in, "w_out": w_out, "doc_host": doc_host, "tiles": tiles, "dst_block": dst_block, "src_block": src_block, "tile_count": tile_count, "teleport": teleport}


def classify(block_docs, w_in, w_out):
    hidden = jax.nn.gelu(jnp.dot(block_docs, w_in, preferred_element_type=jnp.float32), approximate=True).astype(jnp.bfloat16)
    logits = jnp.dot(hidden, w_out, preferred_element_type=jnp.float32)
    return jax.nn.softmax(logits, axis=-1)


def reference(docs, w_in, w_out, doc_host, tiles, dst_block, src_block, tile_count, teleport):
    probs = lax.map(lambda b: classify(b, w_in, w_out), docs.reshape(DEVICES, DOC_DEV, D)).reshape(DOCS, TOPICS)
    doc_part = (jnp.arange(DOCS) // (DOC_DEV * N_DOC)).astype(jnp.int32)
    host_global = (doc_part * HOST_DEV + doc_host).astype(jnp.int32)
    host_topic = jax.ops.segment_sum(probs, host_global, num_segments=HOSTS)
    slot = jnp.arange(TILES)
    valid = ((slot % TILE_DEV) < tile_count[slot // TILE_DEV]).astype(jnp.float32)
    colsum = jnp.sum(tiles.astype(jnp.float32), axis=1) * valid[:, None]
    degree = jax.ops.segment_sum(colsum, src_block, num_segments=NBLK).reshape(HOSTS)
    inverse = 1.0 / jnp.maximum(degree, 1.0)
    member = teleport.astype(jnp.float32)[:, None]
    mass = jnp.sum(member * host_topic, axis=0)
    tele = member * host_topic / mass
    tiles_part = tiles.reshape(N_HST, TILE_DEV * N_DOC, BLOCK, BLOCK)
    dst_part = dst_block.reshape(N_HST, TILE_DEV * N_DOC)
    src_part = src_block.reshape(N_HST, TILE_DEV * N_DOC)
    valid_part = valid.reshape(N_HST, TILE_DEV * N_DOC)
    x = tele
    for hop in range(HOPS):
        sent = (x * inverse[:, None]).astype(jnp.bfloat16).reshape(NBLK, BLOCK, TOPICS)

        def part_flow(item):
            tile_set, dst, src, used = item
            slabs = sent[src].astype(jnp.float32)
            prod = jnp.einsum("kij,kjt->kit", tile_set.astype(jnp.float32), slabs, precision=lax.Precision.HIGHEST)
            prod = prod * used[:, None, None]
            return jax.ops.segment_sum(prod, dst, num_segments=BLK_PART)

        inflow = lax.map(part_flow, (tiles_part, dst_part, src_part, valid_part)).reshape(HOSTS, TOPICS)
        x = 0.85 * inflow + 0.15 * tele
    return HOSTS * x
```

```python
import functools

import jax
import jax.numpy as jnp
from jax import lax
from jax.experimental import pallas as pl
from jax.experimental.pallas import tpu as pltpu
from jax.sharding import PartitionSpec as P

HOPS = 3
DIGITS = 4
DOC_BLOCK = 1024
GROUP = 8
LIFT = 2.0**64
NT = (((1,), (1,)), ((), ()))
MIB = 1 << 20


def xor_send(value, axis, step):
    size = lax.axis_size(axis)
    return lax.ppermute(value, axis, [(i, i ^ step) for i in range(size)])


def column_sum_kernel(meta, tiles, *rest):
    outs, total = rest[:-1], rest[-1]
    step = pl.program_id(0)

    @pl.when(step == 0)
    def _():
        total[...] = jnp.zeros_like(total)

    for i in range(GROUP):
        row = meta[step * GROUP + i]
        part = jnp.sum(tiles[i].astype(jnp.float32), axis=0, keepdims=True)
        total[pl.ds(row, 1), :] += part

    @pl.when(step == pl.num_programs(0) - 1)
    def _():
        rows = outs[0].shape[0]
        for j, out in enumerate(outs):
            out[...] = total[j * rows : (j + 1) * rows, :]


def column_sums(meta, tiles, parts, rows):
    slots, block, _ = tiles.shape
    shape = jax.ShapeDtypeStruct((rows, block), jnp.float32)
    return pl.pallas_call(
        column_sum_kernel,
        grid_spec=pltpu.PrefetchScalarGridSpec(
            num_scalar_prefetch=1,
            grid=(slots // GROUP,),
            in_specs=[pl.BlockSpec((GROUP, block, block), lambda i, m: (i, 0, 0))],
            out_specs=[pl.BlockSpec((rows, block), lambda i, m: (0, 0))] * parts,
            scratch_shapes=[pltpu.VMEM((parts * rows + 8, block), jnp.float32)],
        ),
        out_shape=[shape] * parts,
        compiler_params=pltpu.CompilerParams(vmem_limit_bytes=16 * MIB),
        cost_estimate=pl.CostEstimate(
            flops=tiles.size, bytes_accessed=tiles.size * 2, transcendentals=0
        ),
        name="column_sums",
    )(meta, tiles)


def documents_kernel(place, docs, w_in, w_out, host, *rest):
    outs, w_out_t, total = rest[:-2], rest[-2], rest[-1]
    step = pl.program_id(0)
    topics = w_out.shape[1]
    width = total.shape[1]

    @pl.when(step == 0)
    def _():
        total[...] = jnp.zeros_like(total)
        w_out_t[...] = w_out[...].astype(jnp.float32).T.astype(jnp.bfloat16)

    hidden = jax.nn.gelu(
        jnp.dot(docs[...], w_in[...], preferred_element_type=jnp.float32), approximate=True
    ).astype(jnp.bfloat16)
    logits = lax.dot_general(w_out_t[...], hidden, NT, preferred_element_type=jnp.float32)
    powers = jnp.exp(logits - jnp.max(logits, axis=0, keepdims=True))
    probs = powers * (1.0 / jnp.sum(powers, axis=0, keepdims=True))
    high = probs.astype(jnp.bfloat16)
    low = (probs - high.astype(jnp.float32)).astype(jnp.bfloat16)
    index = host[0]
    digit = index // width
    within = index - digit * width
    picks = [jnp.where(digit == j, 1.0, 0.0).astype(jnp.bfloat16) for j in range(DIGITS)]
    left = jnp.concatenate([high * p for p in picks] + [low * p for p in picks], axis=0)
    places = lax.broadcasted_iota(jnp.int32, (width, index.shape[1]), 0)
    right = jnp.where(places == within, 1.0, 0.0).astype(jnp.bfloat16)
    total[...] += lax.dot_general(left, right, NT, preferred_element_type=jnp.float32)

    @pl.when(step == pl.num_programs(0) - 1)
    def _():
        per = outs[0].shape[0]
        for j, out in enumerate(outs):
            first = (place[0] ^ j) * per
            for d in range(DIGITS):
                high_rows = pl.ds(pl.multiple_of(d * topics + first, 8), per)
                low_rows = pl.ds(pl.multiple_of((DIGITS + d) * topics + first, 8), per)
                out[:, d * width : (d + 1) * width] = total[high_rows, :] + total[low_rows, :]


def document_topics(place, docs, w_in, w_out, doc_host, hosts, split):
    count, depth = docs.shape
    hid, topics = w_out.shape
    per = topics // split
    width = hosts // DIGITS
    steps = count // DOC_BLOCK
    shape = jax.ShapeDtypeStruct((per, hosts), jnp.float32)
    return pl.pallas_call(
        documents_kernel,
        grid_spec=pltpu.PrefetchScalarGridSpec(
            num_scalar_prefetch=1,
            grid=(steps,),
            in_specs=[
                pl.BlockSpec((DOC_BLOCK, depth), lambda i, m: (i, 0)),
                pl.BlockSpec((depth, hid), lambda i, m: (0, 0)),
                pl.BlockSpec((hid, topics), lambda i, m: (0, 0)),
                pl.BlockSpec((1, 1, DOC_BLOCK), lambda i, m: (i, 0, 0)),
            ],
            out_specs=[pl.BlockSpec((per, hosts), lambda i, m: (0, 0))] * split,
            scratch_shapes=[
                pltpu.VMEM((topics, hid), jnp.bfloat16),
                pltpu.VMEM((2 * DIGITS * topics, width), jnp.float32),
            ],
        ),
        out_shape=[shape] * split,
        compiler_params=pltpu.CompilerParams(vmem_limit_bytes=40 * MIB),
        cost_estimate=pl.CostEstimate(
            flops=2 * count * (depth * hid + hid * topics + 2 * topics * hosts),
            bytes_accessed=docs.size * 2,
            transcendentals=count * (hid + topics),
        ),
        name="document_topics",
    )(place, docs, w_in, w_out, doc_host.reshape(steps, 1, DOC_BLOCK))


def start_kernel(split, teleport, *rest):
    sums, degrees = rest[:split], rest[split : 2 * split]
    sent, start, inverse = rest[2 * split :]
    block = inverse.shape[1]
    degree = sum(ref[...] for ref in degrees[1:]) + degrees[0][...]
    inv = 1.0 / jnp.maximum(degree, 1.0)
    inverse[...] = inv
    member = teleport[...].astype(jnp.float32) * LIFT
    mass = jnp.zeros((start.shape[0], 1), jnp.float32)
    for b in range(inv.shape[0]):
        cols = slice(b * block, (b + 1) * block)
        value = sum(ref[:, cols] for ref in sums[1:]) + sums[0][:, cols]
        value = value * member[b : b + 1, :]
        start[:, cols] = value
        sent[:, cols] = (value * inv[b : b + 1, :]).astype(jnp.bfloat16)
        mass = mass + jnp.sum(value, axis=1, keepdims=True)
    lane = lax.broadcasted_iota(jnp.int32, (start.shape[0], block), 1)
    first = mass.astype(jnp.bfloat16).astype(jnp.float32)
    second = (mass - first).astype(jnp.bfloat16).astype(jnp.float32)
    third = mass - first - second
    pieces = jnp.where(lane == 0, first, jnp.where(lane == 1, second, jnp.where(lane == 2, third, 0.0)))
    sent[:, inv.shape[0] * block :] = pieces.astype(jnp.bfloat16)


def start_values(teleport, sums, degrees):
    per, hosts = sums[0].shape
    blocks, block = degrees[0].shape
    return pl.pallas_call(
        functools.partial(start_kernel, len(sums)),
        out_shape=[
            jax.ShapeDtypeStruct((per, hosts + block), jnp.bfloat16),
            jax.ShapeDtypeStruct((per, hosts), jnp.float32),
            jax.ShapeDtypeStruct((blocks, block), jnp.float32),
        ],
        compiler_params=pltpu.CompilerParams(vmem_limit_bytes=16 * MIB),
        name="start_values",
    )(teleport.reshape(blocks, block), *sums, *degrees)


def hop_kernel(first, last, parts, split, meta, place, *rest):
    shards, tiles = rest[:parts], rest[parts : parts + split]
    tele, inverse = rest[parts + split : parts + split + 2]
    outs, slabs, inflow = rest[parts + split + 2 : -2], rest[-2], rest[-1]
    blocks, block = inverse.shape
    slots = tiles[0].shape[0] * pl.num_programs(0)
    span = meta.shape[0] // split
    step = pl.program_id(0)

    @pl.when(step == 0)
    def _():
        inflow[...] = jnp.zeros_like(inflow)
        slabs[parts * blocks] = jnp.zeros(slabs.shape[1:], slabs.dtype)
        for j, shard in enumerate(shards):
            for b in range(blocks):
                slabs[j * blocks + b] = shard[:, b * block : (b + 1) * block]

    for q in range(split):
        base = q * span

        @pl.when(step * GROUP < meta[base + 2 * slots])
        def _():
            products = []
            for i in range(GROUP):
                slab = slabs[meta[base + step * GROUP + i]]
                products.append(
                    lax.dot_general(slab, tiles[q][i], NT, preferred_element_type=jnp.float32)
                )
            for i in range(GROUP):
                inflow[meta[base + slots + step * GROUP + i]] += products[i]

    @pl.when(step == pl.num_programs(0) - 1)
    def _():
        if first:
            mass = sum(jnp.sum(s[:, blocks * block :].astype(jnp.float32), axis=1, keepdims=True) for s in shards)
        for b in range(blocks):
            cols = slice(b * block, (b + 1) * block)
            own = tele[:, cols]
            state = 0.85 * inflow[b] + 0.15 * own
            if first:
                state = state / mass
                outs[1][:, cols] = own / mass
            if last:
                inflow[b] = state
            else:
                outs[0][:, cols] = (state * inverse[b : b + 1, :]).astype(jnp.bfloat16)
        if last:
            count = outs[0].shape[1] // block
            for j, out in enumerate(outs):
                begin = (place[0] ^ j) * count
                for i in range(count):
                    out[:, i * block : (i + 1) * block] = inflow[begin + i]


def hop(first, last, meta, place, shards, tiles, tele, inverse):
    per, hosts = tele.shape
    blocks, block = inverse.shape
    parts, split = len(shards), len(tiles)
    slots = tiles[0].shape[0]
    whole = lambda i, m, p: (0, 0)
    if last:
        out_shape = [jax.ShapeDtypeStruct((per, hosts // split), jnp.float32)] * split
    else:
        out_shape = [jax.ShapeDtypeStruct((per, hosts), jnp.bfloat16)]
        if first:
            out_shape.append(jax.ShapeDtypeStruct((per, hosts), jnp.float32))
    return pl.pallas_call(
        functools.partial(hop_kernel, first, last, parts, split),
        grid_spec=pltpu.PrefetchScalarGridSpec(
            num_scalar_prefetch=2,
            grid=(slots // GROUP,),
            in_specs=[pl.BlockSpec(s.shape, whole) for s in shards]
            + [pl.BlockSpec((GROUP, block, block), lambda i, m, p: (i, 0, 0))] * split
            + [pl.BlockSpec(tele.shape, whole), pl.BlockSpec(inverse.shape, whole)],
            out_specs=[pl.BlockSpec(s.shape, whole) for s in out_shape],
            scratch_shapes=[
                pltpu.VMEM((parts * blocks + 1, per, block), jnp.bfloat16),
                pltpu.VMEM((blocks, per, block), jnp.float32),
            ],
        ),
        out_shape=out_shape,
        compiler_params=pltpu.CompilerParams(vmem_limit_bytes=32 * MIB),
        cost_estimate=pl.CostEstimate(
            flops=2 * split * slots * block * block * per,
            bytes_accessed=split * slots * block * block * 2,
            transcendentals=0,
        ),
        name="hop",
    )(meta, place, *shards, *tiles, tele, inverse)


def finish_kernel(scale, place, *rest):
    chunks, out, whole = rest[:-2], rest[-2], rest[-1]
    per = chunks[0].shape[0]
    for j, chunk in enumerate(chunks):
        whole[pl.ds(pl.multiple_of((place[0] ^ j) * per, 8), per), :] = chunk[...] * scale
    out[...] = whole[...].T


def finish(place, chunks, scale):
    per, rows = chunks[0].shape
    topics = per * len(chunks)
    return pl.pallas_call(
        functools.partial(finish_kernel, scale),
        in_specs=[pl.BlockSpec(memory_space=pltpu.SMEM)]
        + [pl.BlockSpec(memory_space=pltpu.VMEM)] * len(chunks),
        out_shape=jax.ShapeDtypeStruct((rows, topics), jnp.float32),
        scratch_shapes=[pltpu.VMEM((topics, rows), jnp.float32)],
        compiler_params=pltpu.CompilerParams(vmem_limit_bytes=16 * MIB),
        name="finish",
    )(place, *chunks)


def body(docs, w_in, w_out, doc_host, tiles, dst_block, src_block, tile_count, teleport):
    hosts = teleport.shape[0]
    slots, block, _ = tiles.shape
    parts, split = lax.axis_size("hst"), lax.axis_size("doc")
    blocks = hosts // block
    part = lax.axis_index("hst").astype(jnp.int32)
    place = lax.axis_index("doc").astype(jnp.int32).reshape(1)

    used = jnp.arange(slots, dtype=jnp.int32) < tile_count[0]
    slab = jnp.where(used, src_block ^ (part * blocks), parts * blocks)
    meta = jnp.concatenate([slab, dst_block, jnp.broadcast_to(tile_count, (2 * slots,))])

    def over_doc(value):
        held = {0: value, 1: xor_send(value, "doc", 1)}
        for j in range(2, split, 2):
            held[j] = xor_send(value, "doc", j)
            held[j + 1] = xor_send(held[j], "doc", 1)
        return [held[j] for j in range(split)]

    all_tiles = over_doc(tiles)
    all_meta = jnp.concatenate([meta] + [xor_send(meta, "doc", j) for j in range(1, split)])

    degree = column_sums(meta, tiles, parts, blocks)
    degree = sum(xor_send(degree[j], "hst", j) for j in range(1, parts)) + degree[0]
    degrees = [degree] + [xor_send(degree, "doc", j) for j in range(1, split)]

    sums = document_topics(place, docs, w_in, w_out, doc_host, hosts, split)
    sums = [sums[0]] + [xor_send(sums[j], "doc", j) for j in range(1, split)]

    sent, tele, inverse = start_values(teleport, sums, degrees)
    for step in range(HOPS):
        shards = [sent] + [xor_send(sent, "hst", j) for j in range(1, parts)]
        first, last = step == 0, step == HOPS - 1
        outs = hop(first, last, all_meta, place, shards, all_tiles, tele, inverse)
        sent = outs[0]
        if first:
            tele = outs[1]
    chunks = [outs[0]] + [xor_send(outs[j], "doc", j) for j in range(1, split)]
    return finish(place, chunks, float(hosts * parts))


def solution(mesh):
    placed = (
        P(("hst", "doc"), None),
        P(),
        P(),
        P(("hst", "doc")),
        P(("hst", "doc"), None, None),
        P(("hst", "doc")),
        P(("hst", "doc")),
        P(("hst", "doc")),
        P("hst"),
    )
    return jax.shard_map(
        body, mesh=mesh, in_specs=placed, out_specs=P(("hst", "doc"), None), check_vma=False
    )
```

```python
import functools

import jax
import jax.numpy as jnp
from jax import lax
from jax.experimental import pallas as pl
from jax.experimental.pallas import tpu as pltpu
from jax.sharding import PartitionSpec as P

HOPS = 3
DIGITS = 4
DOC_BLOCK = 1024
GROUP = 8
TILE_GROUP = 16
LIFT = 2.0**64
NT = (((1,), (1,)), ((), ()))
MIB = 1 << 20


def xor_send(value, axis, step):
    size = lax.axis_size(axis)
    return lax.ppermute(value, axis, [(i, i ^ step) for i in range(size)])


def column_sum_kernel(meta, tiles, out, total):
    step = pl.program_id(0)

    @pl.when(step == 0)
    def _():
        total[...] = jnp.zeros_like(total)

    for i in range(GROUP):
        row = meta[step * GROUP + i]
        part = jnp.sum(tiles[i].astype(jnp.float32), axis=0, keepdims=True)
        total[pl.ds(row, 1), :] += part

    @pl.when(step == pl.num_programs(0) - 1)
    def _():
        rows = out.shape[1]
        for j in range(out.shape[0]):
            out[j] = total[j * rows : (j + 1) * rows, :]


def column_sums(meta, tiles, parts, rows):
    slots, block, _ = tiles.shape
    shape = (parts, rows, block)
    return pl.pallas_call(
        column_sum_kernel,
        grid_spec=pltpu.PrefetchScalarGridSpec(
            num_scalar_prefetch=1,
            grid=(slots // GROUP,),
            in_specs=[pl.BlockSpec((GROUP, block, block), lambda i, m: (i, 0, 0))],
            out_specs=pl.BlockSpec(shape, lambda i, m: (0, 0, 0)),
            scratch_shapes=[pltpu.VMEM((parts * rows + 8, block), jnp.float32)],
        ),
        out_shape=jax.ShapeDtypeStruct(shape, jnp.float32),
        compiler_params=pltpu.CompilerParams(vmem_limit_bytes=16 * MIB),
        cost_estimate=pl.CostEstimate(
            flops=tiles.size, bytes_accessed=tiles.size * 2, transcendentals=0
        ),
        name="column_sums",
    )(meta, tiles)


def documents_kernel(docs, w_in, w_out_t, host, degrees, labels, out, total):
    step = pl.program_id(0)
    topics = w_out_t.shape[0]
    width = total.shape[1]

    hidden = jax.nn.gelu(
        jnp.dot(docs[...], w_in[...], preferred_element_type=jnp.float32), approximate=True
    ).astype(jnp.bfloat16)
    logits = lax.dot_general(w_out_t[...], hidden, NT, preferred_element_type=jnp.float32)
    powers = jnp.exp(logits - jnp.max(logits, axis=0, keepdims=True))
    probs = powers * (1.0 / jnp.sum(powers, axis=0, keepdims=True))
    high = probs.astype(jnp.bfloat16)
    low = (probs - high.astype(jnp.float32)).astype(jnp.bfloat16)
    index = host[0]
    digit = index // width
    within = index - digit * width
    picks = [jnp.where(digit == j, 1.0, 0.0).astype(jnp.bfloat16) for j in range(DIGITS)]
    left = jnp.concatenate([high * p for p in picks] + [low * p for p in picks], axis=0)
    places = lax.broadcasted_iota(jnp.int32, (width, index.shape[1]), 0)
    right = jnp.where(places == within, 1.0, 0.0).astype(jnp.bfloat16)
    added = lax.dot_general(left, right, NT, preferred_element_type=jnp.float32)

    @pl.when(step == 0)
    def _():
        total[...] = added

    @pl.when(step > 0)
    def _():
        total[...] += added

    @pl.when(step == pl.num_programs(0) - 1)
    def _():
        split, per, _ = out.shape
        hosts = DIGITS * width
        degree = sum(degrees[j] for j in range(1, degrees.shape[0])) + degrees[0]
        blocks, block = degree.shape
        for q in range(split):
            for d in range(DIGITS):
                first = d * topics + q * per
                second = first + DIGITS * topics
                out[q, :, d * width : (d + 1) * width] = (
                    total[first : first + per, :] + total[second : second + per, :]
                )
            for c in range(blocks // per):
                cols = slice(hosts + c * block, hosts + (c + 1) * block)
                out[q, :, cols] = degree[c * per : (c + 1) * per, :]
            wide = hosts + blocks // per * block
            out[q, :, wide:] = jnp.zeros((per, labels.shape[1]), jnp.float32)
            out[q, : labels.shape[0], wide:] = labels[...].astype(jnp.float32)


def document_topics(docs, w_in, w_out, doc_host, degrees, labels, hosts, split):
    count, depth = docs.shape
    hid, topics = w_out.shape
    per = topics // split
    width = hosts // DIGITS
    steps = count // DOC_BLOCK
    shape = (split, per, hosts + hosts // per + labels.shape[1])
    return pl.pallas_call(
        documents_kernel,
        grid=(steps,),
        in_specs=[
            pl.BlockSpec((DOC_BLOCK, depth), lambda i: (i, 0)),
            pl.BlockSpec((depth, hid), lambda i: (0, 0)),
            pl.BlockSpec((topics, hid), lambda i: (0, 0)),
            pl.BlockSpec((1, 1, DOC_BLOCK), lambda i: (i, 0, 0)),
            pl.BlockSpec(degrees.shape, lambda i: (0, 0, 0)),
            pl.BlockSpec(labels.shape, lambda i: (0, 0)),
        ],
        out_specs=pl.BlockSpec(shape, lambda i: (0, 0, 0)),
        scratch_shapes=[pltpu.VMEM((2 * DIGITS * topics, width), jnp.float32)],
        out_shape=jax.ShapeDtypeStruct(shape, jnp.float32),
        compiler_params=pltpu.CompilerParams(vmem_limit_bytes=56 * MIB),
        cost_estimate=pl.CostEstimate(
            flops=2 * count * (depth * hid + hid * topics + 2 * topics * hosts),
            bytes_accessed=docs.size * 2,
            transcendentals=count * (hid + topics),
        ),
        name="document_topics",
    )(docs, w_in, w_out.T, doc_host.reshape(steps, 1, DOC_BLOCK), degrees, labels)


def start_kernel(teleport, sums, late, sent, start, inverse, late_out):
    split, per, _ = sums.shape
    hosts = start.shape[1]
    blocks, block = teleport.shape
    member = teleport[...].astype(jnp.float32) * LIFT
    mass = jnp.zeros((per, 1), jnp.float32)
    tail = slice(hosts, hosts + inverse.shape[1])
    degree = sum(sums[j, :, tail] for j in range(1, split)) + sums[0, :, tail]
    inv = 1.0 / jnp.maximum(degree, 1.0)
    inverse[...] = inv
    for b in range(blocks):
        cols = slice(b * block, (b + 1) * block)
        value = sum(sums[j, :, cols] for j in range(1, split)) + sums[0, :, cols]
        value = value * member[b : b + 1, :]
        start[:, cols] = value
        c, r = b // per, b % per
        row = inv[r : r + 1, c * block : (c + 1) * block]
        scaled = (value * row).astype(jnp.bfloat16)
        for j in range(sent.shape[0]):
            sent[j, :, cols] = scaled
        mass = mass + jnp.sum(value, axis=1, keepdims=True)
    lane = lax.broadcasted_iota(jnp.int32, (per, block), 1)
    first = mass.astype(jnp.bfloat16).astype(jnp.float32)
    second = (mass - first).astype(jnp.bfloat16).astype(jnp.float32)
    third = mass - first - second
    pieces = jnp.where(
        lane == 0, first, jnp.where(lane == 1, second, jnp.where(lane == 2, third, 0.0))
    ).astype(jnp.bfloat16)
    for j in range(sent.shape[0]):
        sent[j, :, blocks * block :] = pieces


def start_values(teleport, sums, parts, block, late):
    _, per, _ = sums.shape
    hosts = teleport.shape[0]
    vmem = pl.BlockSpec(memory_space=pltpu.VMEM)
    keep = pl.BlockSpec(memory_space=pl.ANY)
    return pl.pallas_call(
        start_kernel,
        in_specs=[vmem, vmem, keep],
        out_specs=[vmem, vmem, vmem, keep],
        out_shape=[
            jax.ShapeDtypeStruct((parts, per, hosts + block), jnp.bfloat16),
            jax.ShapeDtypeStruct((per, hosts), jnp.float32),
            jax.ShapeDtypeStruct((per, hosts // per), jnp.float32),
            jax.ShapeDtypeStruct(late.shape, late.dtype),
        ],
        input_output_aliases={2: 3},
        compiler_params=pltpu.CompilerParams(vmem_limit_bytes=16 * MIB),
        name="start_values",
    )(teleport.reshape(hosts // block, block), sums, late)


def hop_kernel(first, last, split, scale, meta, place, shards, *rest):
    tiles, (tele, inverse), outs = rest[:split], rest[split : split + 2], rest[split + 2 : -2]
    slabs, inflow = rest[-2:]
    blocks, per, block = inflow.shape
    parts = shards.shape[0]
    slots = tiles[0].shape[0] * pl.num_programs(0)
    span = meta.shape[0] // split
    step = pl.program_id(0)

    @pl.when(step == 0)
    def _():
        inflow[...] = jnp.zeros_like(inflow)
        slabs[parts * blocks] = jnp.zeros(slabs.shape[1:], slabs.dtype)
        for j in range(parts):
            for b in range(blocks):
                slabs[j * blocks + b] = shards[j, :, b * block : (b + 1) * block]

    empty = jnp.zeros((per, block), jnp.bfloat16)
    for q in range(split):
        start = (place[0] ^ q) * span
        base = start + step * TILE_GROUP

        @pl.when(step * TILE_GROUP < meta[start + 2 * slots])
        def _():
            products = []
            for c in range(0, TILE_GROUP, 4):
                held = [slabs[meta[base + c + i]] for i in range(4)]
                left = jnp.concatenate(
                    [
                        jnp.concatenate([held[0], held[1], empty, empty], axis=0),
                        jnp.concatenate([empty, empty, held[2], held[3]], axis=0),
                    ],
                    axis=1,
                )
                right = jnp.concatenate(
                    [
                        tiles[q][c : c + 2].reshape(2 * block, block),
                        tiles[q][c + 2 : c + 4].reshape(2 * block, block),
                    ],
                    axis=1,
                )
                both = lax.dot_general(left, right, NT, preferred_element_type=jnp.float32)
                for i in range(4):
                    side = (i % 2) * block
                    products.append(both[i * per : (i + 1) * per, side : side + block])
            for i in range(TILE_GROUP):
                inflow[meta[base + slots + i]] += products[i]

    @pl.when(step == pl.num_programs(0) - 1)
    def _():
        if first:
            tail = sum(shards[j, :, blocks * block :].astype(jnp.float32) for j in range(parts))
            mass = jnp.sum(tail, axis=1, keepdims=True)
        for b in range(blocks):
            cols = slice(b * block, (b + 1) * block)
            own = tele[:, cols]
            state = 0.85 * inflow[b] + 0.15 * own
            if first:
                state = state / mass
                outs[1][:, cols] = own / mass
            if last:
                count = outs[0].shape[2] // block
                into = slice((b % count) * block, (b % count + 1) * block)
                outs[0][b // count, :, into] = state * scale
            else:
                c, r = b // per, b % per
                row = inverse[r : r + 1, c * block : (c + 1) * block]
                scaled = (state * row).astype(jnp.bfloat16)
                for j in range(parts):
                    outs[0][j, :, cols] = scaled


def hop(first, last, meta, place, shards, tiles, tele, inverse):
    per, hosts = tele.shape
    slots, block, _ = tiles[0].shape
    blocks = hosts // block
    parts, split = shards.shape[0], len(tiles)
    if last:
        out_shape = [jax.ShapeDtypeStruct((split, per, hosts // split), jnp.float32)]
    else:
        out_shape = [jax.ShapeDtypeStruct((parts, per, hosts), jnp.bfloat16)]
        if first:
            out_shape.append(jax.ShapeDtypeStruct((per, hosts), jnp.float32))

    def whole(array):
        return pl.BlockSpec(array.shape, lambda i, m, p: (0,) * len(array.shape))

    return pl.pallas_call(
        functools.partial(hop_kernel, first, last, split, float(parts * hosts)),
        grid_spec=pltpu.PrefetchScalarGridSpec(
            num_scalar_prefetch=2,
            grid=(slots // TILE_GROUP,),
            in_specs=[whole(shards)]
            + [pl.BlockSpec((TILE_GROUP, block, block), lambda i, m, p: (i, 0, 0))] * split
            + [whole(tele), whole(inverse)],
            out_specs=[whole(s) for s in out_shape],
            scratch_shapes=[
                pltpu.VMEM((parts * blocks + 1, per, block), jnp.bfloat16),
                pltpu.VMEM((blocks, per, block), jnp.float32),
            ],
        ),
        out_shape=out_shape,
        compiler_params=pltpu.CompilerParams(vmem_limit_bytes=32 * MIB),
        cost_estimate=pl.CostEstimate(
            flops=2 * split * slots * block * block * per,
            bytes_accessed=split * slots * block * block * 2,
            transcendentals=0,
        ),
        name="hop",
    )(meta, place, shards, *tiles, tele, inverse)


def swap(value, axis):
    return lax.all_to_all(value, axis, split_axis=0, concat_axis=0, tiled=True)


def body(docs, w_in, w_out, doc_host, tiles, dst_block, src_block, tile_count, teleport):
    hosts = teleport.shape[0]
    slots, block, _ = tiles.shape
    topics = w_out.shape[1]
    parts, split = lax.axis_size("hst"), lax.axis_size("doc")
    blocks = hosts // block

    used = jnp.arange(slots, dtype=jnp.int32) < tile_count[0]
    slab = jnp.where(used, src_block, parts * blocks)
    meta = jnp.concatenate([slab, dst_block, jnp.broadcast_to(tile_count, (2 * slots,))])
    labels = meta.reshape(-1, block)
    place = lax.axis_index("doc").astype(jnp.int32).reshape(1)

    sets = {0: tiles, 1: xor_send(tiles, "doc", 1)}
    for j in range(2, split, 2):
        sets[j] = xor_send(tiles, "doc", j)
    degrees = swap(column_sums(meta, tiles, parts, blocks), "hst")
    sums = swap(document_topics(docs, w_in, w_out, doc_host, degrees, labels, hosts, split), "doc")
    all_meta = sums[:, : labels.shape[0], -block:].astype(jnp.int32).reshape(-1)
    sent, tele, inverse, sets[2] = start_values(teleport, sums, parts, block, sets[2])
    for j in range(2, split, 2):
        sets[j + 1] = xor_send(sets[j], "doc", 1)
    all_tiles = [sets[j] for j in range(split)]
    for step in range(HOPS):
        first, last = step == 0, step == HOPS - 1
        outs = hop(first, last, all_meta, place, swap(sent, "hst"), all_tiles, tele, inverse)
        sent = outs[0]
        if first:
            tele = outs[1]
    return swap(sent, "doc").reshape(topics, hosts // split).T


def solution(mesh):
    placed = (
        P(("hst", "doc"), None),
        P(),
        P(),
        P(("hst", "doc")),
        P(("hst", "doc"), None, None),
        P(("hst", "doc")),
        P(("hst", "doc")),
        P(("hst", "doc")),
        P("hst"),
    )
    return jax.shard_map(
        body, mesh=mesh, in_specs=placed, out_specs=P(("hst", "doc"), None), check_vma=False
    )
```

```python
import functools

import jax
import jax.numpy as jnp
from jax import lax
from jax.experimental import pallas as pl
from jax.experimental.pallas import tpu as pltpu
from jax.sharding import PartitionSpec as P

HOPS = 3
DIGITS = 4
DOC_BLOCK = 1024
GROUP = 8
TILE_GROUP = 16
LIFT = 2.0**64
NT = (((1,), (1,)), ((), ()))
MIB = 1 << 20


def xor_send(value, axis, step):
    size = lax.axis_size(axis)
    return lax.ppermute(value, axis, [(i, i ^ step) for i in range(size)])


def column_sum_kernel(source, count, tiles, out, total):
    step = pl.program_id(0)
    parts, rows, _ = out.shape

    @pl.when(step == 0)
    def _():
        total[...] = jnp.zeros_like(total)

    for i in range(GROUP):
        k = step * GROUP + i
        row = jnp.where(k < count[0], source[k], parts * rows)
        part = jnp.sum(tiles[i].astype(jnp.float32), axis=0, keepdims=True)
        total[pl.ds(row, 1), :] += part

    @pl.when(step == pl.num_programs(0) - 1)
    def _():
        for j in range(parts):
            out[j] = total[j * rows : (j + 1) * rows, :]


def column_sums(source, count, tiles, parts, rows):
    slots, block, _ = tiles.shape
    shape = (parts, rows, block)
    return pl.pallas_call(
        column_sum_kernel,
        grid_spec=pltpu.PrefetchScalarGridSpec(
            num_scalar_prefetch=2,
            grid=(slots // GROUP,),
            in_specs=[pl.BlockSpec((GROUP, block, block), lambda i, s, c: (i, 0, 0))],
            out_specs=pl.BlockSpec(shape, lambda i, s, c: (0, 0, 0)),
            scratch_shapes=[pltpu.VMEM((parts * rows + 8, block), jnp.float32)],
        ),
        out_shape=jax.ShapeDtypeStruct(shape, jnp.float32),
        compiler_params=pltpu.CompilerParams(vmem_limit_bytes=16 * MIB),
        cost_estimate=pl.CostEstimate(
            flops=tiles.size, bytes_accessed=tiles.size * 2, transcendentals=0
        ),
        name="column_sums",
    )(source, count, tiles)


def block_topics(docs, w_in, w_out_t, host, width):
    hidden = jax.nn.gelu(
        jnp.dot(docs[...], w_in[...], preferred_element_type=jnp.float32), approximate=True
    ).astype(jnp.bfloat16)
    logits = lax.dot_general(w_out_t[...], hidden, NT, preferred_element_type=jnp.float32)
    powers = jnp.exp(logits - jnp.max(logits, axis=0, keepdims=True))
    probs = powers * (1.0 / jnp.sum(powers, axis=0, keepdims=True))
    high = probs.astype(jnp.bfloat16)
    low = (probs - high.astype(jnp.float32)).astype(jnp.bfloat16)
    index = host[0]
    digit = index // width
    within = index - digit * width
    picks = [jnp.where(digit == j, 1.0, 0.0).astype(jnp.bfloat16) for j in range(DIGITS)]
    left = jnp.concatenate([high * p for p in picks] + [low * p for p in picks], axis=0)
    places = lax.broadcasted_iota(jnp.int32, (width, index.shape[1]), 0)
    right = jnp.where(places == within, 1.0, 0.0).astype(jnp.bfloat16)
    return lax.dot_general(left, right, NT, preferred_element_type=jnp.float32)


def early_documents_kernel(docs, w_in, w_out_t, host, total):
    step = pl.program_id(0)
    added = block_topics(docs, w_in, w_out_t, host, total.shape[1])

    @pl.when(step == 0)
    def _():
        total[...] = added

    @pl.when(step > 0)
    def _():
        total[...] += added


def late_documents_kernel(place, docs, w_in, w_out_t, host, carried, degrees, labels, *rest):
    outs, total = rest[:-1], rest[-1]
    step = pl.program_id(0)
    topics = w_out_t.shape[0]
    width = total.shape[1]
    added = block_topics(docs, w_in, w_out_t, host, width)

    @pl.when(step == 0)
    def _():
        total[...] = carried[...] + added

    @pl.when(step > 0)
    def _():
        total[...] += added

    @pl.when(step == pl.num_programs(0) - 1)
    def _():
        per = outs[0].shape[0]
        hosts = DIGITS * width
        degree = sum(degrees[j] for j in range(1, degrees.shape[0])) + degrees[0]
        blocks, block = degree.shape
        wide = hosts + blocks // per * block
        for j, out in enumerate(outs):
            chunk = (place[0] ^ j) * per
            for d in range(DIGITS):
                first = pl.ds(pl.multiple_of(d * topics + chunk, 8), per)
                second = pl.ds(pl.multiple_of((DIGITS + d) * topics + chunk, 8), per)
                out[:, d * width : (d + 1) * width] = total[first, :] + total[second, :]
            for c in range(blocks // per):
                cols = slice(hosts + c * block, hosts + (c + 1) * block)
                out[:, cols] = degree[c * per : (c + 1) * per, :]
            out[:, wide:] = jnp.zeros((per, block), jnp.float32)
            out[: labels.shape[0], wide:] = labels[...].astype(jnp.float32)


def documents(docs, w_in, w_out, doc_host, hosts, split, place, degree_parts, labels, ready):
    count, depth = docs.shape
    hid, topics = w_out.shape
    per = topics // split
    width = hosts // DIGITS
    steps = count // DOC_BLOCK
    half = steps // 2
    host = doc_host.reshape(steps, 1, DOC_BLOCK)
    w_out_t = w_out.T

    def specs(start):
        return [
            pl.BlockSpec((DOC_BLOCK, depth), lambda i, *_: (i + start, 0)),
            pl.BlockSpec((depth, hid), lambda i, *_: (0, 0)),
            pl.BlockSpec((topics, hid), lambda i, *_: (0, 0)),
            pl.BlockSpec((1, 1, DOC_BLOCK), lambda i, *_: (i + start, 0, 0)),
        ]

    def cost(blocks):
        rows = blocks * DOC_BLOCK
        return pl.CostEstimate(
            flops=2 * rows * (depth * hid + hid * topics + 2 * topics * hosts),
            bytes_accessed=rows * depth * 2,
            transcendentals=rows * (hid + topics),
        )

    held = (2 * DIGITS * topics, width)
    carried = pl.pallas_call(
        early_documents_kernel,
        grid=(half,),
        in_specs=specs(0),
        out_specs=pl.BlockSpec(held, lambda i: (0, 0)),
        out_shape=jax.ShapeDtypeStruct(held, jnp.float32),
        compiler_params=pltpu.CompilerParams(vmem_limit_bytes=56 * MIB),
        cost_estimate=cost(half),
        name="early_documents",
    )(docs, w_in, w_out_t, host)
    degrees = lax.all_to_all(degree_parts, "hst", split_axis=0, concat_axis=0, tiled=True)
    degrees, ready = lax.optimization_barrier((degrees, ready))
    shape = (per, hosts + hosts // per + labels.shape[1])
    sums = pl.pallas_call(
        late_documents_kernel,
        grid_spec=pltpu.PrefetchScalarGridSpec(
            num_scalar_prefetch=1,
            grid=(steps - half,),
            in_specs=specs(half)
            + [
                pl.BlockSpec(held, lambda i, p: (0, 0)),
                pl.BlockSpec(degrees.shape, lambda i, p: (0, 0, 0)),
                pl.BlockSpec(labels.shape, lambda i, p: (0, 0)),
            ],
            out_specs=[pl.BlockSpec(shape, lambda i, p: (0, 0))] * split,
            scratch_shapes=[pltpu.VMEM(held, jnp.float32)],
        ),
        out_shape=[jax.ShapeDtypeStruct(shape, jnp.float32)] * split,
        compiler_params=pltpu.CompilerParams(vmem_limit_bytes=56 * MIB),
        cost_estimate=cost(steps - half),
        name="late_documents",
    )(place, docs, w_in, w_out_t, host, carried, degrees, labels)
    return sums, ready


def start_kernel(teleport, *rest):
    sums, (sent, start, inverse, meta) = rest[:-4], rest[-4:]
    per, hosts = start.shape
    blocks, block = teleport.shape
    member = teleport[...].astype(jnp.float32) * LIFT
    mass = jnp.zeros((per, 1), jnp.float32)
    tail = slice(hosts, hosts + inverse.shape[1])
    inv = 1.0 / jnp.maximum(sum(s[:, tail] for s in sums[1:]) + sums[0][:, tail], 1.0)
    inverse[...] = inv
    rows = meta.shape[0] // len(sums)
    for j, s in enumerate(sums):
        meta[j * rows : (j + 1) * rows, :] = s[:rows, tail.stop :].astype(jnp.int32)
    for b in range(blocks):
        cols = slice(b * block, (b + 1) * block)
        value = sum(s[:, cols] for s in sums[1:]) + sums[0][:, cols]
        value = value * member[b : b + 1, :]
        start[:, cols] = value
        c, r = b // per, b % per
        row = inv[r : r + 1, c * block : (c + 1) * block]
        sent[:, cols] = (value * row).astype(jnp.bfloat16)
        mass = mass + jnp.sum(value, axis=1, keepdims=True)
    lane = lax.broadcasted_iota(jnp.int32, (per, block), 1)
    first = mass.astype(jnp.bfloat16).astype(jnp.float32)
    second = (mass - first).astype(jnp.bfloat16).astype(jnp.float32)
    third = mass - first - second
    pieces = jnp.where(
        lane == 0, first, jnp.where(lane == 1, second, jnp.where(lane == 2, third, 0.0))
    )
    sent[:, blocks * block :] = pieces.astype(jnp.bfloat16)


def start_values(teleport, sums, block, label_rows):
    per, _ = sums[0].shape
    hosts = teleport.shape[0]
    vmem = pl.BlockSpec(memory_space=pltpu.VMEM)
    return pl.pallas_call(
        start_kernel,
        in_specs=[vmem] * (1 + len(sums)),
        out_specs=[vmem] * 4,
        out_shape=[
            jax.ShapeDtypeStruct((per, hosts + block), jnp.bfloat16),
            jax.ShapeDtypeStruct((per, hosts), jnp.float32),
            jax.ShapeDtypeStruct((per, hosts // per), jnp.float32),
            jax.ShapeDtypeStruct((len(sums) * label_rows, block), jnp.int32),
        ],
        compiler_params=pltpu.CompilerParams(vmem_limit_bytes=16 * MIB),
        name="start_values",
    )(teleport.reshape(hosts // block, block), *sums)


def hop_kernel(first, last, parts, split, scale, meta, here, *rest):
    shards, tiles = rest[:parts], rest[parts : parts + split]
    tele, inverse = rest[parts + split : parts + split + 2]
    outs, slabs, inflow = rest[parts + split + 2 : -2], rest[-2], rest[-1]
    blocks, per, block = inflow.shape
    slots = tiles[0].shape[0] * pl.num_programs(0)
    rows = meta.shape[0] // split
    step = pl.program_id(0)

    @pl.when(step == 0)
    def _():
        inflow[...] = jnp.zeros_like(inflow)
        slabs[parts * blocks] = jnp.zeros(slabs.shape[1:], slabs.dtype)
        for j, shard in enumerate(shards):
            for b in range(blocks):
                slabs[j * blocks + b] = shard[:, b * block : (b + 1) * block]

    empty = jnp.zeros((per, block), jnp.bfloat16)
    for q in range(split):
        count = meta[q * rows + 1, 0]

        @pl.when(step * TILE_GROUP < count)
        def _():
            products = []
            for c in range(0, TILE_GROUP, 4):
                held = []
                for i in range(4):
                    k = step * TILE_GROUP + c + i
                    source = meta[q * rows, k] ^ here[0]
                    held.append(slabs[jnp.where(k < count, source, parts * blocks)])
                left = jnp.concatenate(
                    [
                        jnp.concatenate([held[0], held[1], empty, empty], axis=0),
                        jnp.concatenate([empty, empty, held[2], held[3]], axis=0),
                    ],
                    axis=1,
                )
                right = jnp.concatenate(
                    [
                        tiles[q][c : c + 2].reshape(2 * block, block),
                        tiles[q][c + 2 : c + 4].reshape(2 * block, block),
                    ],
                    axis=1,
                )
                both = lax.dot_general(left, right, NT, preferred_element_type=jnp.float32)
                for i in range(4):
                    side = (i % 2) * block
                    products.append(both[i * per : (i + 1) * per, side : side + block])
            for i in range(TILE_GROUP):
                inflow[meta[q * rows, slots + step * TILE_GROUP + i]] += products[i]

    @pl.when(step == pl.num_programs(0) - 1)
    def _():
        if first:
            tail = sum(s[:, blocks * block :].astype(jnp.float32) for s in shards)
            mass = jnp.sum(tail, axis=1, keepdims=True)
        for b in range(blocks):
            cols = slice(b * block, (b + 1) * block)
            own = tele[:, cols]
            state = 0.85 * inflow[b] + 0.15 * own
            if first:
                state = state / mass
                outs[1][:, cols] = own / mass
            if last:
                inflow[b] = state * scale
            else:
                c, r = b // per, b % per
                row = inverse[r : r + 1, c * block : (c + 1) * block]
                outs[0][:, cols] = (state * row).astype(jnp.bfloat16)
        if last:
            count = outs[0].shape[1] // block
            for j, out in enumerate(outs):
                begin = (here[1] ^ j) * count
                for i in range(count):
                    out[:, i * block : (i + 1) * block] = inflow[begin + i]


def hop(first, last, meta, here, shards, tiles, tele, inverse):
    per, hosts = tele.shape
    slots, block, _ = tiles[0].shape
    blocks = hosts // block
    parts, split = len(shards), len(tiles)
    if last:
        out_shape = [jax.ShapeDtypeStruct((per, hosts // split), jnp.float32)] * split
    else:
        out_shape = [jax.ShapeDtypeStruct((per, hosts), jnp.bfloat16)]
        if first:
            out_shape.append(jax.ShapeDtypeStruct((per, hosts), jnp.float32))

    def whole(array):
        return pl.BlockSpec(array.shape, lambda i, m, p: (0,) * len(array.shape))

    return pl.pallas_call(
        functools.partial(hop_kernel, first, last, parts, split, float(parts * hosts)),
        grid_spec=pltpu.PrefetchScalarGridSpec(
            num_scalar_prefetch=2,
            grid=(slots // TILE_GROUP,),
            in_specs=[whole(s) for s in shards]
            + [pl.BlockSpec((TILE_GROUP, block, block), lambda i, m, p: (i, 0, 0))] * split
            + [whole(tele), whole(inverse)],
            out_specs=[whole(s) for s in out_shape],
            scratch_shapes=[
                pltpu.VMEM((parts * blocks + 1, per, block), jnp.bfloat16),
                pltpu.VMEM((blocks, per, block), jnp.float32),
            ],
        ),
        out_shape=out_shape,
        compiler_params=pltpu.CompilerParams(vmem_limit_bytes=32 * MIB),
        cost_estimate=pl.CostEstimate(
            flops=2 * split * slots * block * block * per,
            bytes_accessed=split * slots * block * block * 2,
            transcendentals=0,
        ),
        name="hop",
    )(meta, here, *shards, *tiles, tele, inverse)


def finish_kernel(here, *rest):
    chunks, out = rest[:-1], rest[-1]
    per = chunks[0].shape[0]
    for j, chunk in enumerate(chunks):
        out[pl.ds(pl.multiple_of((here[1] ^ j) * per, 8), per), :] = chunk[...]


def finish(here, chunks):
    per, rows = chunks[0].shape
    topics = per * len(chunks)
    return pl.pallas_call(
        finish_kernel,
        in_specs=[pl.BlockSpec(memory_space=pltpu.SMEM)]
        + [pl.BlockSpec(memory_space=pltpu.VMEM)] * len(chunks),
        out_shape=jax.ShapeDtypeStruct((topics, rows), jnp.float32),
        compiler_params=pltpu.CompilerParams(vmem_limit_bytes=16 * MIB),
        name="finish",
    )(here, *chunks)


def spread(sent, axis):
    held = {0: sent}
    for j in range(2, lax.axis_size(axis), 2):
        held[j] = xor_send(sent, axis, j)
    for j in range(0, lax.axis_size(axis), 2):
        held[j + 1] = xor_send(held[j], axis, 1)
    return [held[j] for j in range(len(held))]


def body(docs, w_in, w_out, doc_host, tiles, dst_block, src_block, tile_count, teleport):
    hosts = teleport.shape[0]
    slots, block, _ = tiles.shape
    parts, split = lax.axis_size("hst"), lax.axis_size("doc")
    blocks = hosts // block
    place = lax.axis_index("doc").astype(jnp.int32)
    here = jnp.stack([lax.axis_index("hst").astype(jnp.int32) * blocks, place])
    labels = jnp.concatenate([src_block, dst_block, jnp.broadcast_to(tile_count, (2 * slots,))])
    labels = labels.reshape(-1, block)

    sets = {0: tiles, 1: xor_send(tiles, "doc", 1)}
    for j in range(2, split, 2):
        sets[j] = xor_send(tiles, "doc", j)
    degree_parts = column_sums(src_block, tile_count, tiles, parts, blocks)
    sums, sets[1] = documents(
        docs, w_in, w_out, doc_host, hosts, split, place.reshape(1), degree_parts, labels, sets[1]
    )
    sums = [sums[0]] + [xor_send(sums[j], "doc", j) for j in range(1, split)]
    sent, tele, inverse, meta = start_values(teleport, sums, block, labels.shape[0])
    for step in range(HOPS):
        first, last = step == 0, step == HOPS - 1
        shards = spread(sent, "hst")
        if first:
            for j in range(2, split, 2):
                sets[j], *shards[1:-1] = lax.optimization_barrier((sets[j], *shards[1:-1]))
                sets[j + 1] = xor_send(sets[j], "doc", 1)
            all_tiles = [sets[j] for j in range(split)]
        outs = hop(first, last, meta, here, shards, all_tiles, tele, inverse)
        sent = outs[0]
        if first:
            tele = outs[1]
    chunks = [outs[0]] + [xor_send(outs[j], "doc", j) for j in range(1, split)]
    return finish(here, chunks).T


def solution(mesh):
    placed = (
        P(("hst", "doc"), None),
        P(),
        P(),
        P(("hst", "doc")),
        P(("hst", "doc"), None, None),
        P(("hst", "doc")),
        P(("hst", "doc")),
        P(("hst", "doc")),
        P("hst"),
    )
    return jax.shard_map(
        body, mesh=mesh, in_specs=placed, out_specs=P(("hst", "doc"), None), check_vma=False
    )
```

```python
import functools

import jax
import jax.numpy as jnp
from jax import lax
from jax.experimental import pallas as pl
from jax.experimental.pallas import tpu as pltpu
from jax.sharding import PartitionSpec as P

HOPS = 3
LABELS = 3
DIGITS = 4
DOC_BLOCK = 1024
GROUP = 8
TILE_GROUP = 16
EARLY_TILES = 48
LIFT = 2.0**64
NT = (((1,), (1,)), ((), ()))
MIB = 1 << 20


def xor_send(value, axis, step):
    size = lax.axis_size(axis)
    return lax.ppermute(value, axis, [(i, i ^ step) for i in range(size)])


def column_sum_kernel(source, count, tiles, out, total):
    step = pl.program_id(0)
    parts, rows, _ = out.shape

    @pl.when(step == 0)
    def _():
        total[...] = jnp.zeros_like(total)

    for i in range(GROUP):
        k = step * GROUP + i
        row = jnp.where(k < count[0], source[k], parts * rows)
        part = jnp.sum(tiles[i].astype(jnp.float32), axis=0, keepdims=True)
        total[pl.ds(row, 1), :] += part

    @pl.when(step == pl.num_programs(0) - 1)
    def _():
        for j in range(parts):
            out[j] = total[j * rows : (j + 1) * rows, :]


def column_sums(source, count, tiles, parts, rows):
    slots, block, _ = tiles.shape
    shape = (parts, rows, block)
    return pl.pallas_call(
        column_sum_kernel,
        grid_spec=pltpu.PrefetchScalarGridSpec(
            num_scalar_prefetch=2,
            grid=(slots // GROUP,),
            in_specs=[pl.BlockSpec((GROUP, block, block), lambda i, s, c: (i, 0, 0))],
            out_specs=pl.BlockSpec(shape, lambda i, s, c: (0, 0, 0)),
            scratch_shapes=[pltpu.VMEM((parts * rows + 8, block), jnp.float32)],
        ),
        out_shape=jax.ShapeDtypeStruct(shape, jnp.float32),
        compiler_params=pltpu.CompilerParams(vmem_limit_bytes=56 * MIB),
        cost_estimate=pl.CostEstimate(
            flops=tiles.size, bytes_accessed=tiles.size * 2, transcendentals=0
        ),
        name="column_sums",
    )(source, count, tiles)


def block_topics(docs, w_in, w_out_t, host, width):
    hidden = jax.nn.gelu(
        jnp.dot(docs[...], w_in[...], preferred_element_type=jnp.float32), approximate=True
    ).astype(jnp.bfloat16)
    logits = lax.dot_general(w_out_t[...], hidden, NT, preferred_element_type=jnp.float32)
    powers = jnp.exp(logits - jnp.max(logits, axis=0, keepdims=True))
    probs = powers * (1.0 / jnp.sum(powers, axis=0, keepdims=True))
    high = probs.astype(jnp.bfloat16)
    low = (probs - high.astype(jnp.float32)).astype(jnp.bfloat16)
    index = host[0]
    digit = index // width
    within = index - digit * width
    picks = [jnp.where(digit == j, 1.0, 0.0).astype(jnp.bfloat16) for j in range(DIGITS)]
    left = jnp.concatenate([high * p for p in picks] + [low * p for p in picks], axis=0)
    places = lax.broadcasted_iota(jnp.int32, (width, index.shape[1]), 0)
    right = jnp.where(places == within, 1.0, 0.0).astype(jnp.bfloat16)
    return lax.dot_general(left, right, NT, preferred_element_type=jnp.float32)


def early_documents_kernel(docs, w_in, w_out_t, host, total):
    step = pl.program_id(0)
    added = block_topics(docs, w_in, w_out_t, host, total.shape[1])

    @pl.when(step == 0)
    def _():
        total[...] = added

    @pl.when(step > 0)
    def _():
        total[...] += added


def late_documents_kernel(place, docs, w_in, w_out_t, host, carried, degrees, *rest):
    labels, outs, total = rest[:LABELS], rest[LABELS:-1], rest[-1]
    step = pl.program_id(0)
    topics = w_out_t.shape[0]
    width = total.shape[1]
    added = block_topics(docs, w_in, w_out_t, host, width)

    @pl.when(step == 0)
    def _():
        total[...] = carried[...] + added

    @pl.when(step > 0)
    def _():
        total[...] += added

    @pl.when(step == pl.num_programs(0) - 1)
    def _():
        per = outs[0].shape[0]
        hosts = DIGITS * width
        degree = sum(degrees[j] for j in range(1, degrees.shape[0])) + degrees[0]
        blocks, block = degree.shape
        wide = hosts + blocks // per * block
        for j, out in enumerate(outs):
            chunk = (place[0] ^ j) * per
            for d in range(DIGITS):
                first = pl.ds(pl.multiple_of(d * topics + chunk, 8), per)
                second = pl.ds(pl.multiple_of((DIGITS + d) * topics + chunk, 8), per)
                out[:, d * width : (d + 1) * width] = total[first, :] + total[second, :]
            for c in range(blocks // per):
                cols = slice(hosts + c * block, hosts + (c + 1) * block)
                out[:, cols] = degree[c * per : (c + 1) * per, :]
            out[:, wide:] = jnp.zeros((per, block), jnp.float32)
            for r, label in enumerate(labels):
                out[r : r + 1, wide : wide + label.shape[1]] = label[...].astype(jnp.float32)


def documents(docs, w_in, w_out, doc_host, hosts, split, place, degree_parts, labels, ready):
    count, depth = docs.shape
    hid, topics = w_out.shape
    per = topics // split
    width = hosts // DIGITS
    steps = count // DOC_BLOCK
    half = steps // 2
    host = doc_host.reshape(steps, 1, DOC_BLOCK)
    w_out_t = w_out.T

    def specs(start):
        return [
            pl.BlockSpec((DOC_BLOCK, depth), lambda i, *_: (i + start, 0)),
            pl.BlockSpec((depth, hid), lambda i, *_: (0, 0)),
            pl.BlockSpec((topics, hid), lambda i, *_: (0, 0)),
            pl.BlockSpec((1, 1, DOC_BLOCK), lambda i, *_: (i + start, 0, 0)),
        ]

    def cost(blocks):
        rows = blocks * DOC_BLOCK
        return pl.CostEstimate(
            flops=2 * rows * (depth * hid + hid * topics + 2 * topics * hosts),
            bytes_accessed=rows * depth * 2,
            transcendentals=rows * (hid + topics),
        )

    held = (2 * DIGITS * topics, width)
    carried = pl.pallas_call(
        early_documents_kernel,
        grid=(half,),
        in_specs=specs(0),
        out_specs=pl.BlockSpec(held, lambda i: (0, 0)),
        out_shape=jax.ShapeDtypeStruct(held, jnp.float32),
        compiler_params=pltpu.CompilerParams(vmem_limit_bytes=50 * MIB),
        cost_estimate=cost(half),
        name="early_documents",
    )(docs, w_in, w_out_t, host)
    degrees = lax.all_to_all(degree_parts, "hst", split_axis=0, concat_axis=0, tiled=True)
    degrees, ready = lax.optimization_barrier((degrees, ready))
    shape = (per, hosts + hosts // per + degrees.shape[2])
    sums = pl.pallas_call(
        late_documents_kernel,
        grid_spec=pltpu.PrefetchScalarGridSpec(
            num_scalar_prefetch=1,
            grid=(steps - half,),
            in_specs=specs(half)
            + [
                pl.BlockSpec(held, lambda i, p: (0, 0)),
                pl.BlockSpec(degrees.shape, lambda i, p: (0, 0, 0)),
            ]
            + [pl.BlockSpec(label.shape, lambda i, p: (0, 0)) for label in labels],
            out_specs=[pl.BlockSpec(shape, lambda i, p: (0, 0))] * split,
            scratch_shapes=[pltpu.VMEM(held, jnp.float32)],
        ),
        out_shape=[jax.ShapeDtypeStruct(shape, jnp.float32)] * split,
        compiler_params=pltpu.CompilerParams(vmem_limit_bytes=50 * MIB),
        cost_estimate=cost(steps - half),
        name="late_documents",
    )(place, docs, w_in, w_out_t, host, carried, degrees, *labels)
    return sums, ready


def start_kernel(teleport, *rest):
    sums, (sent, start, inverse, meta) = rest[:-4], rest[-4:]
    per, hosts = start.shape
    blocks, block = teleport.shape
    member = teleport[...].astype(jnp.float32) * LIFT
    mass = jnp.zeros((per, 1), jnp.float32)
    tail = slice(hosts, hosts + inverse.shape[1])
    inv = 1.0 / jnp.maximum(sum(s[:, tail] for s in sums[1:]) + sums[0][:, tail], 1.0)
    inverse[...] = inv
    for j, s in enumerate(sums):
        meta[j * LABELS : (j + 1) * LABELS, :] = s[:LABELS, tail.stop :].astype(jnp.int32)
    for b in range(blocks):
        cols = slice(b * block, (b + 1) * block)
        value = sum(s[:, cols] for s in sums[1:]) + sums[0][:, cols]
        value = value * member[b : b + 1, :]
        start[:, cols] = value
        c, r = b // per, b % per
        row = inv[r : r + 1, c * block : (c + 1) * block]
        sent[:, cols] = (value * row).astype(jnp.bfloat16)
        mass = mass + jnp.sum(value, axis=1, keepdims=True)
    lane = lax.broadcasted_iota(jnp.int32, (per, block), 1)
    first = mass.astype(jnp.bfloat16).astype(jnp.float32)
    second = (mass - first).astype(jnp.bfloat16).astype(jnp.float32)
    third = mass - first - second
    pieces = jnp.where(
        lane == 0, first, jnp.where(lane == 1, second, jnp.where(lane == 2, third, 0.0))
    )
    sent[:, blocks * block :] = pieces.astype(jnp.bfloat16)


def start_values(teleport, sums, block):
    per, _ = sums[0].shape
    hosts = teleport.shape[0]
    vmem = pl.BlockSpec(memory_space=pltpu.VMEM)
    return pl.pallas_call(
        start_kernel,
        in_specs=[vmem] * (1 + len(sums)),
        out_specs=[vmem] * 4,
        out_shape=[
            jax.ShapeDtypeStruct((per, hosts + block), jnp.bfloat16),
            jax.ShapeDtypeStruct((per, hosts), jnp.float32),
            jax.ShapeDtypeStruct((per, hosts // per), jnp.float32),
            jax.ShapeDtypeStruct((len(sums) * LABELS, block), jnp.int32),
        ],
        compiler_params=pltpu.CompilerParams(vmem_limit_bytes=16 * MIB),
        name="start_values",
    )(teleport.reshape(hosts // block, block), *sums)


def hop_kernel(first, last, parts, spans, scale, meta, here, *rest):
    shards, rest = rest[:parts], rest[parts:]
    chunks, rest = rest[: len(spans)], rest[len(spans) :]
    (tele, inverse), outs, (slabs, inflow) = rest[:2], rest[2:-2], rest[-2:]
    blocks, per, block = inflow.shape
    step = pl.program_id(0)

    @pl.when(step == 0)
    def _():
        inflow[...] = jnp.zeros_like(inflow)
        slabs[parts * blocks] = jnp.zeros(slabs.shape[1:], slabs.dtype)
        for j, shard in enumerate(shards):
            for b in range(blocks):
                slabs[j * blocks + b] = shard[:, b * block : (b + 1) * block]

    empty = jnp.zeros((per, block), jnp.bfloat16)
    for tiles, (q, begin, end) in zip(chunks, spans):
        count = meta[q * LABELS + 2, 0]
        within = jnp.logical_and(step >= begin, step < end)

        @pl.when(jnp.logical_and(within, step * TILE_GROUP < count))
        def _():
            products = []
            for c in range(0, TILE_GROUP, 4):
                held = []
                for i in range(4):
                    k = step * TILE_GROUP + c + i
                    source = meta[q * LABELS, k] ^ here[0]
                    held.append(slabs[jnp.where(k < count, source, parts * blocks)])
                left = jnp.concatenate(
                    [
                        jnp.concatenate([held[0], held[1], empty, empty], axis=0),
                        jnp.concatenate([empty, empty, held[2], held[3]], axis=0),
                    ],
                    axis=1,
                )
                right = jnp.concatenate(
                    [
                        tiles[c : c + 2].reshape(2 * block, block),
                        tiles[c + 2 : c + 4].reshape(2 * block, block),
                    ],
                    axis=1,
                )
                both = lax.dot_general(left, right, NT, preferred_element_type=jnp.float32)
                for i in range(4):
                    side = (i % 2) * block
                    products.append(both[i * per : (i + 1) * per, side : side + block])
            for i in range(TILE_GROUP):
                inflow[meta[q * LABELS + 1, step * TILE_GROUP + i]] += products[i]

    @pl.when(step == pl.num_programs(0) - 1)
    def _():
        if first:
            tail = sum(s[:, blocks * block :].astype(jnp.float32) for s in shards)
            mass = jnp.sum(tail, axis=1, keepdims=True)
        for b in range(blocks):
            cols = slice(b * block, (b + 1) * block)
            own = tele[:, cols]
            state = 0.85 * inflow[b] + 0.15 * own
            if first:
                state = state / mass
                outs[1][:, cols] = own / mass
            if last:
                inflow[b] = state * scale
            else:
                c, r = b // per, b % per
                row = inverse[r : r + 1, c * block : (c + 1) * block]
                outs[0][:, cols] = (state * row).astype(jnp.bfloat16)
        if last:
            count = outs[0].shape[1] // block
            for j, out in enumerate(outs):
                begin = (here[1] ^ j) * count
                for i in range(count):
                    out[:, i * block : (i + 1) * block] = inflow[begin + i]


def hop(first, last, meta, here, shards, sets, tele, inverse):
    per, hosts = tele.shape
    slots = sum(chunk.shape[0] for chunk in sets[0])
    block = sets[0][0].shape[1]
    blocks = hosts // block
    parts, split = len(shards), len(sets)
    chunks, spans = [], []
    for q, held in enumerate(sets):
        begin = 0
        for chunk in held:
            end = begin + chunk.shape[0] // TILE_GROUP
            chunks.append(chunk)
            spans.append((q, begin, end))
            begin = end

    def stream(span):
        _, begin, end = span
        return pl.BlockSpec(
            (TILE_GROUP, block, block),
            lambda i, m, p: (jnp.clip(i - begin, 0, end - begin - 1), 0, 0),
        )

    if last:
        out_shape = [jax.ShapeDtypeStruct((per, hosts // split), jnp.float32)] * split
    else:
        out_shape = [jax.ShapeDtypeStruct((per, hosts), jnp.bfloat16)]
        if first:
            out_shape.append(jax.ShapeDtypeStruct((per, hosts), jnp.float32))

    def whole(array):
        return pl.BlockSpec(array.shape, lambda i, m, p: (0,) * len(array.shape))

    return pl.pallas_call(
        functools.partial(hop_kernel, first, last, parts, spans, float(parts * hosts)),
        grid_spec=pltpu.PrefetchScalarGridSpec(
            num_scalar_prefetch=2,
            grid=(slots // TILE_GROUP,),
            in_specs=[whole(s) for s in shards]
            + [stream(span) for span in spans]
            + [whole(tele), whole(inverse)],
            out_specs=[whole(s) for s in out_shape],
            scratch_shapes=[
                pltpu.VMEM((parts * blocks + 1, per, block), jnp.bfloat16),
                pltpu.VMEM((blocks, per, block), jnp.float32),
            ],
        ),
        out_shape=out_shape,
        compiler_params=pltpu.CompilerParams(vmem_limit_bytes=16 * MIB),
        cost_estimate=pl.CostEstimate(
            flops=2 * split * slots * block * block * per,
            bytes_accessed=split * slots * block * block * 2,
            transcendentals=0,
        ),
        name="hop",
    )(meta, here, *shards, *chunks, tele, inverse)


def finish_kernel(here, *rest):
    chunks, out = rest[:-1], rest[-1]
    per = chunks[0].shape[0]
    for j, chunk in enumerate(chunks):
        out[pl.ds(pl.multiple_of((here[1] ^ j) * per, 8), per), :] = chunk[...]


def finish(here, chunks):
    per, rows = chunks[0].shape
    topics = per * len(chunks)
    return pl.pallas_call(
        finish_kernel,
        in_specs=[pl.BlockSpec(memory_space=pltpu.SMEM)]
        + [pl.BlockSpec(memory_space=pltpu.VMEM)] * len(chunks),
        out_shape=jax.ShapeDtypeStruct((topics, rows), jnp.float32),
        compiler_params=pltpu.CompilerParams(vmem_limit_bytes=16 * MIB),
        name="finish",
    )(here, *chunks)


def spread(sent, axis):
    held = {0: sent}
    for j in range(2, lax.axis_size(axis), 2):
        held[j] = xor_send(sent, axis, j)
    for j in range(0, lax.axis_size(axis), 2):
        held[j + 1] = xor_send(held[j], axis, 1)
    return [held[j] for j in range(len(held))]


def body(docs, w_in, w_out, doc_host, tiles, dst_block, src_block, tile_count, teleport):
    hosts = teleport.shape[0]
    slots, block, _ = tiles.shape
    parts, split = lax.axis_size("hst"), lax.axis_size("doc")
    blocks = hosts // block
    place = lax.axis_index("doc").astype(jnp.int32)
    here = jnp.stack([lax.axis_index("hst").astype(jnp.int32) * blocks, place])
    labels = [label.reshape(1, -1) for label in (src_block, dst_block, tile_count)]

    near = xor_send(tiles, "doc", 1)
    cut = slots * EARLY_TILES // 64
    early, late = tiles[:cut], tiles[cut:]
    far = {j: [xor_send(early, "doc", j)] for j in range(2, split, 2)}
    degree_parts = column_sums(src_block, tile_count, tiles, parts, blocks)
    sums, near = documents(
        docs, w_in, w_out, doc_host, hosts, split, place.reshape(1), degree_parts, labels, near
    )
    sums = [sums[0]] + [xor_send(sums[j], "doc", j) for j in range(1, split)]
    sums, late, far = lax.optimization_barrier((sums, late, far))
    for j in range(2, split, 2):
        far[j].append(xor_send(late, "doc", j))
        far[j + 1] = [xor_send(far[j][0], "doc", 1)]
    sent, tele, inverse, meta = start_values(teleport, sums, block)
    for step in range(HOPS):
        first, last = step == 0, step == HOPS - 1
        shards = spread(sent, "hst")
        if first:
            for j in range(2, split, 2):
                far[j][1], *shards[1:-1] = lax.optimization_barrier((far[j][1], *shards[1:-1]))
                far[j + 1].append(xor_send(far[j][1], "doc", 1))
            sets = [[tiles], [near]] + [far[j] for j in range(2, split)]
        outs = hop(first, last, meta, here, shards, sets, tele, inverse)
        sent = outs[0]
        if first:
            tele = outs[1]
    chunks = [outs[0]] + [xor_send(outs[j], "doc", j) for j in range(1, split)]
    return finish(here, chunks).T


def solution(mesh):
    placed = (
        P(("hst", "doc"), None),
        P(),
        P(),
        P(("hst", "doc")),
        P(("hst", "doc"), None, None),
        P(("hst", "doc")),
        P(("hst", "doc")),
        P(("hst", "doc")),
        P("hst"),
    )
    return jax.shard_map(
        body, mesh=mesh, in_specs=placed, out_specs=P(("hst", "doc"), None), check_vma=False
    )
```

```python
import functools

import jax
import jax.numpy as jnp
from jax import lax
from jax.experimental import pallas as pl
from jax.experimental.pallas import tpu as pltpu
from jax.sharding import PartitionSpec as P

HOPS = 3
LABELS = 3
DIGITS = 4
DOC_BLOCK = 1024
GROUP = 8
TILE_GROUP = 16
EARLY_TILES = 48
LIFT = 2.0**64
NT = (((1,), (1,)), ((), ()))
MIB = 1 << 20


def xor_send(value, axis, step):
    size = lax.axis_size(axis)
    return lax.ppermute(value, axis, [(i, i ^ step) for i in range(size)])


def column_sum_kernel(cut, source, count, tiles, out, early, late, total):
    step = pl.program_id(0)
    parts, rows, _ = out.shape

    @pl.when(step == 0)
    def _():
        total[...] = jnp.zeros_like(total)

    @pl.when(step < cut)
    def _():
        early[...] = tiles[...]

    @pl.when(step >= cut)
    def _():
        late[...] = tiles[...]

    for i in range(TILE_GROUP):
        k = step * TILE_GROUP + i
        row = jnp.where(k < count[0], source[k], parts * rows)
        part = jnp.sum(tiles[i].astype(jnp.float32), axis=0, keepdims=True)
        total[pl.ds(row, 1), :] += part

    @pl.when(step == pl.num_programs(0) - 1)
    def _():
        for j in range(parts):
            out[j] = total[j * rows : (j + 1) * rows, :]


def column_sums(source, count, tiles, parts, rows):
    slots, block, _ = tiles.shape
    shape = (parts, rows, block)
    steps = slots // TILE_GROUP
    cut = steps * EARLY_TILES // 64
    group = (TILE_GROUP, block, block)
    return pl.pallas_call(
        functools.partial(column_sum_kernel, cut),
        grid_spec=pltpu.PrefetchScalarGridSpec(
            num_scalar_prefetch=2,
            grid=(steps,),
            in_specs=[pl.BlockSpec(group, lambda i, s, c: (i, 0, 0))],
            out_specs=[
                pl.BlockSpec(shape, lambda i, s, c: (0, 0, 0)),
                pl.BlockSpec(group, lambda i, s, c: (jnp.minimum(i, cut - 1), 0, 0)),
                pl.BlockSpec(group, lambda i, s, c: (jnp.maximum(i - cut, 0), 0, 0)),
            ],
            scratch_shapes=[pltpu.VMEM((parts * rows + 8, block), jnp.float32)],
        ),
        out_shape=[
            jax.ShapeDtypeStruct(shape, jnp.float32),
            jax.ShapeDtypeStruct((cut * TILE_GROUP, block, block), tiles.dtype),
            jax.ShapeDtypeStruct(((steps - cut) * TILE_GROUP, block, block), tiles.dtype),
        ],
        compiler_params=pltpu.CompilerParams(vmem_limit_bytes=16 * MIB),
        cost_estimate=pl.CostEstimate(
            flops=tiles.size, bytes_accessed=tiles.size * 4, transcendentals=0
        ),
        name="column_sums",
    )(source, count, tiles)


def block_topics(docs, w_in, w_out_t, host, width):
    hidden = jax.nn.gelu(
        jnp.dot(docs[...], w_in[...], preferred_element_type=jnp.float32), approximate=True
    ).astype(jnp.bfloat16)
    logits = lax.dot_general(w_out_t[...], hidden, NT, preferred_element_type=jnp.float32)
    powers = jnp.exp(logits - jnp.max(logits, axis=0, keepdims=True))
    probs = powers * (1.0 / jnp.sum(powers, axis=0, keepdims=True))
    high = probs.astype(jnp.bfloat16)
    low = (probs - high.astype(jnp.float32)).astype(jnp.bfloat16)
    index = host[0]
    digit = index // width
    within = index - digit * width
    picks = [jnp.where(digit == j, 1.0, 0.0).astype(jnp.bfloat16) for j in range(DIGITS)]
    left = jnp.concatenate([high * p for p in picks] + [low * p for p in picks], axis=0)
    places = lax.broadcasted_iota(jnp.int32, (width, index.shape[1]), 0)
    right = jnp.where(places == within, 1.0, 0.0).astype(jnp.bfloat16)
    return lax.dot_general(left, right, NT, preferred_element_type=jnp.float32)


def documents_kernel(place, docs, w_in, w_out_t, host, *rest):
    labels, outs, total = rest[:LABELS], rest[LABELS:-1], rest[-1]
    step = pl.program_id(0)
    topics = w_out_t.shape[0]
    width = total.shape[1]
    added = block_topics(docs, w_in, w_out_t, host, width)

    @pl.when(step == 0)
    def _():
        total[...] = added

    @pl.when(step > 0)
    def _():
        total[...] += added

    @pl.when(step == pl.num_programs(0) - 1)
    def _():
        per = outs[0].shape[0]
        hosts = DIGITS * width
        for j, out in enumerate(outs):
            chunk = (place[0] ^ j) * per
            for d in range(DIGITS):
                first = pl.ds(pl.multiple_of(d * topics + chunk, 8), per)
                second = pl.ds(pl.multiple_of((DIGITS + d) * topics + chunk, 8), per)
                out[:, d * width : (d + 1) * width] = total[first, :] + total[second, :]
            out[:, hosts:] = jnp.zeros((per, out.shape[1] - hosts), jnp.float32)
            for r, label in enumerate(labels):
                out[r : r + 1, hosts : hosts + label.shape[1]] = label[...].astype(jnp.float32)


def documents(docs, w_in, w_out, doc_host, hosts, split, place, labels, block):
    count, depth = docs.shape
    hid, topics = w_out.shape
    per = topics // split
    width = hosts // DIGITS
    steps = count // DOC_BLOCK
    shape = (per, hosts + block)
    return pl.pallas_call(
        documents_kernel,
        grid_spec=pltpu.PrefetchScalarGridSpec(
            num_scalar_prefetch=1,
            grid=(steps,),
            in_specs=[
                pl.BlockSpec((DOC_BLOCK, depth), lambda i, p: (i, 0)),
                pl.BlockSpec((depth, hid), lambda i, p: (0, 0)),
                pl.BlockSpec((topics, hid), lambda i, p: (0, 0)),
                pl.BlockSpec((1, 1, DOC_BLOCK), lambda i, p: (i, 0, 0)),
            ]
            + [pl.BlockSpec(label.shape, lambda i, p: (0, 0)) for label in labels],
            out_specs=[pl.BlockSpec(shape, lambda i, p: (0, 0))] * split,
            scratch_shapes=[pltpu.VMEM((2 * DIGITS * topics, width), jnp.float32)],
        ),
        out_shape=[jax.ShapeDtypeStruct(shape, jnp.float32)] * split,
        compiler_params=pltpu.CompilerParams(vmem_limit_bytes=48 * MIB),
        cost_estimate=pl.CostEstimate(
            flops=2 * count * (depth * hid + hid * topics + 2 * topics * hosts),
            bytes_accessed=docs.size * 2,
            transcendentals=count * (hid + topics),
        ),
        name="documents",
    )(place, docs, w_in, w_out.T, doc_host.reshape(steps, 1, DOC_BLOCK), *labels)


def start_kernel(teleport, *rest):
    (sent, start, inverse, meta), rest = rest[-4:], rest[:-4]
    sums, degrees = rest[: len(rest) // 2], rest[len(rest) // 2 :]
    per, hosts = start.shape
    blocks, block = teleport.shape
    member = teleport[...].astype(jnp.float32) * LIFT
    mass = jnp.zeros((per, 1), jnp.float32)
    inv = 1.0 / jnp.maximum(sum(d[...] for d in degrees[1:]) + degrees[0][...], 1.0)
    inverse[...] = inv
    for j, s in enumerate(sums):
        meta[j * LABELS : (j + 1) * LABELS, :] = s[:LABELS, hosts:].astype(jnp.int32)
    for b in range(blocks):
        cols = slice(b * block, (b + 1) * block)
        value = sum(s[:, cols] for s in sums[1:]) + sums[0][:, cols]
        value = value * member[b : b + 1, :]
        start[:, cols] = value
        sent[:, cols] = (value * inv[b : b + 1, :]).astype(jnp.bfloat16)
        mass = mass + jnp.sum(value, axis=1, keepdims=True)
    lane = lax.broadcasted_iota(jnp.int32, (per, block), 1)
    first = mass.astype(jnp.bfloat16).astype(jnp.float32)
    second = (mass - first).astype(jnp.bfloat16).astype(jnp.float32)
    third = mass - first - second
    pieces = jnp.where(
        lane == 0, first, jnp.where(lane == 1, second, jnp.where(lane == 2, third, 0.0))
    )
    sent[:, blocks * block :] = pieces.astype(jnp.bfloat16)


def start_values(teleport, sums, degrees):
    per, _ = sums[0].shape
    hosts = teleport.shape[0]
    block = degrees[0].shape[1]
    vmem = pl.BlockSpec(memory_space=pltpu.VMEM)
    return pl.pallas_call(
        start_kernel,
        in_specs=[vmem] * (1 + 2 * len(sums)),
        out_specs=[vmem] * 4,
        out_shape=[
            jax.ShapeDtypeStruct((per, hosts + block), jnp.bfloat16),
            jax.ShapeDtypeStruct((per, hosts), jnp.float32),
            jax.ShapeDtypeStruct(degrees[0].shape, jnp.float32),
            jax.ShapeDtypeStruct((len(sums) * LABELS, block), jnp.int32),
        ],
        compiler_params=pltpu.CompilerParams(vmem_limit_bytes=16 * MIB),
        name="start_values",
    )(teleport.reshape(hosts // block, block), *sums, *degrees)


def hop_kernel(first, last, parts, spans, scale, meta, here, *rest):
    shards, rest = rest[:parts], rest[parts:]
    chunks, rest = rest[: len(spans)], rest[len(spans) :]
    (tele, inverse), outs, (slabs, inflow) = rest[:2], rest[2:-2], rest[-2:]
    blocks, per, block = inflow.shape
    step = pl.program_id(0)

    @pl.when(step == 0)
    def _():
        inflow[...] = jnp.zeros_like(inflow)
        slabs[parts * blocks] = jnp.zeros(slabs.shape[1:], slabs.dtype)
        for j, shard in enumerate(shards):
            for b in range(blocks):
                slabs[j * blocks + b] = shard[:, b * block : (b + 1) * block]

    empty = jnp.zeros((per, block), jnp.bfloat16)
    for tiles, (q, begin, end) in zip(chunks, spans):
        count = meta[q * LABELS + 2, 0]
        within = jnp.logical_and(step >= begin, step < end)

        @pl.when(jnp.logical_and(within, step * TILE_GROUP < count))
        def _():
            products = []
            for c in range(0, TILE_GROUP, 4):
                held = []
                for i in range(4):
                    k = step * TILE_GROUP + c + i
                    source = meta[q * LABELS, k] ^ here[0]
                    held.append(slabs[jnp.where(k < count, source, parts * blocks)])
                left = jnp.concatenate(
                    [
                        jnp.concatenate([held[0], held[1], empty, empty], axis=0),
                        jnp.concatenate([empty, empty, held[2], held[3]], axis=0),
                    ],
                    axis=1,
                )
                right = jnp.concatenate(
                    [
                        tiles[c : c + 2].reshape(2 * block, block),
                        tiles[c + 2 : c + 4].reshape(2 * block, block),
                    ],
                    axis=1,
                )
                both = lax.dot_general(left, right, NT, preferred_element_type=jnp.float32)
                for i in range(4):
                    side = (i % 2) * block
                    products.append(both[i * per : (i + 1) * per, side : side + block])
            for i in range(TILE_GROUP):
                inflow[meta[q * LABELS + 1, step * TILE_GROUP + i]] += products[i]

    @pl.when(step == pl.num_programs(0) - 1)
    def _():
        if first:
            tail = sum(s[:, blocks * block :].astype(jnp.float32) for s in shards)
            mass = jnp.sum(tail, axis=1, keepdims=True)
        for b in range(blocks):
            cols = slice(b * block, (b + 1) * block)
            own = tele[:, cols]
            state = 0.85 * inflow[b] + 0.15 * own
            if first:
                state = state / mass
                outs[1][:, cols] = own / mass
            if last:
                inflow[b] = state * scale
            else:
                outs[0][:, cols] = (state * inverse[b : b + 1, :]).astype(jnp.bfloat16)
        if last:
            count = outs[0].shape[1] // block
            for j, out in enumerate(outs):
                begin = (here[1] ^ j) * count
                for i in range(count):
                    out[:, i * block : (i + 1) * block] = inflow[begin + i]


def hop(first, last, meta, here, shards, sets, tele, inverse):
    per, hosts = tele.shape
    slots = sum(chunk.shape[0] for chunk in sets[0])
    block = sets[0][0].shape[1]
    blocks = hosts // block
    parts, split = len(shards), len(sets)
    chunks, spans = [], []
    for q, held in enumerate(sets):
        begin = 0
        for chunk in held:
            end = begin + chunk.shape[0] // TILE_GROUP
            chunks.append(chunk)
            spans.append((q, begin, end))
            begin = end

    def stream(span):
        _, begin, end = span
        return pl.BlockSpec(
            (TILE_GROUP, block, block),
            lambda i, m, p: (jnp.clip(i - begin, 0, end - begin - 1), 0, 0),
        )

    if last:
        out_shape = [jax.ShapeDtypeStruct((per, hosts // split), jnp.float32)] * split
    else:
        out_shape = [jax.ShapeDtypeStruct((per, hosts), jnp.bfloat16)]
        if first:
            out_shape.append(jax.ShapeDtypeStruct((per, hosts), jnp.float32))

    def whole(array):
        return pl.BlockSpec(array.shape, lambda i, m, p: (0,) * len(array.shape))

    return pl.pallas_call(
        functools.partial(hop_kernel, first, last, parts, spans, float(parts * hosts)),
        grid_spec=pltpu.PrefetchScalarGridSpec(
            num_scalar_prefetch=2,
            grid=(slots // TILE_GROUP,),
            in_specs=[whole(s) for s in shards]
            + [stream(span) for span in spans]
            + [whole(tele), whole(inverse)],
            out_specs=[whole(s) for s in out_shape],
            scratch_shapes=[
                pltpu.VMEM((parts * blocks + 1, per, block), jnp.bfloat16),
                pltpu.VMEM((blocks, per, block), jnp.float32),
            ],
        ),
        out_shape=out_shape,
        compiler_params=pltpu.CompilerParams(vmem_limit_bytes=16 * MIB),
        cost_estimate=pl.CostEstimate(
            flops=2 * split * slots * block * block * per,
            bytes_accessed=split * slots * block * block * 2,
            transcendentals=0,
        ),
        name="hop",
    )(meta, here, *shards, *chunks, tele, inverse)


def finish_kernel(here, *rest):
    chunks, out = rest[:-1], rest[-1]
    per = chunks[0].shape[0]
    for j, chunk in enumerate(chunks):
        out[pl.ds(pl.multiple_of((here[1] ^ j) * per, 8), per), :] = chunk[...]


def finish(here, chunks):
    per, rows = chunks[0].shape
    topics = per * len(chunks)
    return pl.pallas_call(
        finish_kernel,
        in_specs=[pl.BlockSpec(memory_space=pltpu.SMEM)]
        + [pl.BlockSpec(memory_space=pltpu.VMEM)] * len(chunks),
        out_shape=jax.ShapeDtypeStruct((topics, rows), jnp.float32),
        compiler_params=pltpu.CompilerParams(vmem_limit_bytes=16 * MIB),
        name="finish",
    )(here, *chunks)


def spread(sent, axis):
    held = {0: sent}
    for j in range(2, lax.axis_size(axis), 2):
        held[j] = xor_send(sent, axis, j)
    for j in range(0, lax.axis_size(axis), 2):
        held[j + 1] = xor_send(held[j], axis, 1)
    return [held[j] for j in range(len(held))]


def body(docs, w_in, w_out, doc_host, tiles, dst_block, src_block, tile_count, teleport):
    hosts = teleport.shape[0]
    slots, block, _ = tiles.shape
    parts, split = lax.axis_size("hst"), lax.axis_size("doc")
    blocks = hosts // block
    place = lax.axis_index("doc").astype(jnp.int32)
    here = jnp.stack([lax.axis_index("hst").astype(jnp.int32) * blocks, place])
    labels = [label.reshape(1, -1) for label in (src_block, dst_block, tile_count)]

    near = xor_send(tiles, "doc", 1)
    degree_parts, early, late = column_sums(src_block, tile_count, tiles, parts, blocks)
    far = {j: [xor_send(early, "doc", j)] for j in range(2, split, 2)}
    degree_parts = lax.all_to_all(degree_parts, "hst", split_axis=0, concat_axis=0, tiled=True)
    sums = list(documents(docs, w_in, w_out, doc_host, hosts, split, place.reshape(1), labels, block))
    degree_parts, sums[0] = lax.optimization_barrier((degree_parts, sums[0]))
    degree = jnp.sum(degree_parts, axis=0)
    degrees = [degree] + [xor_send(degree, "doc", j) for j in range(1, split)]
    sums = [sums[0]] + [xor_send(sums[j], "doc", j) for j in range(1, split)]
    late, far, _ = lax.optimization_barrier((late, far, sums[1:]))
    for j in range(2, split, 2):
        far[j].append(xor_send(late, "doc", j))
        far[j + 1] = [xor_send(far[j][0], "doc", 1)]
    sent, tele, inverse, meta = start_values(teleport, sums, degrees)
    for step in range(HOPS):
        first, last = step == 0, step == HOPS - 1
        shards = spread(sent, "hst")
        if first:
            for j in range(2, split, 2):
                far[j][1], _ = lax.optimization_barrier((far[j][1], shards[1:-1]))
                far[j + 1].append(xor_send(far[j][1], "doc", 1))
            sets = [[tiles], [near]] + [far[j] for j in range(2, split)]
        outs = hop(first, last, meta, here, shards, sets, tele, inverse)
        sent = outs[0]
        if first:
            tele = outs[1]
    chunks = [outs[0]] + [xor_send(outs[j], "doc", j) for j in range(1, split)]
    return finish(here, chunks).T


def solution(mesh):
    placed = (
        P(("hst", "doc"), None),
        P(),
        P(),
        P(("hst", "doc")),
        P(("hst", "doc"), None, None),
        P(("hst", "doc")),
        P(("hst", "doc")),
        P(("hst", "doc")),
        P("hst"),
    )
    return jax.shard_map(
        body, mesh=mesh, in_specs=placed, out_specs=P(("hst", "doc"), None), check_vma=False
    )
```

```python
import functools

import jax
import jax.numpy as jnp
from jax import lax
from jax.experimental import pallas as pl
from jax.experimental.pallas import tpu as pltpu
from jax.sharding import PartitionSpec as P

HOPS = 3
LABELS = 3
DIGITS = 4
DOC_BLOCK = 1024
GROUP = 8
TILE_GROUP = 16
LIFT = 2.0**64
NT = (((1,), (1,)), ((), ()))
MIB = 1 << 20


def xor_send(value, axis, step):
    size = lax.axis_size(axis)
    return lax.ppermute(value, axis, [(i, i ^ step) for i in range(size)])


def column_sum_kernel(begin, end, source, count, tiles, out, middle, late, total):
    step = pl.program_id(0)
    parts, rows, _ = out.shape

    @pl.when(step == 0)
    def _():
        total[...] = jnp.zeros_like(total)

    @pl.when(jnp.logical_and(step >= begin, step < end))
    def _():
        middle[...] = tiles[...]

    @pl.when(step >= end)
    def _():
        late[...] = tiles[...]

    for i in range(TILE_GROUP):
        k = step * TILE_GROUP + i
        row = jnp.where(k < count[0], source[k], parts * rows)
        part = jnp.sum(tiles[i].astype(jnp.float32), axis=0, keepdims=True)
        total[pl.ds(row, 1), :] += part

    @pl.when(step == pl.num_programs(0) - 1)
    def _():
        for j in range(parts):
            out[j] = total[j * rows : (j + 1) * rows, :]


def column_sums(source, count, tiles, parts, rows, edges):
    slots, block, _ = tiles.shape
    shape = (parts, rows, block)
    steps = slots // TILE_GROUP
    begin, end = (edge // TILE_GROUP for edge in edges)
    group = (TILE_GROUP, block, block)
    return pl.pallas_call(
        functools.partial(column_sum_kernel, begin, end),
        grid_spec=pltpu.PrefetchScalarGridSpec(
            num_scalar_prefetch=2,
            grid=(steps,),
            in_specs=[pl.BlockSpec(group, lambda i, s, c: (i, 0, 0))],
            out_specs=[
                pl.BlockSpec(shape, lambda i, s, c: (0, 0, 0)),
                pl.BlockSpec(group, lambda i, s, c: (jnp.clip(i - begin, 0, end - begin - 1), 0, 0)),
                pl.BlockSpec(group, lambda i, s, c: (jnp.maximum(i - end, 0), 0, 0)),
            ],
            scratch_shapes=[pltpu.VMEM((parts * rows + 8, block), jnp.float32)],
        ),
        out_shape=[
            jax.ShapeDtypeStruct(shape, jnp.float32),
            jax.ShapeDtypeStruct(((end - begin) * TILE_GROUP, block, block), tiles.dtype),
            jax.ShapeDtypeStruct(((steps - end) * TILE_GROUP, block, block), tiles.dtype),
        ],
        compiler_params=pltpu.CompilerParams(vmem_limit_bytes=16 * MIB),
        cost_estimate=pl.CostEstimate(
            flops=tiles.size, bytes_accessed=tiles.size * 4, transcendentals=0
        ),
        name="column_sums",
    )(source, count, tiles)


def block_topics(docs, w_in, w_out_t, host, width):
    hidden = jax.nn.gelu(
        jnp.dot(docs[...], w_in[...], preferred_element_type=jnp.float32), approximate=True
    ).astype(jnp.bfloat16)
    logits = lax.dot_general(w_out_t[...], hidden, NT, preferred_element_type=jnp.float32)
    powers = jnp.exp(logits - jnp.max(logits, axis=0, keepdims=True))
    probs = powers * (1.0 / jnp.sum(powers, axis=0, keepdims=True))
    high = probs.astype(jnp.bfloat16)
    low = (probs - high.astype(jnp.float32)).astype(jnp.bfloat16)
    index = host[0]
    digit = index // width
    within = index - digit * width
    picks = [jnp.where(digit == j, 1.0, 0.0).astype(jnp.bfloat16) for j in range(DIGITS)]
    left = jnp.concatenate([high * p for p in picks] + [low * p for p in picks], axis=0)
    places = lax.broadcasted_iota(jnp.int32, (width, index.shape[1]), 0)
    right = jnp.where(places == within, 1.0, 0.0).astype(jnp.bfloat16)
    return lax.dot_general(left, right, NT, preferred_element_type=jnp.float32)


def documents_kernel(place, docs, w_in, w_out_t, host, degrees, *rest):
    labels, outs, total = rest[:LABELS], rest[LABELS:-1], rest[-1]
    step = pl.program_id(0)
    topics = w_out_t.shape[0]
    width = total.shape[1]
    added = block_topics(docs, w_in, w_out_t, host, width)

    @pl.when(step == 0)
    def _():
        total[...] = added

    @pl.when(step > 0)
    def _():
        total[...] += added

    @pl.when(step == pl.num_programs(0) - 1)
    def _():
        per = outs[0].shape[0]
        hosts = DIGITS * width
        degree = sum(degrees[j] for j in range(1, degrees.shape[0])) + degrees[0]
        blocks, block = degree.shape
        wide = hosts + blocks // per * block
        for j, out in enumerate(outs):
            chunk = (place[0] ^ j) * per
            for d in range(DIGITS):
                first = pl.ds(pl.multiple_of(d * topics + chunk, 8), per)
                second = pl.ds(pl.multiple_of((DIGITS + d) * topics + chunk, 8), per)
                out[:, d * width : (d + 1) * width] = total[first, :] + total[second, :]
            for c in range(blocks // per):
                cols = slice(hosts + c * block, hosts + (c + 1) * block)
                out[:, cols] = degree[c * per : (c + 1) * per, :]
            out[:, wide:] = jnp.zeros((per, block), jnp.float32)
            for r, label in enumerate(labels):
                out[r : r + 1, wide : wide + label.shape[1]] = label[...].astype(jnp.float32)


def documents(docs, w_in, w_out, doc_host, hosts, split, place, degrees, labels):
    count, depth = docs.shape
    hid, topics = w_out.shape
    per = topics // split
    width = hosts // DIGITS
    steps = count // DOC_BLOCK
    shape = (per, hosts + hosts // per + degrees.shape[2])
    return pl.pallas_call(
        documents_kernel,
        grid_spec=pltpu.PrefetchScalarGridSpec(
            num_scalar_prefetch=1,
            grid=(steps,),
            in_specs=[
                pl.BlockSpec((DOC_BLOCK, depth), lambda i, p: (i, 0)),
                pl.BlockSpec((depth, hid), lambda i, p: (0, 0)),
                pl.BlockSpec((topics, hid), lambda i, p: (0, 0)),
                pl.BlockSpec((1, 1, DOC_BLOCK), lambda i, p: (i, 0, 0)),
                pl.BlockSpec(degrees.shape, lambda i, p: (0, 0, 0)),
            ]
            + [pl.BlockSpec(label.shape, lambda i, p: (0, 0)) for label in labels],
            out_specs=[pl.BlockSpec(shape, lambda i, p: (0, 0))] * split,
            scratch_shapes=[pltpu.VMEM((2 * DIGITS * topics, width), jnp.float32)],
        ),
        out_shape=[jax.ShapeDtypeStruct(shape, jnp.float32)] * split,
        compiler_params=pltpu.CompilerParams(vmem_limit_bytes=48 * MIB),
        cost_estimate=pl.CostEstimate(
            flops=2 * count * (depth * hid + hid * topics + 2 * topics * hosts),
            bytes_accessed=docs.size * 2,
            transcendentals=count * (hid + topics),
        ),
        name="documents",
    )(place, docs, w_in, w_out.T, doc_host.reshape(steps, 1, DOC_BLOCK), degrees, *labels)


def start_kernel(teleport, *rest):
    sums, (sent, start, inverse, meta) = rest[:-4], rest[-4:]
    per, hosts = start.shape
    blocks, block = teleport.shape
    member = teleport[...].astype(jnp.float32) * LIFT
    mass = jnp.zeros((per, 1), jnp.float32)
    tail = slice(hosts, hosts + hosts // per)
    packed = 1.0 / jnp.maximum(sum(s[:, tail] for s in sums[1:]) + sums[0][:, tail], 1.0)
    for c in range(blocks // per):
        inverse[c * per : (c + 1) * per, :] = packed[:, c * block : (c + 1) * block]
    for j, s in enumerate(sums):
        meta[j * LABELS : (j + 1) * LABELS, :] = s[:LABELS, tail.stop :].astype(jnp.int32)
    for b in range(blocks):
        cols = slice(b * block, (b + 1) * block)
        value = sum(s[:, cols] for s in sums[1:]) + sums[0][:, cols]
        value = value * member[b : b + 1, :]
        start[:, cols] = value
        sent[:, cols] = (value * inverse[b : b + 1, :]).astype(jnp.bfloat16)
        mass = mass + jnp.sum(value, axis=1, keepdims=True)
    lane = lax.broadcasted_iota(jnp.int32, (per, block), 1)
    first = mass.astype(jnp.bfloat16).astype(jnp.float32)
    second = (mass - first).astype(jnp.bfloat16).astype(jnp.float32)
    third = mass - first - second
    pieces = jnp.where(
        lane == 0, first, jnp.where(lane == 1, second, jnp.where(lane == 2, third, 0.0))
    )
    sent[:, blocks * block :] = pieces.astype(jnp.bfloat16)


def start_values(teleport, sums, block):
    per, _ = sums[0].shape
    hosts = teleport.shape[0]
    vmem = pl.BlockSpec(memory_space=pltpu.VMEM)
    return pl.pallas_call(
        start_kernel,
        in_specs=[vmem] * (1 + len(sums)),
        out_specs=[vmem] * 4,
        out_shape=[
            jax.ShapeDtypeStruct((per, hosts + block), jnp.bfloat16),
            jax.ShapeDtypeStruct((per, hosts), jnp.float32),
            jax.ShapeDtypeStruct((hosts // block, block), jnp.float32),
            jax.ShapeDtypeStruct((len(sums) * LABELS, block), jnp.int32),
        ],
        compiler_params=pltpu.CompilerParams(vmem_limit_bytes=16 * MIB),
        name="start_values",
    )(teleport.reshape(hosts // block, block), *sums)


def hop_kernel(first, last, parts, spans, scale, meta, here, *rest):
    shards, rest = rest[:parts][::-1], rest[parts:]
    chunks, rest = rest[: len(spans)], rest[len(spans) :]
    (tele, inverse), outs, (slabs, inflow) = rest[:2], rest[2:-2], rest[-2:]
    blocks, per, block = inflow.shape
    step = pl.program_id(0)

    @pl.when(step == 0)
    def _():
        inflow[...] = jnp.zeros_like(inflow)
        slabs[parts * blocks] = jnp.zeros(slabs.shape[1:], slabs.dtype)
        for j, shard in enumerate(shards):
            for b in range(blocks):
                slabs[j * blocks + b] = shard[:, b * block : (b + 1) * block]

    empty = jnp.zeros((per, block), jnp.bfloat16)
    for tiles, (q, begin, end) in zip(chunks, spans):
        count = meta[q * LABELS + 2, 0]
        within = jnp.logical_and(step >= begin, step < end)

        @pl.when(jnp.logical_and(within, step * TILE_GROUP < count))
        def _():
            products = []
            for c in range(0, TILE_GROUP, 4):
                held = []
                for i in range(4):
                    k = step * TILE_GROUP + c + i
                    source = meta[q * LABELS, k] ^ here[0]
                    held.append(slabs[jnp.where(k < count, source, parts * blocks)])
                left = jnp.concatenate(
                    [
                        jnp.concatenate([held[0], held[1], empty, empty], axis=0),
                        jnp.concatenate([empty, empty, held[2], held[3]], axis=0),
                    ],
                    axis=1,
                )
                right = jnp.concatenate(
                    [
                        tiles[c : c + 2].reshape(2 * block, block),
                        tiles[c + 2 : c + 4].reshape(2 * block, block),
                    ],
                    axis=1,
                )
                both = lax.dot_general(left, right, NT, preferred_element_type=jnp.float32)
                for i in range(4):
                    side = (i % 2) * block
                    products.append(both[i * per : (i + 1) * per, side : side + block])
            for i in range(TILE_GROUP):
                inflow[meta[q * LABELS + 1, step * TILE_GROUP + i]] += products[i]

    @pl.when(step == pl.num_programs(0) - 1)
    def _():
        if first:
            tail = sum(s[:, blocks * block :].astype(jnp.float32) for s in shards)
            mass = jnp.sum(tail, axis=1, keepdims=True)
        for b in range(blocks):
            cols = slice(b * block, (b + 1) * block)
            own = tele[:, cols]
            state = 0.85 * inflow[b] + 0.15 * own
            if first:
                state = state / mass
                outs[1][:, cols] = own / mass
            if last:
                inflow[b] = state * scale
            else:
                outs[0][:, cols] = (state * inverse[b : b + 1, :]).astype(jnp.bfloat16)
        if last:
            count = outs[0].shape[1] // block
            for j, out in enumerate(outs):
                begin = (here[1] ^ j) * count
                for i in range(count):
                    out[:, i * block : (i + 1) * block] = inflow[begin + i]


def hop(first, last, meta, here, shards, sets, tele, inverse):
    per, hosts = tele.shape
    slots = sum(chunk.shape[0] for chunk in sets[0])
    block = sets[0][0].shape[1]
    blocks = hosts // block
    parts, split = len(shards), len(sets)
    chunks, spans = [], []
    for q, held in enumerate(sets):
        begin = 0
        for chunk in held:
            end = begin + chunk.shape[0] // TILE_GROUP
            chunks.append(chunk)
            spans.append((q, begin, end))
            begin = end

    def stream(span):
        _, begin, end = span
        return pl.BlockSpec(
            (TILE_GROUP, block, block),
            lambda i, m, p: (jnp.clip(i - begin, 0, end - begin - 1), 0, 0),
        )

    if last:
        out_shape = [jax.ShapeDtypeStruct((per, hosts // split), jnp.float32)] * split
    else:
        out_shape = [jax.ShapeDtypeStruct((per, hosts), jnp.bfloat16)]
        if first:
            out_shape.append(jax.ShapeDtypeStruct((per, hosts), jnp.float32))

    def whole(array):
        return pl.BlockSpec(array.shape, lambda i, m, p: (0,) * len(array.shape))

    return pl.pallas_call(
        functools.partial(hop_kernel, first, last, parts, spans, float(parts * hosts)),
        grid_spec=pltpu.PrefetchScalarGridSpec(
            num_scalar_prefetch=2,
            grid=(slots // TILE_GROUP,),
            in_specs=[whole(s) for s in reversed(shards)]
            + [stream(span) for span in spans]
            + [whole(tele), whole(inverse)],
            out_specs=[whole(s) for s in out_shape],
            scratch_shapes=[
                pltpu.VMEM((parts * blocks + 1, per, block), jnp.bfloat16),
                pltpu.VMEM((blocks, per, block), jnp.float32),
            ],
        ),
        out_shape=out_shape,
        compiler_params=pltpu.CompilerParams(vmem_limit_bytes=16 * MIB),
        cost_estimate=pl.CostEstimate(
            flops=2 * split * slots * block * block * per,
            bytes_accessed=split * slots * block * block * 2,
            transcendentals=0,
        ),
        name="hop",
    )(meta, here, *reversed(shards), *chunks, tele, inverse)


def finish_kernel(here, *rest):
    chunks, out = rest[:-1], rest[-1]
    per = chunks[0].shape[0]
    for j, chunk in enumerate(chunks):
        out[pl.ds(pl.multiple_of((here[1] ^ j) * per, 8), per), :] = chunk[...]


def finish(here, chunks):
    per, rows = chunks[0].shape
    topics = per * len(chunks)
    return pl.pallas_call(
        finish_kernel,
        in_specs=[pl.BlockSpec(memory_space=pltpu.SMEM)]
        + [pl.BlockSpec(memory_space=pltpu.VMEM)] * len(chunks),
        out_shape=jax.ShapeDtypeStruct((topics, rows), jnp.float32),
        compiler_params=pltpu.CompilerParams(vmem_limit_bytes=16 * MIB),
        name="finish",
    )(here, *chunks)


def spread(sent, axis):
    size = lax.axis_size(axis)
    held = {0: sent}
    for j in range(size - 2, 2, -2):
        held[j] = xor_send(sent, axis, j)
    held[1] = xor_send(sent, axis, 1)
    held[2] = xor_send(sent, axis, 2)
    for j in range(size - 2, 0, -2):
        held[j + 1] = xor_send(held[j], axis, 1)
    return [held[j] for j in range(size)]


def body(docs, w_in, w_out, doc_host, tiles, dst_block, src_block, tile_count, teleport):
    hosts = teleport.shape[0]
    slots, block, _ = tiles.shape
    parts, split = lax.axis_size("hst"), lax.axis_size("doc")
    blocks = hosts // block
    place = lax.axis_index("doc").astype(jnp.int32)
    here = jnp.stack([lax.axis_index("hst").astype(jnp.int32) * blocks, place])
    labels = [label.reshape(1, -1) for label in (src_block, dst_block, tile_count)]

    edges = (slots // 4, 3 * slots // 4)
    early = tiles[: edges[0]]
    far = {j: [xor_send(early, "doc", j)] for j in range(2, split, 2)}
    near = xor_send(tiles, "doc", 1)
    degrees, middle, late = column_sums(src_block, tile_count, tiles, parts, blocks, edges)
    for j in range(2, split, 2):
        far[j].append(xor_send(middle, "doc", j))
    degrees = lax.all_to_all(degrees, "hst", split_axis=0, concat_axis=0, tiled=True)
    sums = documents(docs, w_in, w_out, doc_host, hosts, split, place.reshape(1), degrees, labels)
    sums = [sums[0]] + [xor_send(sums[j], "doc", j) for j in range(1, split)]
    late, far, _ = lax.optimization_barrier((late, far, sums[1:]))
    for j in range(2, split, 2):
        far[j].append(xor_send(late, "doc", j))
        far[j + 1] = [xor_send(chunk, "doc", 1) for chunk in far[j][:2]]
    sent, tele, inverse, meta = start_values(teleport, sums, block)
    for step in range(HOPS):
        first, last = step == 0, step == HOPS - 1
        shards = spread(sent, "hst")
        if first:
            for j in range(2, split, 2):
                far[j][2], _ = lax.optimization_barrier((far[j][2], shards[1:-1]))
                far[j + 1].append(xor_send(far[j][2], "doc", 1))
            sets = [[tiles], [near]] + [far[j] for j in range(2, split)]
        outs = hop(first, last, meta, here, shards, sets, tele, inverse)
        sent = outs[0]
        if first:
            tele = outs[1]
    chunks = [outs[0]] + [xor_send(outs[j], "doc", j) for j in range(1, split)]
    return finish(here, chunks).T


def solution(mesh):
    placed = (
        P(("hst", "doc"), None),
        P(),
        P(),
        P(("hst", "doc")),
        P(("hst", "doc"), None, None),
        P(("hst", "doc")),
        P(("hst", "doc")),
        P(("hst", "doc")),
        P("hst"),
    )
    return jax.shard_map(
        body, mesh=mesh, in_specs=placed, out_specs=P(("hst", "doc"), None), check_vma=False
    )
```

```python
import functools

import jax
import jax.numpy as jnp
from jax import lax
from jax.experimental import pallas as pl
from jax.experimental.pallas import tpu as pltpu
from jax.sharding import PartitionSpec as P

HOPS = 3
LABELS = 3
DIGITS = 4
DOC_BLOCK = 1024
TILE_GROUP = 16
LIFT = 2.0**64
NT = (((1,), (1,)), ((), ()))
MIB = 1 << 20


def xor_send(value, axis, step):
    size = lax.axis_size(axis)
    return lax.ppermute(value, axis, [(i, i ^ step) for i in range(size)])


def column_sum_kernel(source, count, tiles, out, total):
    step = pl.program_id(0)
    parts, rows, _ = out.shape

    @pl.when(step == 0)
    def _():
        total[...] = jnp.zeros_like(total)

    for i in range(TILE_GROUP):
        k = step * TILE_GROUP + i
        row = jnp.where(k < count[0], source[k], parts * rows)
        part = jnp.sum(tiles[i].astype(jnp.float32), axis=0, keepdims=True)
        total[pl.ds(row, 1), :] += part

    @pl.when(step == pl.num_programs(0) - 1)
    def _():
        for j in range(parts):
            out[j] = total[j * rows : (j + 1) * rows, :]


def column_sums(source, count, tiles, parts, rows):
    slots, block, _ = tiles.shape
    shape = (parts, rows, block)
    return pl.pallas_call(
        column_sum_kernel,
        grid_spec=pltpu.PrefetchScalarGridSpec(
            num_scalar_prefetch=2,
            grid=(slots // TILE_GROUP,),
            in_specs=[pl.BlockSpec((TILE_GROUP, block, block), lambda i, s, c: (i, 0, 0))],
            out_specs=pl.BlockSpec(shape, lambda i, s, c: (0, 0, 0)),
            scratch_shapes=[pltpu.VMEM((parts * rows + 8, block), jnp.float32)],
        ),
        out_shape=jax.ShapeDtypeStruct(shape, jnp.float32),
        compiler_params=pltpu.CompilerParams(vmem_limit_bytes=16 * MIB),
        cost_estimate=pl.CostEstimate(
            flops=tiles.size, bytes_accessed=tiles.size * 2, transcendentals=0
        ),
        name="column_sums",
    )(source, count, tiles)


def block_topics(docs, w_in, w_out_t, host, width):
    hidden = jax.nn.gelu(
        jnp.dot(docs[...], w_in[...], preferred_element_type=jnp.float32), approximate=True
    ).astype(jnp.bfloat16)
    logits = lax.dot_general(w_out_t[...], hidden, NT, preferred_element_type=jnp.float32)
    powers = jnp.exp(logits - jnp.max(logits, axis=0, keepdims=True))
    probs = powers * (1.0 / jnp.sum(powers, axis=0, keepdims=True))
    high = probs.astype(jnp.bfloat16)
    low = (probs - high.astype(jnp.float32)).astype(jnp.bfloat16)
    index = host[0]
    digit = index // width
    within = index - digit * width
    picks = [jnp.where(digit == j, 1.0, 0.0).astype(jnp.bfloat16) for j in range(DIGITS)]
    left = jnp.concatenate([high * p for p in picks] + [low * p for p in picks], axis=0)
    places = lax.broadcasted_iota(jnp.int32, (width, index.shape[1]), 0)
    right = jnp.where(places == within, 1.0, 0.0).astype(jnp.bfloat16)
    return lax.dot_general(left, right, NT, preferred_element_type=jnp.float32)


def documents_kernel(place, docs, w_in, w_out_t, host, degrees, *rest):
    labels, outs, total = rest[:LABELS], rest[LABELS:-1], rest[-1]
    step = pl.program_id(0)
    topics = w_out_t.shape[0]
    width = total.shape[1]
    added = block_topics(docs, w_in, w_out_t, host, width)

    @pl.when(step == 0)
    def _():
        total[...] = added

    @pl.when(step > 0)
    def _():
        total[...] += added

    @pl.when(step == pl.num_programs(0) - 1)
    def _():
        per = outs[0].shape[0]
        hosts = DIGITS * width
        degree = sum(degrees[j] for j in range(1, degrees.shape[0])) + degrees[0]
        blocks, block = degree.shape
        wide = hosts + blocks // per * block
        for j, out in enumerate(outs):
            chunk = (place[0] ^ j) * per
            for d in range(DIGITS):
                first = pl.ds(pl.multiple_of(d * topics + chunk, 8), per)
                second = pl.ds(pl.multiple_of((DIGITS + d) * topics + chunk, 8), per)
                out[:, d * width : (d + 1) * width] = total[first, :] + total[second, :]
            for c in range(blocks // per):
                cols = slice(hosts + c * block, hosts + (c + 1) * block)
                out[:, cols] = degree[c * per : (c + 1) * per, :]
            out[:, wide:] = jnp.zeros((per, block), jnp.float32)
            for r, label in enumerate(labels):
                out[r : r + 1, wide : wide + label.shape[1]] = label[...].astype(jnp.float32)


def documents(docs, w_in, w_out, doc_host, hosts, split, place, degrees, labels):
    count, depth = docs.shape
    hid, topics = w_out.shape
    per = topics // split
    width = hosts // DIGITS
    steps = count // DOC_BLOCK
    shape = (per, hosts + hosts // per + degrees.shape[2])
    return pl.pallas_call(
        documents_kernel,
        grid_spec=pltpu.PrefetchScalarGridSpec(
            num_scalar_prefetch=1,
            grid=(steps,),
            in_specs=[
                pl.BlockSpec((DOC_BLOCK, depth), lambda i, p: (i, 0)),
                pl.BlockSpec((depth, hid), lambda i, p: (0, 0)),
                pl.BlockSpec((topics, hid), lambda i, p: (0, 0)),
                pl.BlockSpec((1, 1, DOC_BLOCK), lambda i, p: (i, 0, 0)),
                pl.BlockSpec(degrees.shape, lambda i, p: (0, 0, 0)),
            ]
            + [pl.BlockSpec(label.shape, lambda i, p: (0, 0)) for label in labels],
            out_specs=[pl.BlockSpec(shape, lambda i, p: (0, 0))] * split,
            scratch_shapes=[pltpu.VMEM((2 * DIGITS * topics, width), jnp.float32)],
        ),
        out_shape=[jax.ShapeDtypeStruct(shape, jnp.float32)] * split,
        compiler_params=pltpu.CompilerParams(vmem_limit_bytes=48 * MIB),
        cost_estimate=pl.CostEstimate(
            flops=2 * count * (depth * hid + hid * topics + 2 * topics * hosts),
            bytes_accessed=docs.size * 2,
            transcendentals=count * (hid + topics),
        ),
        name="documents",
    )(place, docs, w_in, w_out.T, doc_host.reshape(steps, 1, DOC_BLOCK), degrees, *labels)


def start_kernel(held, teleport, *rest):
    sums, rest = rest[: len(rest) - 2 * held - 4], rest[len(rest) - held - 4 :]
    sent, start, inverse, meta = rest[:4]
    per, hosts = start.shape
    blocks, block = teleport.shape
    member = teleport[...].astype(jnp.float32) * LIFT
    mass = jnp.zeros((per, 1), jnp.float32)
    tail = slice(hosts, hosts + hosts // per)
    packed = 1.0 / jnp.maximum(sum(s[:, tail] for s in sums[1:]) + sums[0][:, tail], 1.0)
    for c in range(blocks // per):
        inverse[c * per : (c + 1) * per, :] = packed[:, c * block : (c + 1) * block]
    for j, s in enumerate(sums):
        meta[j * LABELS : (j + 1) * LABELS, :] = s[:LABELS, tail.stop :].astype(jnp.int32)
    for b in range(blocks):
        cols = slice(b * block, (b + 1) * block)
        value = sum(s[:, cols] for s in sums[1:]) + sums[0][:, cols]
        value = value * member[b : b + 1, :]
        start[:, cols] = value
        sent[:, cols] = (value * inverse[b : b + 1, :]).astype(jnp.bfloat16)
        mass = mass + jnp.sum(value, axis=1, keepdims=True)
    lane = lax.broadcasted_iota(jnp.int32, (per, block), 1)
    first = mass.astype(jnp.bfloat16).astype(jnp.float32)
    second = (mass - first).astype(jnp.bfloat16).astype(jnp.float32)
    third = mass - first - second
    pieces = jnp.where(
        lane == 0, first, jnp.where(lane == 1, second, jnp.where(lane == 2, third, 0.0))
    )
    sent[:, blocks * block :] = pieces.astype(jnp.bfloat16)


def start_values(teleport, sums, block, held):
    per, _ = sums[0].shape
    hosts = teleport.shape[0]
    vmem = pl.BlockSpec(memory_space=pltpu.VMEM)
    keep = pl.BlockSpec(memory_space=pl.ANY)
    return pl.pallas_call(
        functools.partial(start_kernel, len(held)),
        in_specs=[vmem] * (1 + len(sums)) + [keep] * len(held),
        out_specs=[vmem] * 4 + [keep] * len(held),
        out_shape=[
            jax.ShapeDtypeStruct((per, hosts + block), jnp.bfloat16),
            jax.ShapeDtypeStruct((per, hosts), jnp.float32),
            jax.ShapeDtypeStruct((hosts // block, block), jnp.float32),
            jax.ShapeDtypeStruct((len(sums) * LABELS, block), jnp.int32),
        ]
        + [jax.ShapeDtypeStruct(array.shape, array.dtype) for array in held],
        input_output_aliases={1 + len(sums) + i: 4 + i for i in range(len(held))},
        compiler_params=pltpu.CompilerParams(vmem_limit_bytes=16 * MIB),
        name="start_values",
    )(teleport.reshape(hosts // block, block), *sums, *held)


def after_kernel(*refs):
    del refs


def after(value, ready):
    keep = pl.BlockSpec(memory_space=pl.ANY)
    return pl.pallas_call(
        after_kernel,
        in_specs=[keep] * (1 + len(ready)),
        out_specs=keep,
        out_shape=jax.ShapeDtypeStruct(value.shape, value.dtype),
        input_output_aliases={0: 0},
        name="after",
    )(value, *ready)


def hop_kernel(first, last, parts, spans, scale, meta, here, *rest):
    shards, rest = rest[:parts][::-1], rest[parts:]
    chunks, rest = rest[: len(spans)], rest[len(spans) :]
    (tele, inverse), outs, (slabs, inflow) = rest[:2], rest[2:-2], rest[-2:]
    blocks, per, block = inflow.shape
    step = pl.program_id(0)

    @pl.when(step == 0)
    def _():
        inflow[...] = jnp.zeros_like(inflow)
        slabs[parts * blocks] = jnp.zeros(slabs.shape[1:], slabs.dtype)
        for j, shard in enumerate(shards):
            for b in range(blocks):
                slabs[j * blocks + b] = shard[:, b * block : (b + 1) * block]

    empty = jnp.zeros((per, block), jnp.bfloat16)
    for tiles, (q, begin, end) in zip(chunks, spans):
        count = meta[q * LABELS + 2, 0]
        within = jnp.logical_and(step >= begin, step < end)

        @pl.when(jnp.logical_and(within, step * TILE_GROUP < count))
        def _():
            products = []
            for c in range(0, TILE_GROUP, 4):
                held = []
                for i in range(4):
                    k = step * TILE_GROUP + c + i
                    source = meta[q * LABELS, k] ^ here[0]
                    held.append(slabs[jnp.where(k < count, source, parts * blocks)])
                left = jnp.concatenate(
                    [
                        jnp.concatenate([held[0], held[1], empty, empty], axis=0),
                        jnp.concatenate([empty, empty, held[2], held[3]], axis=0),
                    ],
                    axis=1,
                )
                right = jnp.concatenate(
                    [
                        tiles[c : c + 2].reshape(2 * block, block),
                        tiles[c + 2 : c + 4].reshape(2 * block, block),
                    ],
                    axis=1,
                )
                both = lax.dot_general(left, right, NT, preferred_element_type=jnp.float32)
                for i in range(4):
                    side = (i % 2) * block
                    products.append(both[i * per : (i + 1) * per, side : side + block])
            for i in range(TILE_GROUP):
                inflow[meta[q * LABELS + 1, step * TILE_GROUP + i]] += products[i]

    @pl.when(step == pl.num_programs(0) - 1)
    def _():
        if first:
            tail = sum(s[:, blocks * block :].astype(jnp.float32) for s in shards)
            mass = jnp.sum(tail, axis=1, keepdims=True)
        for b in range(blocks):
            cols = slice(b * block, (b + 1) * block)
            own = tele[:, cols]
            state = 0.85 * inflow[b] + 0.15 * own
            if first:
                state = state / mass
                outs[1][:, cols] = own / mass
            if last:
                inflow[b] = state * scale
            else:
                outs[0][:, cols] = (state * inverse[b : b + 1, :]).astype(jnp.bfloat16)
        if last:
            count = outs[0].shape[1] // block
            for j, out in enumerate(outs):
                begin = (here[1] ^ j) * count
                for i in range(count):
                    out[:, i * block : (i + 1) * block] = inflow[begin + i]


def hop(first, last, meta, here, shards, sets, tele, inverse):
    per, hosts = tele.shape
    slots = sum(chunk.shape[0] for chunk in sets[0])
    block = sets[0][0].shape[1]
    blocks = hosts // block
    parts, split = len(shards), len(sets)
    chunks, spans = [], []
    for q, held in enumerate(sets):
        begin = 0
        for chunk in held:
            end = begin + chunk.shape[0] // TILE_GROUP
            chunks.append(chunk)
            spans.append((q, begin, end))
            begin = end

    def stream(span):
        _, begin, end = span
        return pl.BlockSpec(
            (TILE_GROUP, block, block),
            lambda i, m, p: (jnp.clip(i - begin, 0, end - begin - 1), 0, 0),
        )

    if last:
        out_shape = [jax.ShapeDtypeStruct((per, hosts // split), jnp.float32)] * split
    else:
        out_shape = [jax.ShapeDtypeStruct((per, hosts), jnp.bfloat16)]
        if first:
            out_shape.append(jax.ShapeDtypeStruct((per, hosts), jnp.float32))

    def whole(array):
        return pl.BlockSpec(array.shape, lambda i, m, p: (0,) * len(array.shape))

    return pl.pallas_call(
        functools.partial(hop_kernel, first, last, parts, spans, float(parts * hosts)),
        grid_spec=pltpu.PrefetchScalarGridSpec(
            num_scalar_prefetch=2,
            grid=(slots // TILE_GROUP,),
            in_specs=[whole(s) for s in reversed(shards)]
            + [stream(span) for span in spans]
            + [whole(tele), whole(inverse)],
            out_specs=[whole(s) for s in out_shape],
            scratch_shapes=[
                pltpu.VMEM((parts * blocks + 1, per, block), jnp.bfloat16),
                pltpu.VMEM((blocks, per, block), jnp.float32),
            ],
        ),
        out_shape=out_shape,
        compiler_params=pltpu.CompilerParams(vmem_limit_bytes=16 * MIB),
        cost_estimate=pl.CostEstimate(
            flops=2 * split * slots * block * block * per,
            bytes_accessed=split * slots * block * block * 2,
            transcendentals=0,
        ),
        name="hop",
    )(meta, here, *reversed(shards), *chunks, tele, inverse)


def finish_kernel(here, *rest):
    chunks, out = rest[:-1], rest[-1]
    per = chunks[0].shape[0]
    for j, chunk in enumerate(chunks):
        out[pl.ds(pl.multiple_of((here[1] ^ j) * per, 8), per), :] = chunk[...]


def finish(here, chunks):
    per, rows = chunks[0].shape
    topics = per * len(chunks)
    return pl.pallas_call(
        finish_kernel,
        in_specs=[pl.BlockSpec(memory_space=pltpu.SMEM)]
        + [pl.BlockSpec(memory_space=pltpu.VMEM)] * len(chunks),
        out_shape=jax.ShapeDtypeStruct((topics, rows), jnp.float32),
        compiler_params=pltpu.CompilerParams(vmem_limit_bytes=16 * MIB),
        name="finish",
    )(here, *chunks)


def spread(sent, axis):
    size = lax.axis_size(axis)
    held = {0: sent}
    for j in range(size - 2, 2, -2):
        held[j] = xor_send(sent, axis, j)
    held[1] = xor_send(sent, axis, 1)
    held[2] = xor_send(sent, axis, 2)
    for j in range(size - 2, 0, -2):
        held[j + 1] = xor_send(held[j], axis, 1)
    return [held[j] for j in range(size)]


def body(docs, w_in, w_out, doc_host, tiles, dst_block, src_block, tile_count, teleport):
    hosts = teleport.shape[0]
    slots, block, _ = tiles.shape
    parts, split = lax.axis_size("hst"), lax.axis_size("doc")
    blocks = hosts // block
    place = lax.axis_index("doc").astype(jnp.int32)
    here = jnp.stack([lax.axis_index("hst").astype(jnp.int32) * blocks, place])
    labels = [label.reshape(1, -1) for label in (src_block, dst_block, tile_count)]

    near = xor_send(tiles, "doc", 1)
    cut = 3 * slots // 4
    early, late = tiles[:cut], tiles[cut:]
    far = {j: [xor_send(early, "doc", j)] for j in range(2, split, 2)}
    degrees = column_sums(src_block, tile_count, tiles, parts, blocks)
    degrees = lax.all_to_all(degrees, "hst", split_axis=0, concat_axis=0, tiled=True)
    sums = documents(docs, w_in, w_out, doc_host, hosts, split, place.reshape(1), degrees, labels)
    sums = [sums[0]] + [xor_send(sums[j], "doc", j) for j in range(1, split)]
    crossed = [far[j][0] for j in range(2, split, 2)]
    sent, tele, inverse, meta, late, *crossed = start_values(
        teleport, sums, block, [late] + crossed
    )
    for j in range(2, split, 2):
        far[j] = [crossed[j // 2 - 1], xor_send(late, "doc", j)]
        far[j + 1] = [xor_send(far[j][0], "doc", 1)]
    for step in range(HOPS):
        first, last = step == 0, step == HOPS - 1
        shards = spread(sent, "hst")
        if first:
            for j in range(2, split, 2):
                far[j][1] = after(far[j][1], shards[1:-1])
                far[j + 1].append(xor_send(far[j][1], "doc", 1))
            sets = [[tiles], [near]] + [far[j] for j in range(2, split)]
        outs = hop(first, last, meta, here, shards, sets, tele, inverse)
        sent = outs[0]
        if first:
            tele = outs[1]
    chunks = [outs[0]] + [xor_send(outs[j], "doc", j) for j in range(1, split)]
    return finish(here, chunks).T


def solution(mesh):
    placed = (
        P(("hst", "doc"), None),
        P(),
        P(),
        P(("hst", "doc")),
        P(("hst", "doc"), None, None),
        P(("hst", "doc")),
        P(("hst", "doc")),
        P(("hst", "doc")),
        P("hst"),
    )
    return jax.shard_map(
        body, mesh=mesh, in_specs=placed, out_specs=P(("hst", "doc"), None), check_vma=False
    )
```

```python
import functools

import jax
import jax.numpy as jnp
from jax import lax
from jax.experimental import pallas as pl
from jax.experimental.pallas import tpu as pltpu
from jax.sharding import PartitionSpec as P

HOPS = 3
LABELS = 3
DIGITS = 4
DOC_BLOCK = 1024
TILE_GROUP = 16
HOP_MIB = 16
LIFT = 2.0**64
NT = (((1,), (1,)), ((), ()))
MIB = 1 << 20


def xor_send(value, axis, step):
    size = lax.axis_size(axis)
    return lax.ppermute(value, axis, [(i, i ^ step) for i in range(size)])


def column_sum_kernel(source, count, tiles, out, total):
    step = pl.program_id(0)
    parts, rows, _ = out.shape

    @pl.when(step == 0)
    def _():
        total[...] = jnp.zeros_like(total)

    for i in range(TILE_GROUP):
        k = step * TILE_GROUP + i
        row = jnp.where(k < count[0], source[k], parts * rows)
        part = jnp.sum(tiles[i].astype(jnp.float32), axis=0, keepdims=True)
        total[pl.ds(row, 1), :] += part

    @pl.when(step == pl.num_programs(0) - 1)
    def _():
        for j in range(parts):
            out[j] = total[j * rows : (j + 1) * rows, :]


def column_sums(source, count, tiles, parts, rows):
    slots, block, _ = tiles.shape
    shape = (parts, rows, block)
    return pl.pallas_call(
        column_sum_kernel,
        grid_spec=pltpu.PrefetchScalarGridSpec(
            num_scalar_prefetch=2,
            grid=(slots // TILE_GROUP,),
            in_specs=[pl.BlockSpec((TILE_GROUP, block, block), lambda i, s, c: (i, 0, 0))],
            out_specs=pl.BlockSpec(shape, lambda i, s, c: (0, 0, 0)),
            scratch_shapes=[pltpu.VMEM((parts * rows + 8, block), jnp.float32)],
        ),
        out_shape=jax.ShapeDtypeStruct(shape, jnp.float32),
        compiler_params=pltpu.CompilerParams(vmem_limit_bytes=16 * MIB),
        cost_estimate=pl.CostEstimate(
            flops=tiles.size, bytes_accessed=tiles.size * 2, transcendentals=0
        ),
        name="column_sums",
    )(source, count, tiles)


def block_topics(docs, w_in, w_out_t, host, width):
    hidden = jax.nn.gelu(
        jnp.dot(docs[...], w_in[...], preferred_element_type=jnp.float32), approximate=True
    ).astype(jnp.bfloat16)
    logits = lax.dot_general(w_out_t[...], hidden, NT, preferred_element_type=jnp.float32)
    powers = jnp.exp(logits - jnp.max(logits, axis=0, keepdims=True))
    probs = powers * (1.0 / jnp.sum(powers, axis=0, keepdims=True))
    high = probs.astype(jnp.bfloat16)
    low = (probs - high.astype(jnp.float32)).astype(jnp.bfloat16)
    index = host[0]
    digit = index // width
    within = index - digit * width
    picks = [jnp.where(digit == j, 1.0, 0.0).astype(jnp.bfloat16) for j in range(DIGITS)]
    left = jnp.concatenate([high * p for p in picks] + [low * p for p in picks], axis=0)
    places = lax.broadcasted_iota(jnp.int32, (width, index.shape[1]), 0)
    right = jnp.where(places == within, 1.0, 0.0).astype(jnp.bfloat16)
    return lax.dot_general(left, right, NT, preferred_element_type=jnp.float32)


def documents_kernel(place, docs, w_in, w_out_t, host, degrees, *rest):
    labels, outs, total = rest[:LABELS], rest[LABELS:-1], rest[-1]
    step = pl.program_id(0)
    topics = w_out_t.shape[0]
    width = total.shape[1]
    added = block_topics(docs, w_in, w_out_t, host, width)

    @pl.when(step == 0)
    def _():
        total[...] = added

    @pl.when(step > 0)
    def _():
        total[...] += added

    @pl.when(step == pl.num_programs(0) - 1)
    def _():
        per = outs[0].shape[0]
        hosts = DIGITS * width
        degree = sum(degrees[j] for j in range(1, degrees.shape[0])) + degrees[0]
        blocks, block = degree.shape
        wide = hosts + blocks // per * block
        for j, out in enumerate(outs):
            chunk = (place[0] ^ j) * per
            for d in range(DIGITS):
                first = pl.ds(pl.multiple_of(d * topics + chunk, 8), per)
                second = pl.ds(pl.multiple_of((DIGITS + d) * topics + chunk, 8), per)
                out[:, d * width : (d + 1) * width] = total[first, :] + total[second, :]
            for c in range(blocks // per):
                cols = slice(hosts + c * block, hosts + (c + 1) * block)
                out[:, cols] = degree[c * per : (c + 1) * per, :]
            out[:, wide:] = jnp.zeros((per, block), jnp.float32)
            for r, label in enumerate(labels):
                out[r : r + 1, wide : wide + label.shape[1]] = label[...].astype(jnp.float32)


def documents(docs, w_in, w_out, doc_host, hosts, split, place, degrees, labels):
    count, depth = docs.shape
    hid, topics = w_out.shape
    per = topics // split
    width = hosts // DIGITS
    steps = count // DOC_BLOCK
    shape = (per, hosts + hosts // per + degrees.shape[2])
    return pl.pallas_call(
        documents_kernel,
        grid_spec=pltpu.PrefetchScalarGridSpec(
            num_scalar_prefetch=1,
            grid=(steps,),
            in_specs=[
                pl.BlockSpec((DOC_BLOCK, depth), lambda i, p: (i, 0)),
                pl.BlockSpec((depth, hid), lambda i, p: (0, 0)),
                pl.BlockSpec((topics, hid), lambda i, p: (0, 0)),
                pl.BlockSpec((1, 1, DOC_BLOCK), lambda i, p: (i, 0, 0)),
                pl.BlockSpec(degrees.shape, lambda i, p: (0, 0, 0)),
            ]
            + [pl.BlockSpec(label.shape, lambda i, p: (0, 0)) for label in labels],
            out_specs=[pl.BlockSpec(shape, lambda i, p: (0, 0))] * split,
            scratch_shapes=[pltpu.VMEM((2 * DIGITS * topics, width), jnp.float32)],
        ),
        out_shape=[jax.ShapeDtypeStruct(shape, jnp.float32)] * split,
        compiler_params=pltpu.CompilerParams(vmem_limit_bytes=48 * MIB),
        cost_estimate=pl.CostEstimate(
            flops=2 * count * (depth * hid + hid * topics + 2 * topics * hosts),
            bytes_accessed=docs.size * 2,
            transcendentals=count * (hid + topics),
        ),
        name="documents",
    )(place, docs, w_in, w_out.T, doc_host.reshape(steps, 1, DOC_BLOCK), degrees, *labels)


def start_kernel(held, teleport, *rest):
    sums, rest = rest[: len(rest) - 2 * held - 4], rest[len(rest) - held - 4 :]
    sent, start, inverse, meta = rest[:4]
    per, hosts = start.shape
    blocks, block = teleport.shape
    member = teleport[...].astype(jnp.float32) * LIFT
    mass = jnp.zeros((per, 1), jnp.float32)
    tail = slice(hosts, hosts + hosts // per)
    packed = 1.0 / jnp.maximum(sum(s[:, tail] for s in sums[1:]) + sums[0][:, tail], 1.0)
    for c in range(blocks // per):
        inverse[c * per : (c + 1) * per, :] = packed[:, c * block : (c + 1) * block]
    for j, s in enumerate(sums):
        meta[j * LABELS : (j + 1) * LABELS, :] = s[:LABELS, tail.stop :].astype(jnp.int32)
    for b in range(blocks):
        cols = slice(b * block, (b + 1) * block)
        value = sum(s[:, cols] for s in sums[1:]) + sums[0][:, cols]
        value = value * member[b : b + 1, :]
        start[:, cols] = value
        sent[:, cols] = (value * inverse[b : b + 1, :]).astype(jnp.bfloat16)
        mass = mass + jnp.sum(value, axis=1, keepdims=True)
    lane = lax.broadcasted_iota(jnp.int32, (per, block), 1)
    first = mass.astype(jnp.bfloat16).astype(jnp.float32)
    second = (mass - first).astype(jnp.bfloat16).astype(jnp.float32)
    third = mass - first - second
    pieces = jnp.where(
        lane == 0, first, jnp.where(lane == 1, second, jnp.where(lane == 2, third, 0.0))
    )
    sent[:, blocks * block :] = pieces.astype(jnp.bfloat16)


def start_values(teleport, sums, block, held):
    per, _ = sums[0].shape
    hosts = teleport.shape[0]
    vmem = pl.BlockSpec(memory_space=pltpu.VMEM)
    keep = pl.BlockSpec(memory_space=pl.ANY)
    return pl.pallas_call(
        functools.partial(start_kernel, len(held)),
        in_specs=[vmem] * (1 + len(sums)) + [keep] * len(held),
        out_specs=[vmem] * 4 + [keep] * len(held),
        out_shape=[
            jax.ShapeDtypeStruct((per, hosts + block), jnp.bfloat16),
            jax.ShapeDtypeStruct((per, hosts), jnp.float32),
            jax.ShapeDtypeStruct((hosts // block, block), jnp.float32),
            jax.ShapeDtypeStruct((len(sums) * LABELS, block), jnp.int32),
        ]
        + [jax.ShapeDtypeStruct(array.shape, array.dtype) for array in held],
        input_output_aliases={1 + len(sums) + i: 4 + i for i in range(len(held))},
        compiler_params=pltpu.CompilerParams(vmem_limit_bytes=16 * MIB),
        name="start_values",
    )(teleport.reshape(hosts // block, block), *sums, *held)


def after_kernel(*refs):
    del refs


def after(value, ready):
    keep = pl.BlockSpec(memory_space=pl.ANY)
    return pl.pallas_call(
        after_kernel,
        in_specs=[keep] * (1 + len(ready)),
        out_specs=keep,
        out_shape=jax.ShapeDtypeStruct(value.shape, value.dtype),
        input_output_aliases={0: 0},
        compiler_params=pltpu.CompilerParams(vmem_limit_bytes=MIB),
        name="after",
    )(value, *ready)


def hop_kernel(first, last, parts, spans, scale, meta, here, *rest):
    shards, rest = rest[:parts][::-1], rest[parts:]
    chunks, rest = rest[: len(spans)], rest[len(spans) :]
    (tele, inverse), outs, (slabs, inflow) = rest[:2], rest[2:-2], rest[-2:]
    blocks, per, block = inflow.shape

    inflow[...] = jnp.zeros_like(inflow)
    slabs[parts * blocks] = jnp.zeros(slabs.shape[1:], slabs.dtype)
    for j, shard in enumerate(shards):
        for b in range(blocks):
            slabs[j * blocks + b] = shard[:, b * block : (b + 1) * block]

    empty = jnp.zeros((per, block), jnp.bfloat16)
    for tiles, (q, begin) in zip(chunks, spans):
        count = meta[q * LABELS + 2, 0]
        size = tiles.shape[0]
        groups = (jnp.clip(count - begin, 0, size) + (TILE_GROUP - 1)) // TILE_GROUP

        def group(step, carry):
            products = []
            for c in range(0, TILE_GROUP, 4):
                held, quad = [], []
                for i in range(4):
                    at = step * TILE_GROUP + c + i
                    source = meta[q * LABELS, begin + at] ^ here[0]
                    held.append(slabs[jnp.where(begin + at < count, source, parts * blocks)])
                    quad.append(tiles[at])
                left = jnp.concatenate(
                    [
                        jnp.concatenate([held[0], held[1], empty, empty], axis=0),
                        jnp.concatenate([empty, empty, held[2], held[3]], axis=0),
                    ],
                    axis=1,
                )
                right = jnp.concatenate(
                    [
                        jnp.concatenate(quad[:2], axis=0),
                        jnp.concatenate(quad[2:], axis=0),
                    ],
                    axis=1,
                )
                both = lax.dot_general(left, right, NT, preferred_element_type=jnp.float32)
                for i in range(4):
                    side = (i % 2) * block
                    products.append(both[i * per : (i + 1) * per, side : side + block])
            for i in range(TILE_GROUP):
                inflow[meta[q * LABELS + 1, begin + step * TILE_GROUP + i]] += products[i]
            return carry

        lax.fori_loop(0, groups, group, 0)

    if first:
        tail = sum(s[:, blocks * block :].astype(jnp.float32) for s in shards)
        mass = jnp.sum(tail, axis=1, keepdims=True)
    for b in range(blocks):
        cols = slice(b * block, (b + 1) * block)
        own = tele[:, cols]
        state = 0.85 * inflow[b] + 0.15 * own
        if first:
            state = state / mass
            outs[1][:, cols] = own / mass
        if last:
            inflow[b] = state * scale
        else:
            outs[0][:, cols] = (state * inverse[b : b + 1, :]).astype(jnp.bfloat16)
    if last:
        count = outs[0].shape[1] // block
        for j, out in enumerate(outs):
            start = (here[1] ^ j) * count
            for i in range(count):
                out[:, i * block : (i + 1) * block] = inflow[start + i]


def hop(first, last, meta, here, shards, sets, tele, inverse):
    per, hosts = tele.shape
    slots = sum(chunk.shape[0] for chunk in sets[0])
    block = sets[0][0].shape[1]
    blocks = hosts // block
    parts, split = len(shards), len(sets)
    chunks, spans = [], []
    for q, held in enumerate(sets):
        begin = 0
        for chunk in held:
            chunks.append(chunk)
            spans.append((q, begin))
            begin += chunk.shape[0]
    if last:
        out_shape = [jax.ShapeDtypeStruct((per, hosts // split), jnp.float32)] * split
    else:
        out_shape = [jax.ShapeDtypeStruct((per, hosts), jnp.bfloat16)]
        if first:
            out_shape.append(jax.ShapeDtypeStruct((per, hosts), jnp.float32))
    smem = pl.BlockSpec(memory_space=pltpu.SMEM)
    vmem = pl.BlockSpec(memory_space=pltpu.VMEM)
    return pl.pallas_call(
        functools.partial(hop_kernel, first, last, parts, spans, float(parts * hosts)),
        in_specs=[smem] * 2 + [vmem] * (parts + len(chunks) + 2),
        out_specs=[vmem] * len(out_shape),
        scratch_shapes=[
            pltpu.VMEM((parts * blocks + 1, per, block), jnp.bfloat16),
            pltpu.VMEM((blocks, per, block), jnp.float32),
        ],
        out_shape=out_shape,
        compiler_params=pltpu.CompilerParams(vmem_limit_bytes=HOP_MIB * MIB),
        cost_estimate=pl.CostEstimate(
            flops=2 * split * slots * block * block * per,
            bytes_accessed=split * slots * block * block * 2,
            transcendentals=0,
        ),
        name="hop",
    )(meta, here, *reversed(shards), *chunks, tele, inverse)


def finish_kernel(here, *rest):
    chunks, out = rest[:-1], rest[-1]
    per = chunks[0].shape[0]
    for j, chunk in enumerate(chunks):
        out[pl.ds(pl.multiple_of((here[1] ^ j) * per, 8), per), :] = chunk[...]


def finish(here, chunks):
    per, rows = chunks[0].shape
    topics = per * len(chunks)
    return pl.pallas_call(
        finish_kernel,
        in_specs=[pl.BlockSpec(memory_space=pltpu.SMEM)]
        + [pl.BlockSpec(memory_space=pltpu.VMEM)] * len(chunks),
        out_shape=jax.ShapeDtypeStruct((topics, rows), jnp.float32),
        compiler_params=pltpu.CompilerParams(vmem_limit_bytes=16 * MIB),
        name="finish",
    )(here, *chunks)


def spread(sent, axis):
    size = lax.axis_size(axis)
    held = {0: sent}
    for j in range(size - 2, 2, -2):
        held[j] = xor_send(sent, axis, j)
    held[1] = xor_send(sent, axis, 1)
    held[2] = xor_send(sent, axis, 2)
    for j in range(size - 2, 0, -2):
        held[j + 1] = xor_send(held[j], axis, 1)
    return [held[j] for j in range(size)]


def body(docs, w_in, w_out, doc_host, tiles, dst_block, src_block, tile_count, teleport):
    hosts = teleport.shape[0]
    slots, block, _ = tiles.shape
    parts, split = lax.axis_size("hst"), lax.axis_size("doc")
    blocks = hosts // block
    place = lax.axis_index("doc").astype(jnp.int32)
    here = jnp.stack([lax.axis_index("hst").astype(jnp.int32) * blocks, place])
    labels = [label.reshape(1, -1) for label in (src_block, dst_block, tile_count)]

    near = xor_send(tiles, "doc", 1)
    cut = 3 * slots // 4
    early, late = tiles[:cut], tiles[cut:]
    far = {j: [xor_send(early, "doc", j)] for j in range(2, split, 2)}
    degrees = column_sums(src_block, tile_count, tiles, parts, blocks)
    degrees = lax.all_to_all(degrees, "hst", split_axis=0, concat_axis=0, tiled=True)
    sums = documents(docs, w_in, w_out, doc_host, hosts, split, place.reshape(1), degrees, labels)
    sums = [sums[0]] + [xor_send(sums[j], "doc", j) for j in range(1, split)]
    crossed = [far[j][0] for j in range(2, split, 2)]
    sent, tele, inverse, meta, late, *crossed = start_values(
        teleport, sums, block, [late] + crossed
    )
    for j in range(2, split, 2):
        far[j] = [crossed[j // 2 - 1], xor_send(late, "doc", j)]
        far[j + 1] = [xor_send(far[j][0], "doc", 1)]
    for step in range(HOPS):
        first, last = step == 0, step == HOPS - 1
        shards = spread(sent, "hst")
        if first:
            for j in range(2, split, 2):
                far[j][1] = after(far[j][1], shards[1:])
                far[j + 1].append(xor_send(far[j][1], "doc", 1))
            sets = [[tiles], [near]] + [far[j] for j in range(2, split)]
        outs = hop(first, last, meta, here, shards, sets, tele, inverse)
        sent = outs[0]
        if first:
            tele = outs[1]
    chunks = [outs[0]] + [xor_send(outs[j], "doc", j) for j in range(1, split)]
    return finish(here, chunks).T


def solution(mesh):
    placed = (
        P(("hst", "doc"), None),
        P(),
        P(),
        P(("hst", "doc")),
        P(("hst", "doc"), None, None),
        P(("hst", "doc")),
        P(("hst", "doc")),
        P(("hst", "doc")),
        P("hst"),
    )
    return jax.shard_map(
        body, mesh=mesh, in_specs=placed, out_specs=P(("hst", "doc"), None), check_vma=False
    )
```

```python
import functools

import jax
import jax.numpy as jnp
from jax import lax
from jax.experimental import pallas as pl
from jax.experimental.pallas import tpu as pltpu
from jax.sharding import PartitionSpec as P

HOPS = 3
LABELS = 3
DIGITS = 4
DOC_BLOCK = 1024
TILE_GROUP = 16
HOP_MIB = 16
LIFT = 2.0**64
NT = (((1,), (1,)), ((), ()))
MIB = 1 << 20


def xor_send(value, axis, step):
    size = lax.axis_size(axis)
    return lax.ppermute(value, axis, [(i, i ^ step) for i in range(size)])


def column_sum_kernel(source, count, tiles, out, total):
    step = pl.program_id(0)
    parts, rows, _ = out.shape

    @pl.when(step == 0)
    def _():
        total[...] = jnp.zeros_like(total)

    for i in range(TILE_GROUP):
        k = step * TILE_GROUP + i
        row = jnp.where(k < count[0], source[k], parts * rows)
        part = jnp.sum(tiles[i].astype(jnp.float32), axis=0, keepdims=True)
        total[pl.ds(row, 1), :] += part

    @pl.when(step == pl.num_programs(0) - 1)
    def _():
        for j in range(parts):
            out[j] = total[j * rows : (j + 1) * rows, :]


def column_sums(source, count, tiles, parts, rows):
    slots, block, _ = tiles.shape
    shape = (parts, rows, block)
    return pl.pallas_call(
        column_sum_kernel,
        grid_spec=pltpu.PrefetchScalarGridSpec(
            num_scalar_prefetch=2,
            grid=(slots // TILE_GROUP,),
            in_specs=[pl.BlockSpec((TILE_GROUP, block, block), lambda i, s, c: (i, 0, 0))],
            out_specs=pl.BlockSpec(shape, lambda i, s, c: (0, 0, 0)),
            scratch_shapes=[pltpu.VMEM((parts * rows + 8, block), jnp.float32)],
        ),
        out_shape=jax.ShapeDtypeStruct(shape, jnp.float32),
        compiler_params=pltpu.CompilerParams(vmem_limit_bytes=16 * MIB),
        cost_estimate=pl.CostEstimate(
            flops=tiles.size, bytes_accessed=tiles.size * 2, transcendentals=0
        ),
        name="column_sums",
    )(source, count, tiles)


def block_topics(docs, w_in, w_out_t, host, width):
    hidden = jax.nn.gelu(
        jnp.dot(docs[...], w_in[...], preferred_element_type=jnp.float32), approximate=True
    ).astype(jnp.bfloat16)
    logits = lax.dot_general(w_out_t[...], hidden, NT, preferred_element_type=jnp.float32)
    powers = jnp.exp(logits - jnp.max(logits, axis=0, keepdims=True))
    probs = powers * (1.0 / jnp.sum(powers, axis=0, keepdims=True))
    high = probs.astype(jnp.bfloat16)
    low = (probs - high.astype(jnp.float32)).astype(jnp.bfloat16)
    index = host[0]
    digit = index // width
    within = index - digit * width
    picks = [jnp.where(digit == j, 1.0, 0.0).astype(jnp.bfloat16) for j in range(DIGITS)]
    left = jnp.concatenate([high * p for p in picks] + [low * p for p in picks], axis=0)
    places = lax.broadcasted_iota(jnp.int32, (width, index.shape[1]), 0)
    right = jnp.where(places == within, 1.0, 0.0).astype(jnp.bfloat16)
    return lax.dot_general(left, right, NT, preferred_element_type=jnp.float32)


def documents_kernel(place, docs, w_in, w_out_t, host, degrees, *rest):
    labels, outs, total = rest[:LABELS], rest[LABELS:-1], rest[-1]
    step = pl.program_id(0)
    topics = w_out_t.shape[0]
    width = total.shape[1]
    added = block_topics(docs, w_in, w_out_t, host, width)

    @pl.when(step == 0)
    def _():
        total[...] = added

    @pl.when(step > 0)
    def _():
        total[...] += added

    @pl.when(step == pl.num_programs(0) - 1)
    def _():
        per = outs[0].shape[0]
        hosts = DIGITS * width
        degree = sum(degrees[j] for j in range(1, degrees.shape[0])) + degrees[0]
        blocks, block = degree.shape
        wide = hosts + blocks // per * block
        for j, out in enumerate(outs):
            chunk = (place[0] ^ j) * per
            for d in range(DIGITS):
                first = pl.ds(pl.multiple_of(d * topics + chunk, 8), per)
                second = pl.ds(pl.multiple_of((DIGITS + d) * topics + chunk, 8), per)
                out[:, d * width : (d + 1) * width] = total[first, :] + total[second, :]
            for c in range(blocks // per):
                cols = slice(hosts + c * block, hosts + (c + 1) * block)
                out[:, cols] = degree[c * per : (c + 1) * per, :]
            out[:, wide:] = jnp.zeros((per, block), jnp.float32)
            for r, label in enumerate(labels):
                out[r : r + 1, wide : wide + label.shape[1]] = label[...].astype(jnp.float32)


def documents(docs, w_in, w_out, doc_host, hosts, split, place, degrees, labels):
    count, depth = docs.shape
    hid, topics = w_out.shape
    per = topics // split
    width = hosts // DIGITS
    steps = count // DOC_BLOCK
    shape = (per, hosts + hosts // per + degrees.shape[2])
    return pl.pallas_call(
        documents_kernel,
        grid_spec=pltpu.PrefetchScalarGridSpec(
            num_scalar_prefetch=1,
            grid=(steps,),
            in_specs=[
                pl.BlockSpec((DOC_BLOCK, depth), lambda i, p: (i, 0)),
                pl.BlockSpec((depth, hid), lambda i, p: (0, 0)),
                pl.BlockSpec((topics, hid), lambda i, p: (0, 0)),
                pl.BlockSpec((1, 1, DOC_BLOCK), lambda i, p: (i, 0, 0)),
                pl.BlockSpec(degrees.shape, lambda i, p: (0, 0, 0)),
            ]
            + [pl.BlockSpec(label.shape, lambda i, p: (0, 0)) for label in labels],
            out_specs=[pl.BlockSpec(shape, lambda i, p: (0, 0))] * split,
            scratch_shapes=[pltpu.VMEM((2 * DIGITS * topics, width), jnp.float32)],
        ),
        out_shape=[jax.ShapeDtypeStruct(shape, jnp.float32)] * split,
        compiler_params=pltpu.CompilerParams(vmem_limit_bytes=48 * MIB),
        cost_estimate=pl.CostEstimate(
            flops=2 * count * (depth * hid + hid * topics + 2 * topics * hosts),
            bytes_accessed=docs.size * 2,
            transcendentals=count * (hid + topics),
        ),
        name="documents",
    )(place, docs, w_in, w_out.T, doc_host.reshape(steps, 1, DOC_BLOCK), degrees, *labels)


def start_kernel(held, teleport, *rest):
    sums, rest = rest[: len(rest) - 2 * held - 4], rest[len(rest) - held - 4 :]
    sent, start, inverse, meta = rest[:4]
    per, hosts = start.shape
    blocks, block = teleport.shape
    member = teleport[...].astype(jnp.float32) * LIFT
    mass = jnp.zeros((per, 1), jnp.float32)
    tail = slice(hosts, hosts + hosts // per)
    packed = 1.0 / jnp.maximum(sum(s[:, tail] for s in sums[1:]) + sums[0][:, tail], 1.0)
    for c in range(blocks // per):
        inverse[c * per : (c + 1) * per, :] = packed[:, c * block : (c + 1) * block]
    for j, s in enumerate(sums):
        meta[j * LABELS : (j + 1) * LABELS, :] = s[:LABELS, tail.stop :].astype(jnp.int32)
    for b in range(blocks):
        cols = slice(b * block, (b + 1) * block)
        value = sum(s[:, cols] for s in sums[1:]) + sums[0][:, cols]
        value = value * member[b : b + 1, :]
        start[:, cols] = value
        sent[:, cols] = (value * inverse[b : b + 1, :]).astype(jnp.bfloat16)
        mass = mass + jnp.sum(value, axis=1, keepdims=True)
    lane = lax.broadcasted_iota(jnp.int32, (per, block), 1)
    first = mass.astype(jnp.bfloat16).astype(jnp.float32)
    second = (mass - first).astype(jnp.bfloat16).astype(jnp.float32)
    third = mass - first - second
    pieces = jnp.where(
        lane == 0, first, jnp.where(lane == 1, second, jnp.where(lane == 2, third, 0.0))
    )
    sent[:, blocks * block :] = pieces.astype(jnp.bfloat16)


def start_values(teleport, sums, block, held):
    per, _ = sums[0].shape
    hosts = teleport.shape[0]
    vmem = pl.BlockSpec(memory_space=pltpu.VMEM)
    keep = pl.BlockSpec(memory_space=pl.ANY)
    return pl.pallas_call(
        functools.partial(start_kernel, len(held)),
        in_specs=[vmem] * (1 + len(sums)) + [keep] * len(held),
        out_specs=[vmem] * 4 + [keep] * len(held),
        out_shape=[
            jax.ShapeDtypeStruct((per, hosts + block), jnp.bfloat16),
            jax.ShapeDtypeStruct((per, hosts), jnp.float32),
            jax.ShapeDtypeStruct((hosts // block, block), jnp.float32),
            jax.ShapeDtypeStruct((len(sums) * LABELS, block), jnp.int32),
        ]
        + [jax.ShapeDtypeStruct(array.shape, array.dtype) for array in held],
        input_output_aliases={1 + len(sums) + i: 4 + i for i in range(len(held))},
        compiler_params=pltpu.CompilerParams(vmem_limit_bytes=16 * MIB),
        name="start_values",
    )(teleport.reshape(hosts // block, block), *sums, *held)


def after_kernel(*refs):
    del refs


def after(value, ready):
    keep = pl.BlockSpec(memory_space=pl.ANY)
    return pl.pallas_call(
        after_kernel,
        in_specs=[keep] * (1 + len(ready)),
        out_specs=keep,
        out_shape=jax.ShapeDtypeStruct(value.shape, value.dtype),
        input_output_aliases={0: 0},
        compiler_params=pltpu.CompilerParams(vmem_limit_bytes=MIB),
        name="after",
    )(value, *ready)


def hop_kernel(first, last, parts, spans, scale, meta, part, place, *rest):
    shards, rest = rest[:parts][::-1], rest[parts:]
    chunks, rest = rest[: len(spans)], rest[len(spans) :]
    (tele, inverse), outs, (slabs, inflow) = rest[:2], rest[2:-2], rest[-2:]
    blocks, per, block = inflow.shape

    inflow[...] = jnp.zeros_like(inflow)
    slabs[parts * blocks] = jnp.zeros(slabs.shape[1:], slabs.dtype)
    for j, shard in enumerate(shards):
        for b in range(blocks):
            slabs[j * blocks + b] = shard[:, b * block : (b + 1) * block]

    split = meta.shape[0] // LABELS
    empty = jnp.zeros((per, block), jnp.bfloat16)
    counts = [meta[q * LABELS + 2, 0] for q in range(split)]
    most = functools.reduce(jnp.maximum, counts)
    edges = sorted({begin for _, begin in spans})
    edges.append(edges[-1] + chunks[-1].shape[0])

    def quads(q, tiles, begin, at):
        for c in range(0, TILE_GROUP, 4):
            held, quad, into = [], [], []
            for i in range(c, c + 4):
                k = begin + at + i
                source = meta[q * LABELS, k] ^ (part[0] * blocks)
                held.append(slabs[jnp.where(k < counts[q], source, parts * blocks)])
                quad.append(tiles[at + i])
                into.append(meta[q * LABELS + 1, k])
            left = jnp.concatenate(
                [
                    jnp.concatenate([held[0], held[1], empty, empty], axis=0),
                    jnp.concatenate([empty, empty, held[2], held[3]], axis=0),
                ],
                axis=1,
            )
            right = jnp.concatenate(
                [jnp.concatenate(quad[:2], axis=0), jnp.concatenate(quad[2:], axis=0)], axis=1
            )
            both = lax.dot_general(left, right, NT, preferred_element_type=jnp.float32)
            for i in range(4):
                side = (i % 2) * block
                inflow[into[i]] += both[i * per : (i + 1) * per, side : side + block]

    for first_slot, end_slot in zip(edges[:-1], edges[1:]):
        groups = jnp.clip(most - first_slot, 0, end_slot - first_slot) + (TILE_GROUP - 1)

        def group(step, carry):
            for q in range(split):
                for tiles, (owner, begin) in zip(chunks, spans):
                    if owner == q and begin <= first_slot < begin + tiles.shape[0]:
                        quads(q, tiles, begin, first_slot - begin + step * TILE_GROUP)
            return carry

        lax.fori_loop(0, groups // TILE_GROUP, group, 0)

    if first:
        tail = sum(s[:, blocks * block :].astype(jnp.float32) for s in shards)
        mass = jnp.sum(tail, axis=1, keepdims=True)
    for b in range(blocks):
        cols = slice(b * block, (b + 1) * block)
        own = tele[:, cols]
        state = 0.85 * inflow[b] + 0.15 * own
        if first:
            state = state / mass
            outs[1][:, cols] = own / mass
        if last:
            inflow[b] = state * scale
        else:
            outs[0][:, cols] = (state * inverse[b : b + 1, :]).astype(jnp.bfloat16)
    if last:
        count = outs[0].shape[1] // block
        for j, out in enumerate(outs):
            start = (place[0] ^ j) * count
            for i in range(count):
                out[:, i * block : (i + 1) * block] = inflow[start + i]


def hop(first, last, meta, part, place, shards, sets, tele, inverse):
    per, hosts = tele.shape
    slots = sum(chunk.shape[0] for chunk in sets[0])
    block = sets[0][0].shape[1]
    blocks = hosts // block
    parts, split = len(shards), len(sets)
    chunks, spans = [], []
    for q, held in enumerate(sets):
        begin = 0
        for chunk in held:
            chunks.append(chunk)
            spans.append((q, begin))
            begin += chunk.shape[0]
    if last:
        out_shape = [jax.ShapeDtypeStruct((per, hosts // split), jnp.float32)] * split
    else:
        out_shape = [jax.ShapeDtypeStruct((per, hosts), jnp.bfloat16)]
        if first:
            out_shape.append(jax.ShapeDtypeStruct((per, hosts), jnp.float32))
    smem = pl.BlockSpec(memory_space=pltpu.SMEM)
    vmem = pl.BlockSpec(memory_space=pltpu.VMEM)
    return pl.pallas_call(
        functools.partial(hop_kernel, first, last, parts, spans, float(parts * hosts)),
        in_specs=[smem] * 3 + [vmem] * (parts + len(chunks) + 2),
        out_specs=[vmem] * len(out_shape),
        scratch_shapes=[
            pltpu.VMEM((parts * blocks + 1, per, block), jnp.bfloat16),
            pltpu.VMEM((blocks, per, block), jnp.float32),
        ],
        out_shape=out_shape,
        compiler_params=pltpu.CompilerParams(vmem_limit_bytes=HOP_MIB * MIB),
        cost_estimate=pl.CostEstimate(
            flops=2 * split * slots * block * block * per,
            bytes_accessed=split * slots * block * block * 2,
            transcendentals=0,
        ),
        name="hop",
    )(meta, part, place, *reversed(shards), *chunks, tele, inverse)


def finish_kernel(place, *rest):
    chunks, out = rest[:-1], rest[-1]
    per = chunks[0].shape[0]
    for j, chunk in enumerate(chunks):
        out[pl.ds(pl.multiple_of((place[0] ^ j) * per, 8), per), :] = chunk[...]


def finish(place, chunks):
    per, rows = chunks[0].shape
    topics = per * len(chunks)
    return pl.pallas_call(
        finish_kernel,
        in_specs=[pl.BlockSpec(memory_space=pltpu.SMEM)]
        + [pl.BlockSpec(memory_space=pltpu.VMEM)] * len(chunks),
        out_shape=jax.ShapeDtypeStruct((topics, rows), jnp.float32),
        compiler_params=pltpu.CompilerParams(vmem_limit_bytes=16 * MIB),
        name="finish",
    )(place, *chunks)


def spread(sent, axis):
    size = lax.axis_size(axis)
    held = {0: sent}
    for j in range(size - 2, 2, -2):
        held[j] = xor_send(sent, axis, j)
    held[1] = xor_send(sent, axis, 1)
    held[2] = xor_send(sent, axis, 2)
    for j in range(size - 2, 0, -2):
        held[j + 1] = xor_send(held[j], axis, 1)
    return [held[j] for j in range(size)]


def body(docs, w_in, w_out, doc_host, tiles, dst_block, src_block, tile_count, teleport):
    hosts = teleport.shape[0]
    slots, block, _ = tiles.shape
    parts, split = lax.axis_size("hst"), lax.axis_size("doc")
    blocks = hosts // block
    part = lax.axis_index("hst").astype(jnp.int32).reshape(1)
    place = lax.axis_index("doc").astype(jnp.int32).reshape(1)
    labels = [label.reshape(1, -1) for label in (src_block, dst_block, tile_count)]

    near = xor_send(tiles, "doc", 1)
    cut = 3 * slots // 4
    early, late = tiles[:cut], tiles[cut:]
    far = {j: [xor_send(early, "doc", j)] for j in range(2, split, 2)}
    degrees = column_sums(src_block, tile_count, tiles, parts, blocks)
    degrees = lax.all_to_all(degrees, "hst", split_axis=0, concat_axis=0, tiled=True)
    sums = documents(docs, w_in, w_out, doc_host, hosts, split, place, degrees, labels)
    sums = [sums[0]] + [xor_send(sums[j], "doc", j) for j in range(1, split)]
    for j in range(2, split, 2):
        far[j][0] = after(far[j][0], [sums[1]])
        far[j + 1] = [xor_send(far[j][0], "doc", 1)]
    sent, tele, inverse, meta, late = start_values(teleport, sums, block, [late])
    for j in range(2, split, 2):
        far[j].append(xor_send(late, "doc", j))
    for step in range(HOPS):
        first, last = step == 0, step == HOPS - 1
        shards = spread(sent, "hst")
        if first:
            for j in range(2, split, 2):
                far[j][1] = after(far[j][1], shards[1:])
                far[j + 1].append(xor_send(far[j][1], "doc", 1))
            sets = [[tiles], [near]] + [far[j] for j in range(2, split)]
        outs = hop(first, last, meta, part, place, shards, sets, tele, inverse)
        sent = outs[0]
        if first:
            tele = outs[1]
    chunks = [outs[0]] + [xor_send(outs[j], "doc", j) for j in range(1, split)]
    return finish(place, chunks).T


def solution(mesh):
    placed = (
        P(("hst", "doc"), None),
        P(),
        P(),
        P(("hst", "doc")),
        P(("hst", "doc"), None, None),
        P(("hst", "doc")),
        P(("hst", "doc")),
        P(("hst", "doc")),
        P("hst"),
    )
    return jax.shard_map(
        body, mesh=mesh, in_specs=placed, out_specs=P(("hst", "doc"), None), check_vma=False
    )
```

```python
import functools

import jax
import jax.numpy as jnp
from jax import lax
from jax.experimental import pallas as pl
from jax.experimental.pallas import tpu as pltpu
from jax.sharding import PartitionSpec as P

HOPS = 3
LABELS = 3
DIGITS = 4
DOC_BLOCK = 1024
TILE_GROUP = 16
HOP_MIB = 16
LIFT = 2.0**64
NT = (((1,), (1,)), ((), ()))
MIB = 1 << 20


def xor_send(value, axis, step):
    size = lax.axis_size(axis)
    return lax.ppermute(value, axis, [(i, i ^ step) for i in range(size)])


def column_sum_kernel(source, count, tiles, out, total):
    step = pl.program_id(0)
    parts, rows, _ = out.shape

    @pl.when(step == 0)
    def _():
        total[...] = jnp.zeros_like(total)

    for i in range(TILE_GROUP):
        k = step * TILE_GROUP + i
        row = jnp.where(k < count[0], source[k], parts * rows)
        part = jnp.sum(tiles[i].astype(jnp.float32), axis=0, keepdims=True)
        total[pl.ds(row, 1), :] += part

    @pl.when(step == pl.num_programs(0) - 1)
    def _():
        for j in range(parts):
            out[j] = total[j * rows : (j + 1) * rows, :]


def column_sums(source, count, tiles, parts, rows):
    slots, block, _ = tiles.shape
    shape = (parts, rows, block)
    return pl.pallas_call(
        column_sum_kernel,
        grid_spec=pltpu.PrefetchScalarGridSpec(
            num_scalar_prefetch=2,
            grid=(slots // TILE_GROUP,),
            in_specs=[pl.BlockSpec((TILE_GROUP, block, block), lambda i, s, c: (i, 0, 0))],
            out_specs=pl.BlockSpec(shape, lambda i, s, c: (0, 0, 0)),
            scratch_shapes=[pltpu.VMEM((parts * rows + 8, block), jnp.float32)],
        ),
        out_shape=jax.ShapeDtypeStruct(shape, jnp.float32),
        compiler_params=pltpu.CompilerParams(vmem_limit_bytes=16 * MIB),
        cost_estimate=pl.CostEstimate(
            flops=tiles.size, bytes_accessed=tiles.size * 2, transcendentals=0
        ),
        name="column_sums",
    )(source, count, tiles)


def block_topics(docs, w_in, w_out_t, host, width):
    hidden = jax.nn.gelu(
        jnp.dot(docs[...], w_in[...], preferred_element_type=jnp.float32), approximate=True
    ).astype(jnp.bfloat16)
    logits = lax.dot_general(w_out_t[...], hidden, NT, preferred_element_type=jnp.float32)
    powers = jnp.exp(logits - jnp.max(logits, axis=0, keepdims=True))
    probs = powers * (1.0 / jnp.sum(powers, axis=0, keepdims=True))
    high = probs.astype(jnp.bfloat16)
    low = (probs - high.astype(jnp.float32)).astype(jnp.bfloat16)
    index = host[0]
    digit = index // width
    within = index - digit * width
    picks = [jnp.where(digit == j, 1.0, 0.0).astype(jnp.bfloat16) for j in range(DIGITS)]
    left = jnp.concatenate([high * p for p in picks] + [low * p for p in picks], axis=0)
    places = lax.broadcasted_iota(jnp.int32, (width, index.shape[1]), 0)
    right = jnp.where(places == within, 1.0, 0.0).astype(jnp.bfloat16)
    return lax.dot_general(left, right, NT, preferred_element_type=jnp.float32)


def documents_kernel(place, part, docs, w_in, w_out_t, host, degrees, *rest):
    labels, outs, total = rest[:LABELS], rest[LABELS:-1], rest[-1]
    step = pl.program_id(0)
    topics = w_out_t.shape[0]
    width = total.shape[1]
    added = block_topics(docs, w_in, w_out_t, host, width)

    @pl.when(step == 0)
    def _():
        total[...] = added

    @pl.when(step > 0)
    def _():
        total[...] += added

    @pl.when(step == pl.num_programs(0) - 1)
    def _():
        per = outs[0].shape[0]
        hosts = DIGITS * width
        degree = sum(degrees[j] for j in range(1, degrees.shape[0])) + degrees[0]
        blocks, block = degree.shape
        wide = hosts + blocks // per * block
        for j, out in enumerate(outs):
            chunk = (place[0] ^ j) * per
            for d in range(DIGITS):
                first = pl.ds(pl.multiple_of(d * topics + chunk, 8), per)
                second = pl.ds(pl.multiple_of((DIGITS + d) * topics + chunk, 8), per)
                out[:, d * width : (d + 1) * width] = total[first, :] + total[second, :]
            for c in range(blocks // per):
                cols = slice(hosts + c * block, hosts + (c + 1) * block)
                out[:, cols] = degree[c * per : (c + 1) * per, :]
            out[:, wide:] = jnp.zeros((per, block), jnp.float32)
            for r, label in enumerate(labels):
                out[r : r + 1, wide : wide + label.shape[1]] = label[...].astype(jnp.float32)


def documents(docs, w_in, w_out, doc_host, hosts, split, place, part, degrees, labels):
    count, depth = docs.shape
    hid, topics = w_out.shape
    per = topics // split
    width = hosts // DIGITS
    steps = count // DOC_BLOCK
    shape = (per, hosts + hosts // per + degrees.shape[2])
    return pl.pallas_call(
        documents_kernel,
        grid_spec=pltpu.PrefetchScalarGridSpec(
            num_scalar_prefetch=2,
            grid=(steps,),
            in_specs=[
                pl.BlockSpec((DOC_BLOCK, depth), lambda i, *p: (i, 0)),
                pl.BlockSpec((depth, hid), lambda i, *p: (0, 0)),
                pl.BlockSpec((topics, hid), lambda i, *p: (0, 0)),
                pl.BlockSpec((1, 1, DOC_BLOCK), lambda i, *p: (i, 0, 0)),
                pl.BlockSpec(degrees.shape, lambda i, *p: (0, 0, 0)),
            ]
            + [pl.BlockSpec(label.shape, lambda i, *p: (0, 0)) for label in labels],
            out_specs=[pl.BlockSpec(shape, lambda i, *p: (0, 0))] * split,
            scratch_shapes=[pltpu.VMEM((2 * DIGITS * topics, width), jnp.float32)],
        ),
        out_shape=[jax.ShapeDtypeStruct(shape, jnp.float32)] * split,
        compiler_params=pltpu.CompilerParams(vmem_limit_bytes=48 * MIB),
        cost_estimate=pl.CostEstimate(
            flops=2 * count * (depth * hid + hid * topics + 2 * topics * hosts),
            bytes_accessed=docs.size * 2,
            transcendentals=count * (hid + topics),
        ),
        name="documents",
    )(place, part, docs, w_in, w_out.T, doc_host.reshape(steps, 1, DOC_BLOCK), degrees, *labels)


def start_kernel(held, teleport, *rest):
    sums, rest = rest[: len(rest) - 2 * held - 4], rest[len(rest) - held - 4 :]
    sent, start, inverse, meta = rest[:4]
    per, hosts = start.shape
    blocks, block = teleport.shape
    member = teleport[...].astype(jnp.float32) * LIFT
    mass = jnp.zeros((per, 1), jnp.float32)
    tail = slice(hosts, hosts + hosts // per)
    packed = 1.0 / jnp.maximum(sum(s[:, tail] for s in sums[1:]) + sums[0][:, tail], 1.0)
    for c in range(blocks // per):
        inverse[c * per : (c + 1) * per, :] = packed[:, c * block : (c + 1) * block]
    for j, s in enumerate(sums):
        meta[j * LABELS : (j + 1) * LABELS, :] = s[:LABELS, tail.stop :].astype(jnp.int32)
    for b in range(blocks):
        cols = slice(b * block, (b + 1) * block)
        value = sum(s[:, cols] for s in sums[1:]) + sums[0][:, cols]
        value = value * member[b : b + 1, :]
        start[:, cols] = value
        sent[:, cols] = (value * inverse[b : b + 1, :]).astype(jnp.bfloat16)
        mass = mass + jnp.sum(value, axis=1, keepdims=True)
    lane = lax.broadcasted_iota(jnp.int32, (per, block), 1)
    first = mass.astype(jnp.bfloat16).astype(jnp.float32)
    second = (mass - first).astype(jnp.bfloat16).astype(jnp.float32)
    third = mass - first - second
    pieces = jnp.where(
        lane == 0, first, jnp.where(lane == 1, second, jnp.where(lane == 2, third, 0.0))
    )
    sent[:, blocks * block :] = pieces.astype(jnp.bfloat16)


def start_values(teleport, sums, block, held):
    per, _ = sums[0].shape
    hosts = teleport.shape[0]
    vmem = pl.BlockSpec(memory_space=pltpu.VMEM)
    keep = pl.BlockSpec(memory_space=pl.ANY)
    return pl.pallas_call(
        functools.partial(start_kernel, len(held)),
        in_specs=[vmem] * (1 + len(sums)) + [keep] * len(held),
        out_specs=[vmem] * 4 + [keep] * len(held),
        out_shape=[
            jax.ShapeDtypeStruct((per, hosts + block), jnp.bfloat16),
            jax.ShapeDtypeStruct((per, hosts), jnp.float32),
            jax.ShapeDtypeStruct((hosts // block, block), jnp.float32),
            jax.ShapeDtypeStruct((len(sums) * LABELS, block), jnp.int32),
        ]
        + [jax.ShapeDtypeStruct(array.shape, array.dtype) for array in held],
        input_output_aliases={1 + len(sums) + i: 4 + i for i in range(len(held))},
        compiler_params=pltpu.CompilerParams(vmem_limit_bytes=16 * MIB),
        name="start_values",
    )(teleport.reshape(hosts // block, block), *sums, *held)


def after_kernel(*refs):
    del refs


def after(value, ready):
    keep = pl.BlockSpec(memory_space=pl.ANY)
    return pl.pallas_call(
        after_kernel,
        in_specs=[keep] * (1 + len(ready)),
        out_specs=keep,
        out_shape=jax.ShapeDtypeStruct(value.shape, value.dtype),
        input_output_aliases={0: 0},
        compiler_params=pltpu.CompilerParams(vmem_limit_bytes=MIB),
        name="after",
    )(value, *ready)


def hop_kernel(first, last, parts, spans, scale, meta, part, place, *rest):
    shards, rest = rest[:parts][::-1], rest[parts:]
    chunks, rest = rest[: len(spans)], rest[len(spans) :]
    (tele, inverse), outs, (slabs, inflow) = rest[:2], rest[2:-2], rest[-2:]
    blocks, per, block = inflow.shape

    inflow[...] = jnp.zeros_like(inflow)
    slabs[parts * blocks] = jnp.zeros(slabs.shape[1:], slabs.dtype)
    for j, shard in enumerate(shards):
        for b in range(blocks):
            slabs[j * blocks + b] = shard[:, b * block : (b + 1) * block]

    split = meta.shape[0] // LABELS
    empty = jnp.zeros((per, block), jnp.bfloat16)
    counts = [meta[q * LABELS + 2, 0] for q in range(split)]
    most = functools.reduce(jnp.maximum, counts)
    edges = sorted({begin for _, begin in spans})
    edges.append(edges[-1] + chunks[-1].shape[0])

    def quads(q, tiles, begin, at):
        for c in range(0, TILE_GROUP, 4):
            held, quad, into = [], [], []
            for i in range(c, c + 4):
                k = begin + at + i
                source = meta[q * LABELS, k] ^ (part[0] * blocks)
                held.append(slabs[jnp.where(k < counts[q], source, parts * blocks)])
                quad.append(tiles[at + i])
                into.append(meta[q * LABELS + 1, k])
            left = jnp.concatenate(
                [
                    jnp.concatenate([held[0], held[1], empty, empty], axis=0),
                    jnp.concatenate([empty, empty, held[2], held[3]], axis=0),
                ],
                axis=1,
            )
            right = jnp.concatenate(
                [jnp.concatenate(quad[:2], axis=0), jnp.concatenate(quad[2:], axis=0)], axis=1
            )
            both = lax.dot_general(left, right, NT, preferred_element_type=jnp.float32)
            for i in range(4):
                side = (i % 2) * block
                inflow[into[i]] += both[i * per : (i + 1) * per, side : side + block]

    for first_slot, end_slot in zip(edges[:-1], edges[1:]):
        groups = jnp.clip(most - first_slot, 0, end_slot - first_slot) + (TILE_GROUP - 1)

        def group(step, carry):
            for q in range(split):
                for tiles, (owner, begin) in zip(chunks, spans):
                    if owner == q and begin <= first_slot < begin + tiles.shape[0]:
                        quads(q, tiles, begin, first_slot - begin + step * TILE_GROUP)
            return carry

        lax.fori_loop(0, groups // TILE_GROUP, group, 0)

    if first:
        tail = sum(s[:, blocks * block :].astype(jnp.float32) for s in shards)
        mass = jnp.sum(tail, axis=1, keepdims=True)
    for b in range(blocks):
        cols = slice(b * block, (b + 1) * block)
        own = tele[:, cols]
        state = 0.85 * inflow[b] + 0.15 * own
        if first:
            state = state / mass
            outs[1][:, cols] = own / mass
        if last:
            inflow[b] = state * scale
        else:
            outs[0][:, cols] = (state * inverse[b : b + 1, :]).astype(jnp.bfloat16)
    if last:
        count = outs[0].shape[1] // block
        for j, out in enumerate(outs):
            start = (place[0] ^ j) * count
            for i in range(count):
                out[:, i * block : (i + 1) * block] = inflow[start + i]


def hop(first, last, meta, part, place, shards, sets, tele, inverse):
    per, hosts = tele.shape
    slots = sum(chunk.shape[0] for chunk in sets[0])
    block = sets[0][0].shape[1]
    blocks = hosts // block
    parts, split = len(shards), len(sets)
    chunks, spans = [], []
    for q, held in enumerate(sets):
        begin = 0
        for chunk in held:
            chunks.append(chunk)
            spans.append((q, begin))
            begin += chunk.shape[0]
    if last:
        out_shape = [jax.ShapeDtypeStruct((per, hosts // split), jnp.float32)] * split
    else:
        out_shape = [jax.ShapeDtypeStruct((per, hosts), jnp.bfloat16)]
        if first:
            out_shape.append(jax.ShapeDtypeStruct((per, hosts), jnp.float32))
    smem = pl.BlockSpec(memory_space=pltpu.SMEM)
    vmem = pl.BlockSpec(memory_space=pltpu.VMEM)
    return pl.pallas_call(
        functools.partial(hop_kernel, first, last, parts, spans, float(parts * hosts)),
        in_specs=[smem] * 3 + [vmem] * (parts + len(chunks) + 2),
        out_specs=[vmem] * len(out_shape),
        scratch_shapes=[
            pltpu.VMEM((parts * blocks + 1, per, block), jnp.bfloat16),
            pltpu.VMEM((blocks, per, block), jnp.float32),
        ],
        out_shape=out_shape,
        compiler_params=pltpu.CompilerParams(vmem_limit_bytes=HOP_MIB * MIB),
        cost_estimate=pl.CostEstimate(
            flops=2 * split * slots * block * block * per,
            bytes_accessed=split * slots * block * block * 2,
            transcendentals=0,
        ),
        name="hop",
    )(meta, part, place, *reversed(shards), *chunks, tele, inverse)


def finish_kernel(place, *rest):
    chunks, out = rest[:-1], rest[-1]
    per = chunks[0].shape[0]
    for j, chunk in enumerate(chunks):
        out[pl.ds(pl.multiple_of((place[0] ^ j) * per, 8), per), :] = chunk[...]


def finish(place, chunks):
    per, rows = chunks[0].shape
    topics = per * len(chunks)
    return pl.pallas_call(
        finish_kernel,
        in_specs=[pl.BlockSpec(memory_space=pltpu.SMEM)]
        + [pl.BlockSpec(memory_space=pltpu.VMEM)] * len(chunks),
        out_shape=jax.ShapeDtypeStruct((topics, rows), jnp.float32),
        compiler_params=pltpu.CompilerParams(vmem_limit_bytes=16 * MIB),
        name="finish",
    )(place, *chunks)


def spread(sent, axis):
    size = lax.axis_size(axis)
    held = {0: sent}
    for j in range(size - 2, 2, -2):
        held[j] = xor_send(sent, axis, j)
    held[1] = xor_send(sent, axis, 1)
    held[2] = xor_send(sent, axis, 2)
    for j in range(size - 2, 0, -2):
        held[j + 1] = xor_send(held[j], axis, 1)
    return [held[j] for j in range(size)]


def body(docs, w_in, w_out, doc_host, tiles, dst_block, src_block, tile_count, teleport):
    hosts = teleport.shape[0]
    slots, block, _ = tiles.shape
    parts, split = lax.axis_size("hst"), lax.axis_size("doc")
    blocks = hosts // block
    part = lax.axis_index("hst").astype(jnp.int32).reshape(1)
    place = lax.axis_index("doc").astype(jnp.int32).reshape(1)
    labels = [label.reshape(1, -1) for label in (src_block, dst_block, tile_count)]

    near = xor_send(tiles, "doc", 1)
    cut = 3 * slots // 4
    early, late = tiles[:cut], tiles[cut:]
    far = {j: [xor_send(early, "doc", j)] for j in range(2, split, 2)}
    degrees = column_sums(src_block, tile_count, tiles, parts, blocks)
    degrees = lax.all_to_all(degrees, "hst", split_axis=0, concat_axis=0, tiled=True)
    sums = documents(docs, w_in, w_out, doc_host, hosts, split, place, part, degrees, labels)
    sums = [sums[0]] + [xor_send(sums[j], "doc", j) for j in range(1, split)]
    for j in range(2, split, 2):
        far[j][0] = after(far[j][0], sums[1:])
        far[j + 1] = [xor_send(far[j][0], "doc", 1)]
    sent, tele, inverse, meta, late, near = start_values(teleport, sums, block, [late, near])
    for j in range(2, split, 2):
        far[j].append(xor_send(late, "doc", j))
    for step in range(HOPS):
        first, last = step == 0, step == HOPS - 1
        shards = spread(sent, "hst")
        if first:
            for j in range(2, split, 2):
                far[j][1] = after(far[j][1], shards[1:])
                far[j + 1].append(xor_send(far[j][1], "doc", 1))
            sets = [[tiles], [near]] + [far[j] for j in range(2, split)]
        outs = hop(first, last, meta, part, place, shards, sets, tele, inverse)
        sent = outs[0]
        if first:
            tele = outs[1]
    chunks = [outs[0]] + [xor_send(outs[j], "doc", j) for j in range(1, split)]
    return finish(place, chunks).T


def solution(mesh):
    placed = (
        P(("hst", "doc"), None),
        P(),
        P(),
        P(("hst", "doc")),
        P(("hst", "doc"), None, None),
        P(("hst", "doc")),
        P(("hst", "doc")),
        P(("hst", "doc")),
        P("hst"),
    )
    return jax.shard_map(
        body, mesh=mesh, in_specs=placed, out_specs=P(("hst", "doc"), None), check_vma=False
    )
```

```python
import functools

import jax
import jax.numpy as jnp
from jax import lax
from jax.experimental import pallas as pl
from jax.experimental.pallas import tpu as pltpu
from jax.sharding import PartitionSpec as P

HOPS = 3
LABELS = 3
DIGITS = 4
DOC_BLOCK = 1024
TILE_GROUP = 16
HOP_MIB = 16
LIFT = 2.0**64
NT = (((1,), (1,)), ((), ()))
MIB = 1 << 20


def xor_send(value, axis, step):
    size = lax.axis_size(axis)
    return lax.ppermute(value, axis, [(i, i ^ step) for i in range(size)])


def column_sum_kernel(source, count, tiles, out, total):
    step = pl.program_id(0)
    parts, rows, _ = out.shape

    @pl.when(step == 0)
    def _():
        total[...] = jnp.zeros_like(total)

    for i in range(TILE_GROUP):
        k = step * TILE_GROUP + i
        row = jnp.where(k < count[0], source[k], parts * rows)
        part = jnp.sum(tiles[i].astype(jnp.float32), axis=0, keepdims=True)
        total[pl.ds(row, 1), :] += part

    @pl.when(step == pl.num_programs(0) - 1)
    def _():
        for j in range(parts):
            out[j] = total[j * rows : (j + 1) * rows, :]


def column_sums(source, count, tiles, parts, rows):
    slots, block, _ = tiles.shape
    shape = (parts, rows, block)
    return pl.pallas_call(
        column_sum_kernel,
        grid_spec=pltpu.PrefetchScalarGridSpec(
            num_scalar_prefetch=2,
            grid=(slots // TILE_GROUP,),
            in_specs=[pl.BlockSpec((TILE_GROUP, block, block), lambda i, s, c: (i, 0, 0))],
            out_specs=pl.BlockSpec(shape, lambda i, s, c: (0, 0, 0)),
            scratch_shapes=[pltpu.VMEM((parts * rows + 8, block), jnp.float32)],
        ),
        out_shape=jax.ShapeDtypeStruct(shape, jnp.float32),
        compiler_params=pltpu.CompilerParams(vmem_limit_bytes=16 * MIB),
        cost_estimate=pl.CostEstimate(
            flops=tiles.size, bytes_accessed=tiles.size * 2, transcendentals=0
        ),
        name="column_sums",
    )(source, count, tiles)


def block_topics(docs, w_in, w_out_t, host, width):
    hidden = jax.nn.gelu(
        jnp.dot(docs[...], w_in[...], preferred_element_type=jnp.float32), approximate=True
    ).astype(jnp.bfloat16)
    logits = lax.dot_general(w_out_t[...], hidden, NT, preferred_element_type=jnp.float32)
    powers = jnp.exp(logits - jnp.max(logits, axis=0, keepdims=True))
    probs = powers * (1.0 / jnp.sum(powers, axis=0, keepdims=True))
    high = probs.astype(jnp.bfloat16)
    low = (probs - high.astype(jnp.float32)).astype(jnp.bfloat16)
    index = host[0]
    digit = index // width
    within = index - digit * width
    picks = [jnp.where(digit == j, 1.0, 0.0).astype(jnp.bfloat16) for j in range(DIGITS)]
    left = jnp.concatenate([high * p for p in picks] + [low * p for p in picks], axis=0)
    places = lax.broadcasted_iota(jnp.int32, (width, index.shape[1]), 0)
    right = jnp.where(places == within, 1.0, 0.0).astype(jnp.bfloat16)
    return lax.dot_general(left, right, NT, preferred_element_type=jnp.float32)


def documents_kernel(place, part, docs, w_in, w_out_t, host, degrees, *rest):
    labels, outs, total = rest[:LABELS], rest[LABELS:-1], rest[-1]
    step = pl.program_id(0)
    topics = w_out_t.shape[0]
    width = total.shape[1]
    added = block_topics(docs, w_in, w_out_t, host, width)

    @pl.when(step == 0)
    def _():
        total[...] = added

    @pl.when(step > 0)
    def _():
        total[...] += added

    @pl.when(step == pl.num_programs(0) - 1)
    def _():
        per = outs[0].shape[0]
        hosts = DIGITS * width
        degree = sum(degrees[j] for j in range(1, degrees.shape[0])) + degrees[0]
        blocks, block = degree.shape
        wide = hosts + blocks // per * block
        for j, out in enumerate(outs):
            chunk = (place[0] ^ j) * per
            for d in range(DIGITS):
                first = pl.ds(pl.multiple_of(d * topics + chunk, 8), per)
                second = pl.ds(pl.multiple_of((DIGITS + d) * topics + chunk, 8), per)
                out[:, d * width : (d + 1) * width] = total[first, :] + total[second, :]
            for c in range(blocks // per):
                cols = slice(hosts + c * block, hosts + (c + 1) * block)
                out[:, cols] = degree[c * per : (c + 1) * per, :]
            out[:, wide:] = jnp.zeros((per, block), jnp.float32)
            for r, label in enumerate(labels):
                out[r : r + 1, wide : wide + label.shape[1]] = label[...].astype(jnp.float32)


def documents(docs, w_in, w_out, doc_host, hosts, split, place, part, degrees, labels):
    count, depth = docs.shape
    hid, topics = w_out.shape
    per = topics // split
    width = hosts // DIGITS
    steps = count // DOC_BLOCK
    shape = (per, hosts + hosts // per + degrees.shape[2])
    return pl.pallas_call(
        documents_kernel,
        grid_spec=pltpu.PrefetchScalarGridSpec(
            num_scalar_prefetch=2,
            grid=(steps,),
            in_specs=[
                pl.BlockSpec((DOC_BLOCK, depth), lambda i, *p: (i, 0)),
                pl.BlockSpec((depth, hid), lambda i, *p: (0, 0)),
                pl.BlockSpec((topics, hid), lambda i, *p: (0, 0)),
                pl.BlockSpec((1, 1, DOC_BLOCK), lambda i, *p: (i, 0, 0)),
                pl.BlockSpec(degrees.shape, lambda i, *p: (0, 0, 0)),
            ]
            + [pl.BlockSpec(label.shape, lambda i, *p: (0, 0)) for label in labels],
            out_specs=[pl.BlockSpec(shape, lambda i, *p: (0, 0))] * split,
            scratch_shapes=[pltpu.VMEM((2 * DIGITS * topics, width), jnp.float32)],
        ),
        out_shape=[jax.ShapeDtypeStruct(shape, jnp.float32)] * split,
        compiler_params=pltpu.CompilerParams(vmem_limit_bytes=48 * MIB),
        cost_estimate=pl.CostEstimate(
            flops=2 * count * (depth * hid + hid * topics + 2 * topics * hosts),
            bytes_accessed=docs.size * 2,
            transcendentals=count * (hid + topics),
        ),
        name="documents",
    )(place, part, docs, w_in, w_out.T, doc_host.reshape(steps, 1, DOC_BLOCK), degrees, *labels)


def start_kernel(held, teleport, *rest):
    sums, rest = rest[: len(rest) - 2 * held - 4], rest[len(rest) - held - 4 :]
    sent, start, inverse, meta = rest[:4]
    per, hosts = start.shape
    blocks, block = teleport.shape
    member = teleport[...].astype(jnp.float32) * LIFT
    mass = jnp.zeros((per, 1), jnp.float32)
    tail = slice(hosts, hosts + hosts // per)
    packed = 1.0 / jnp.maximum(sum(s[:, tail] for s in sums[1:]) + sums[0][:, tail], 1.0)
    for c in range(blocks // per):
        inverse[c * per : (c + 1) * per, :] = packed[:, c * block : (c + 1) * block]
    for j, s in enumerate(sums):
        meta[j * LABELS : (j + 1) * LABELS, :] = s[:LABELS, tail.stop :].astype(jnp.int32)
    for b in range(blocks):
        cols = slice(b * block, (b + 1) * block)
        value = sum(s[:, cols] for s in sums[1:]) + sums[0][:, cols]
        value = value * member[b : b + 1, :]
        start[:, cols] = value
        sent[:, cols] = (value * inverse[b : b + 1, :]).astype(jnp.bfloat16)
        mass = mass + jnp.sum(value, axis=1, keepdims=True)
    lane = lax.broadcasted_iota(jnp.int32, (per, block), 1)
    first = mass.astype(jnp.bfloat16).astype(jnp.float32)
    second = (mass - first).astype(jnp.bfloat16).astype(jnp.float32)
    third = mass - first - second
    pieces = jnp.where(
        lane == 0, first, jnp.where(lane == 1, second, jnp.where(lane == 2, third, 0.0))
    )
    sent[:, blocks * block :] = pieces.astype(jnp.bfloat16)


def start_values(teleport, sums, block, held):
    per, _ = sums[0].shape
    hosts = teleport.shape[0]
    vmem = pl.BlockSpec(memory_space=pltpu.VMEM)
    keep = pl.BlockSpec(memory_space=pl.ANY)
    return pl.pallas_call(
        functools.partial(start_kernel, len(held)),
        in_specs=[vmem] * (1 + len(sums)) + [keep] * len(held),
        out_specs=[vmem] * 4 + [keep] * len(held),
        out_shape=[
            jax.ShapeDtypeStruct((per, hosts + block), jnp.bfloat16),
            jax.ShapeDtypeStruct((per, hosts), jnp.float32),
            jax.ShapeDtypeStruct((hosts // block, block), jnp.float32),
            jax.ShapeDtypeStruct((len(sums) * LABELS, block), jnp.int32),
        ]
        + [jax.ShapeDtypeStruct(array.shape, array.dtype) for array in held],
        input_output_aliases={1 + len(sums) + i: 4 + i for i in range(len(held))},
        compiler_params=pltpu.CompilerParams(vmem_limit_bytes=16 * MIB),
        name="start_values",
    )(teleport.reshape(hosts // block, block), *sums, *held)


def take_kernel(begin, source, out, sems):
    size = out.shape[0] // sems.shape[0]
    copies = []
    for i in range(sems.shape[0]):
        rows = pl.ds(begin + i * size, size)
        copies.append(
            pltpu.make_async_copy(source.at[rows], out.at[pl.ds(i * size, size)], sems.at[i])
        )
    for copy in copies:
        copy.start()
    for copy in copies:
        copy.wait()


def take(tiles, begin, end):
    keep = pl.BlockSpec(memory_space=pl.ANY)
    return pl.pallas_call(
        functools.partial(take_kernel, begin),
        in_specs=[keep],
        out_specs=keep,
        out_shape=jax.ShapeDtypeStruct((end - begin, *tiles.shape[1:]), tiles.dtype),
        scratch_shapes=[pltpu.SemaphoreType.DMA((4,))],
        compiler_params=pltpu.CompilerParams(vmem_limit_bytes=MIB),
        name="take",
    )(tiles)


def after_kernel(*refs):
    del refs


def after(value, ready):
    keep = pl.BlockSpec(memory_space=pl.ANY)
    return pl.pallas_call(
        after_kernel,
        in_specs=[keep] * (1 + len(ready)),
        out_specs=keep,
        out_shape=jax.ShapeDtypeStruct(value.shape, value.dtype),
        input_output_aliases={0: 0},
        compiler_params=pltpu.CompilerParams(vmem_limit_bytes=MIB),
        name="after",
    )(value, *ready)


def hop_kernel(first, last, parts, spans, scale, meta, part, place, *rest):
    shards, rest = rest[:parts], rest[parts:]
    chunks, rest = rest[: len(spans)], rest[len(spans) :]
    (tele, inverse), outs, (slabs, inflow) = rest[:2], rest[2:-2], rest[-2:]
    blocks, per, block = inflow.shape

    inflow[...] = jnp.zeros_like(inflow)
    slabs[parts * blocks] = jnp.zeros(slabs.shape[1:], slabs.dtype)
    for j, shard in enumerate(shards):
        for b in range(blocks):
            slabs[j * blocks + b] = shard[:, b * block : (b + 1) * block]

    split = meta.shape[0] // LABELS
    empty = jnp.zeros((per, block), jnp.bfloat16)
    counts = [meta[q * LABELS + 2, 0] for q in range(split)]
    most = functools.reduce(jnp.maximum, counts)
    edges = sorted({begin for _, begin in spans})
    edges.append(edges[-1] + chunks[-1].shape[0])

    def quads(q, tiles, begin, at):
        for c in range(0, TILE_GROUP, 4):
            held, quad, into = [], [], []
            for i in range(c, c + 4):
                k = begin + at + i
                source = meta[q * LABELS, k] ^ (part[0] * blocks)
                held.append(slabs[jnp.where(k < counts[q], source, parts * blocks)])
                quad.append(tiles[at + i])
                into.append(meta[q * LABELS + 1, k])
            left = jnp.concatenate(
                [
                    jnp.concatenate([held[0], held[1], empty, empty], axis=0),
                    jnp.concatenate([empty, empty, held[2], held[3]], axis=0),
                ],
                axis=1,
            )
            right = jnp.concatenate(
                [jnp.concatenate(quad[:2], axis=0), jnp.concatenate(quad[2:], axis=0)], axis=1
            )
            both = lax.dot_general(left, right, NT, preferred_element_type=jnp.float32)
            for i in range(4):
                side = (i % 2) * block
                inflow[into[i]] += both[i * per : (i + 1) * per, side : side + block]

    for first_slot, end_slot in zip(edges[:-1], edges[1:]):
        groups = jnp.clip(most - first_slot, 0, end_slot - first_slot) + (TILE_GROUP - 1)

        def group(step, carry):
            for q in range(split):
                for tiles, (owner, begin) in zip(chunks, spans):
                    if owner == q and begin <= first_slot < begin + tiles.shape[0]:
                        quads(q, tiles, begin, first_slot - begin + step * TILE_GROUP)
            return carry

        lax.fori_loop(0, groups // TILE_GROUP, group, 0)

    if first:
        tail = sum(s[:, blocks * block :].astype(jnp.float32) for s in shards)
        mass = jnp.sum(tail, axis=1, keepdims=True)
    for b in range(blocks):
        cols = slice(b * block, (b + 1) * block)
        own = tele[:, cols]
        state = 0.85 * inflow[b] + 0.15 * own
        if first:
            state = state / mass
            outs[1][:, cols] = own / mass
        if last:
            inflow[b] = state * scale
        else:
            outs[0][:, cols] = (state * inverse[b : b + 1, :]).astype(jnp.bfloat16)
    if last:
        count = outs[0].shape[1] // block
        for j, out in enumerate(outs):
            start = (place[0] ^ j) * count
            for i in range(count):
                out[:, i * block : (i + 1) * block] = inflow[start + i]


def hop(first, last, meta, part, place, shards, sets, tele, inverse):
    per, hosts = tele.shape
    slots = sum(chunk.shape[0] for chunk in sets[0])
    block = sets[0][0].shape[1]
    blocks = hosts // block
    parts, split = len(shards), len(sets)
    chunks, spans = [], []
    for q, held in enumerate(sets):
        begin = 0
        for chunk in held:
            chunks.append(chunk)
            spans.append((q, begin))
            begin += chunk.shape[0]
    if last:
        out_shape = [jax.ShapeDtypeStruct((per, hosts // split), jnp.float32)] * split
    else:
        out_shape = [jax.ShapeDtypeStruct((per, hosts), jnp.bfloat16)]
        if first:
            out_shape.append(jax.ShapeDtypeStruct((per, hosts), jnp.float32))
    smem = pl.BlockSpec(memory_space=pltpu.SMEM)
    vmem = pl.BlockSpec(memory_space=pltpu.VMEM)
    return pl.pallas_call(
        functools.partial(hop_kernel, first, last, parts, spans, float(parts * hosts)),
        in_specs=[smem] * 3 + [vmem] * (parts + len(chunks) + 2),
        out_specs=[vmem] * len(out_shape),
        scratch_shapes=[
            pltpu.VMEM((parts * blocks + 1, per, block), jnp.bfloat16),
            pltpu.VMEM((blocks, per, block), jnp.float32),
        ],
        out_shape=out_shape,
        compiler_params=pltpu.CompilerParams(vmem_limit_bytes=HOP_MIB * MIB),
        cost_estimate=pl.CostEstimate(
            flops=2 * split * slots * block * block * per,
            bytes_accessed=split * slots * block * block * 2,
            transcendentals=0,
        ),
        name="hop",
    )(meta, part, place, *shards, *chunks, tele, inverse)


def finish_kernel(place, *rest):
    chunks, out = rest[:-1], rest[-1]
    per = chunks[0].shape[0]
    for j, chunk in enumerate(chunks):
        out[pl.ds(pl.multiple_of((place[0] ^ j) * per, 8), per), :] = chunk[...]


def finish(place, chunks):
    per, rows = chunks[0].shape
    topics = per * len(chunks)
    return pl.pallas_call(
        finish_kernel,
        in_specs=[pl.BlockSpec(memory_space=pltpu.SMEM)]
        + [pl.BlockSpec(memory_space=pltpu.VMEM)] * len(chunks),
        out_shape=jax.ShapeDtypeStruct((topics, rows), jnp.float32),
        compiler_params=pltpu.CompilerParams(vmem_limit_bytes=16 * MIB),
        name="finish",
    )(place, *chunks)


def spread(sent, axis):
    size = lax.axis_size(axis)
    held = {0: sent}
    for j in range(2, size, 2):
        held[j] = xor_send(sent, axis, j)
    held[1] = xor_send(sent, axis, 1)
    for j in range(2, size, 2):
        held[j + 1] = xor_send(held[j], axis, 1)
    return [held[j] for j in range(size)]


def body(docs, w_in, w_out, doc_host, tiles, dst_block, src_block, tile_count, teleport):
    hosts = teleport.shape[0]
    slots, block, _ = tiles.shape
    parts, split = lax.axis_size("hst"), lax.axis_size("doc")
    blocks = hosts // block
    part = lax.axis_index("hst").astype(jnp.int32).reshape(1)
    place = lax.axis_index("doc").astype(jnp.int32).reshape(1)
    labels = [label.reshape(1, -1) for label in (src_block, dst_block, tile_count)]

    near = xor_send(tiles, "doc", 1)
    cut = 3 * slots // 4
    early, late = take(tiles, 0, cut), take(tiles, cut, slots)
    far = {j: [xor_send(early, "doc", j)] for j in range(2, split, 2)}
    degrees = column_sums(src_block, tile_count, tiles, parts, blocks)
    degrees = lax.all_to_all(degrees, "hst", split_axis=0, concat_axis=0, tiled=True)
    sums = documents(docs, w_in, w_out, doc_host, hosts, split, place, part, degrees, labels)
    sums = [sums[0]] + [xor_send(sums[j], "doc", j) for j in range(1, split)]
    for j in range(2, split, 2):
        far[j][0] = after(far[j][0], sums[1:])
        far[j + 1] = [xor_send(far[j][0], "doc", 1)]
    sent, tele, inverse, meta, late, near = start_values(teleport, sums, block, [late, near])
    for j in range(2, split, 2):
        far[j].append(xor_send(late, "doc", j))
    for step in range(HOPS):
        first, last = step == 0, step == HOPS - 1
        shards = spread(sent, "hst")
        if first:
            for j in range(2, split, 2):
                far[j][1] = after(far[j][1], shards[1:])
                far[j + 1].append(xor_send(far[j][1], "doc", 1))
            sets = [[tiles], [near]] + [far[j] for j in range(2, split)]
        outs = hop(first, last, meta, part, place, shards, sets, tele, inverse)
        sent = outs[0]
        if first:
            tele = outs[1]
    chunks = [outs[0]] + [xor_send(outs[j], "doc", j) for j in range(1, split)]
    return finish(place, chunks).T


def solution(mesh):
    placed = (
        P(("hst", "doc"), None),
        P(),
        P(),
        P(("hst", "doc")),
        P(("hst", "doc"), None, None),
        P(("hst", "doc")),
        P(("hst", "doc")),
        P(("hst", "doc")),
        P("hst"),
    )
    return jax.shard_map(
        body, mesh=mesh, in_specs=placed, out_specs=P(("hst", "doc"), None), check_vma=False
    )
```

```python
import functools

import jax
import jax.numpy as jnp
from jax import lax
from jax.experimental import pallas as pl
from jax.experimental.pallas import tpu as pltpu
from jax.sharding import PartitionSpec as P

HOPS = 3
LABELS = 3
DIGITS = 4
DOC_BLOCK = 1024
TILE_GROUP = 8
SUM_GROUP = 16
HOP_MIB = 16
LIFT = 2.0**64
NT = (((1,), (1,)), ((), ()))
MIB = 1 << 20


def xor_send(value, axis, step):
    size = lax.axis_size(axis)
    return lax.ppermute(value, axis, [(i, i ^ step) for i in range(size)])


def column_sum_kernel(source, count, tiles, out, total):
    step = pl.program_id(0)
    parts, rows, _ = out.shape

    @pl.when(step == 0)
    def _():
        total[...] = jnp.zeros_like(total)

    for i in range(SUM_GROUP):
        k = step * SUM_GROUP + i
        row = jnp.where(k < count[0], source[k], parts * rows)
        part = jnp.sum(tiles[i].astype(jnp.float32), axis=0, keepdims=True)
        total[pl.ds(row, 1), :] += part

    @pl.when(step == pl.num_programs(0) - 1)
    def _():
        for j in range(parts):
            out[j] = total[j * rows : (j + 1) * rows, :]


def column_sums(source, count, tiles, parts, rows):
    slots, block, _ = tiles.shape
    shape = (parts, rows, block)
    return pl.pallas_call(
        column_sum_kernel,
        grid_spec=pltpu.PrefetchScalarGridSpec(
            num_scalar_prefetch=2,
            grid=(slots // SUM_GROUP,),
            in_specs=[pl.BlockSpec((SUM_GROUP, block, block), lambda i, s, c: (i, 0, 0))],
            out_specs=pl.BlockSpec(shape, lambda i, s, c: (0, 0, 0)),
            scratch_shapes=[pltpu.VMEM((parts * rows + 8, block), jnp.float32)],
        ),
        out_shape=jax.ShapeDtypeStruct(shape, jnp.float32),
        compiler_params=pltpu.CompilerParams(vmem_limit_bytes=16 * MIB),
        cost_estimate=pl.CostEstimate(
            flops=tiles.size, bytes_accessed=tiles.size * 2, transcendentals=0
        ),
        name="column_sums",
    )(source, count, tiles)


def block_topics(docs, w_in, w_out_t, host, width):
    hidden = jax.nn.gelu(
        jnp.dot(docs[...], w_in[...], preferred_element_type=jnp.float32), approximate=True
    ).astype(jnp.bfloat16)
    logits = lax.dot_general(w_out_t[...], hidden, NT, preferred_element_type=jnp.float32)
    powers = jnp.exp(logits - jnp.max(logits, axis=0, keepdims=True))
    probs = powers * (1.0 / jnp.sum(powers, axis=0, keepdims=True))
    high = probs.astype(jnp.bfloat16)
    low = (probs - high.astype(jnp.float32)).astype(jnp.bfloat16)
    index = host[0]
    digit = index // width
    within = index - digit * width
    picks = [jnp.where(digit == j, 1.0, 0.0).astype(jnp.bfloat16) for j in range(DIGITS)]
    left = jnp.concatenate([high * p for p in picks] + [low * p for p in picks], axis=0)
    places = lax.broadcasted_iota(jnp.int32, (width, index.shape[1]), 0)
    right = jnp.where(places == within, 1.0, 0.0).astype(jnp.bfloat16)
    return lax.dot_general(left, right, NT, preferred_element_type=jnp.float32)


def documents_kernel(place, part, docs, w_in, w_out_t, host, degrees, *rest):
    labels, outs, total = rest[:LABELS], rest[LABELS:-1], rest[-1]
    step = pl.program_id(0)
    topics = w_out_t.shape[0]
    width = total.shape[1]
    added = block_topics(docs, w_in, w_out_t, host, width)

    @pl.when(step == 0)
    def _():
        total[...] = added

    @pl.when(step > 0)
    def _():
        total[...] += added

    @pl.when(step == pl.num_programs(0) - 1)
    def _():
        per = outs[0].shape[0]
        hosts = DIGITS * width
        degree = sum(degrees[j] for j in range(1, degrees.shape[0])) + degrees[0]
        blocks, block = degree.shape
        wide = hosts + blocks // per * block
        for j, out in enumerate(outs):
            chunk = (place[0] ^ j) * per
            for d in range(DIGITS):
                first = pl.ds(pl.multiple_of(d * topics + chunk, 8), per)
                second = pl.ds(pl.multiple_of((DIGITS + d) * topics + chunk, 8), per)
                out[:, d * width : (d + 1) * width] = total[first, :] + total[second, :]
            for c in range(blocks // per):
                cols = slice(hosts + c * block, hosts + (c + 1) * block)
                out[:, cols] = degree[c * per : (c + 1) * per, :]
            out[:, wide:] = jnp.zeros((per, block), jnp.float32)
            for r, label in enumerate(labels):
                out[r : r + 1, wide : wide + label.shape[1]] = label[...].astype(jnp.float32)


def documents(docs, w_in, w_out, doc_host, hosts, split, place, part, degrees, labels):
    count, depth = docs.shape
    hid, topics = w_out.shape
    per = topics // split
    width = hosts // DIGITS
    steps = count // DOC_BLOCK
    shape = (per, hosts + hosts // per + degrees.shape[2])
    return pl.pallas_call(
        documents_kernel,
        grid_spec=pltpu.PrefetchScalarGridSpec(
            num_scalar_prefetch=2,
            grid=(steps,),
            in_specs=[
                pl.BlockSpec((DOC_BLOCK, depth), lambda i, *p: (i, 0)),
                pl.BlockSpec((depth, hid), lambda i, *p: (0, 0)),
                pl.BlockSpec((topics, hid), lambda i, *p: (0, 0)),
                pl.BlockSpec((1, 1, DOC_BLOCK), lambda i, *p: (i, 0, 0)),
                pl.BlockSpec(degrees.shape, lambda i, *p: (0, 0, 0)),
            ]
            + [pl.BlockSpec(label.shape, lambda i, *p: (0, 0)) for label in labels],
            out_specs=[pl.BlockSpec(shape, lambda i, *p: (0, 0))] * split,
            scratch_shapes=[pltpu.VMEM((2 * DIGITS * topics, width), jnp.float32)],
        ),
        out_shape=[jax.ShapeDtypeStruct(shape, jnp.float32)] * split,
        compiler_params=pltpu.CompilerParams(vmem_limit_bytes=48 * MIB),
        cost_estimate=pl.CostEstimate(
            flops=2 * count * (depth * hid + hid * topics + 2 * topics * hosts),
            bytes_accessed=docs.size * 2,
            transcendentals=count * (hid + topics),
        ),
        name="documents",
    )(place, part, docs, w_in, w_out.T, doc_host.reshape(steps, 1, DOC_BLOCK), degrees, *labels)


def start_kernel(held, teleport, *rest):
    sums, rest = rest[: len(rest) - 2 * held - 4], rest[len(rest) - held - 4 :]
    sent, start, inverse, meta = rest[:4]
    per, hosts = start.shape
    blocks, block = teleport.shape
    member = teleport[...].astype(jnp.float32) * LIFT
    mass = jnp.zeros((per, 1), jnp.float32)
    tail = slice(hosts, hosts + hosts // per)
    packed = 1.0 / jnp.maximum(sum(s[:, tail] for s in sums[1:]) + sums[0][:, tail], 1.0)
    for c in range(blocks // per):
        inverse[c * per : (c + 1) * per, :] = packed[:, c * block : (c + 1) * block]
    for j, s in enumerate(sums):
        meta[j * LABELS : (j + 1) * LABELS, :] = s[:LABELS, tail.stop :].astype(jnp.int32)
    for b in range(blocks):
        cols = slice(b * block, (b + 1) * block)
        value = sum(s[:, cols] for s in sums[1:]) + sums[0][:, cols]
        value = value * member[b : b + 1, :]
        start[:, cols] = value
        sent[:, cols] = (value * inverse[b : b + 1, :]).astype(jnp.bfloat16)
        mass = mass + jnp.sum(value, axis=1, keepdims=True)
    lane = lax.broadcasted_iota(jnp.int32, (per, block), 1)
    first = mass.astype(jnp.bfloat16).astype(jnp.float32)
    second = (mass - first).astype(jnp.bfloat16).astype(jnp.float32)
    third = mass - first - second
    pieces = jnp.where(
        lane == 0, first, jnp.where(lane == 1, second, jnp.where(lane == 2, third, 0.0))
    )
    sent[:, blocks * block :] = pieces.astype(jnp.bfloat16)


def start_values(teleport, sums, block, held):
    per, _ = sums[0].shape
    hosts = teleport.shape[0]
    vmem = pl.BlockSpec(memory_space=pltpu.VMEM)
    keep = pl.BlockSpec(memory_space=pl.ANY)
    return pl.pallas_call(
        functools.partial(start_kernel, len(held)),
        in_specs=[vmem] * (1 + len(sums)) + [keep] * len(held),
        out_specs=[vmem] * 4 + [keep] * len(held),
        out_shape=[
            jax.ShapeDtypeStruct((per, hosts + block), jnp.bfloat16),
            jax.ShapeDtypeStruct((per, hosts), jnp.float32),
            jax.ShapeDtypeStruct((hosts // block, block), jnp.float32),
            jax.ShapeDtypeStruct((len(sums) * LABELS, block), jnp.int32),
        ]
        + [jax.ShapeDtypeStruct(array.shape, array.dtype) for array in held],
        input_output_aliases={1 + len(sums) + i: 4 + i for i in range(len(held))},
        compiler_params=pltpu.CompilerParams(vmem_limit_bytes=16 * MIB),
        name="start_values",
    )(teleport.reshape(hosts // block, block), *sums, *held)


def take_kernel(source, early, late, sems):
    copies = []
    begin = 0
    for out in (early, late):
        size = out.shape[0] // 4
        for i in range(4):
            rows = pl.ds(begin + i * size, size)
            sem = sems.at[len(copies)]
            copies.append(
                pltpu.make_async_copy(source.at[rows], out.at[pl.ds(i * size, size)], sem)
            )
        begin += out.shape[0]
    for copy in copies:
        copy.start()
    for copy in copies:
        copy.wait()


def take(tiles, cut):
    slots, *tile = tiles.shape
    keep = pl.BlockSpec(memory_space=pl.ANY)
    return pl.pallas_call(
        take_kernel,
        in_specs=[keep],
        out_specs=[keep, keep],
        out_shape=[
            jax.ShapeDtypeStruct((cut, *tile), tiles.dtype),
            jax.ShapeDtypeStruct((slots - cut, *tile), tiles.dtype),
        ],
        scratch_shapes=[pltpu.SemaphoreType.DMA((8,))],
        compiler_params=pltpu.CompilerParams(vmem_limit_bytes=MIB),
        name="take",
    )(tiles)


def after_kernel(*refs):
    del refs


def after(value, ready):
    keep = pl.BlockSpec(memory_space=pl.ANY)
    return pl.pallas_call(
        after_kernel,
        in_specs=[keep] * (1 + len(ready)),
        out_specs=keep,
        out_shape=jax.ShapeDtypeStruct(value.shape, value.dtype),
        input_output_aliases={0: 0},
        compiler_params=pltpu.CompilerParams(vmem_limit_bytes=MIB),
        name="after",
    )(value, *ready)


def hop_kernel(first, last, parts, spans, scale, meta, part, place, *rest):
    shards, rest = rest[:parts], rest[parts:]
    chunks, rest = rest[: len(spans)], rest[len(spans) :]
    (tele, inverse), outs, (slabs, inflow) = rest[:2], rest[2:-2], rest[-2:]
    blocks, per, block = inflow.shape

    inflow[...] = jnp.zeros_like(inflow)
    slabs[parts * blocks] = jnp.zeros(slabs.shape[1:], slabs.dtype)
    for j, shard in enumerate(shards):
        for b in range(blocks):
            slabs[j * blocks + b] = shard[:, b * block : (b + 1) * block]

    split = meta.shape[0] // LABELS
    empty = jnp.zeros((per, block), jnp.bfloat16)
    counts = [meta[q * LABELS + 2, 0] for q in range(split)]
    most = functools.reduce(jnp.maximum, counts)
    edges = sorted({begin for _, begin in spans})
    edges.append(edges[-1] + chunks[-1].shape[0])

    def quads(q, tiles, begin, at):
        for c in range(0, TILE_GROUP, 4):
            held, quad, into = [], [], []
            for i in range(c, c + 4):
                k = begin + at + i
                source = meta[q * LABELS, k] ^ (part[0] * blocks)
                held.append(slabs[jnp.where(k < counts[q], source, parts * blocks)])
                quad.append(tiles[at + i])
                into.append(meta[q * LABELS + 1, k])
            left = jnp.concatenate(
                [
                    jnp.concatenate([held[0], held[1], empty, empty], axis=0),
                    jnp.concatenate([empty, empty, held[2], held[3]], axis=0),
                ],
                axis=1,
            )
            right = jnp.concatenate(
                [jnp.concatenate(quad[:2], axis=0), jnp.concatenate(quad[2:], axis=0)], axis=1
            )
            both = lax.dot_general(left, right, NT, preferred_element_type=jnp.float32)
            for i in range(4):
                side = (i % 2) * block
                inflow[into[i]] += both[i * per : (i + 1) * per, side : side + block]

    for first_slot, end_slot in zip(edges[:-1], edges[1:]):
        groups = jnp.clip(most - first_slot, 0, end_slot - first_slot) + (TILE_GROUP - 1)

        def group(step, carry):
            for q in range(split):
                for tiles, (owner, begin) in zip(chunks, spans):
                    if owner == q and begin <= first_slot < begin + tiles.shape[0]:
                        quads(q, tiles, begin, first_slot - begin + step * TILE_GROUP)
            return carry

        lax.fori_loop(0, groups // TILE_GROUP, group, 0)

    if first:
        tail = sum(s[:, blocks * block :].astype(jnp.float32) for s in shards)
        mass = jnp.sum(tail, axis=1, keepdims=True)
    for b in range(blocks):
        cols = slice(b * block, (b + 1) * block)
        own = tele[:, cols]
        state = 0.85 * inflow[b] + 0.15 * own
        if first:
            state = state / mass
            outs[1][:, cols] = own / mass
        if last:
            inflow[b] = state * scale
        else:
            outs[0][:, cols] = (state * inverse[b : b + 1, :]).astype(jnp.bfloat16)
    if last:
        count = outs[0].shape[1] // block
        for j, out in enumerate(outs):
            start = (place[0] ^ j) * count
            for i in range(count):
                out[:, i * block : (i + 1) * block] = inflow[start + i]


def hop(first, last, meta, part, place, shards, sets, tele, inverse):
    per, hosts = tele.shape
    slots = sum(chunk.shape[0] for chunk in sets[0])
    block = sets[0][0].shape[1]
    blocks = hosts // block
    parts, split = len(shards), len(sets)
    chunks, spans = [], []
    for q, held in enumerate(sets):
        begin = 0
        for chunk in held:
            chunks.append(chunk)
            spans.append((q, begin))
            begin += chunk.shape[0]
    if last:
        out_shape = [jax.ShapeDtypeStruct((per, hosts // split), jnp.float32)] * split
    else:
        out_shape = [jax.ShapeDtypeStruct((per, hosts), jnp.bfloat16)]
        if first:
            out_shape.append(jax.ShapeDtypeStruct((per, hosts), jnp.float32))
    smem = pl.BlockSpec(memory_space=pltpu.SMEM)
    vmem = pl.BlockSpec(memory_space=pltpu.VMEM)
    return pl.pallas_call(
        functools.partial(hop_kernel, first, last, parts, spans, float(parts * hosts)),
        in_specs=[smem] * 3 + [vmem] * (parts + len(chunks) + 2),
        out_specs=[vmem] * len(out_shape),
        scratch_shapes=[
            pltpu.VMEM((parts * blocks + 1, per, block), jnp.bfloat16),
            pltpu.VMEM((blocks, per, block), jnp.float32),
        ],
        out_shape=out_shape,
        compiler_params=pltpu.CompilerParams(vmem_limit_bytes=HOP_MIB * MIB),
        cost_estimate=pl.CostEstimate(
            flops=2 * split * slots * block * block * per,
            bytes_accessed=split * slots * block * block * 2,
            transcendentals=0,
        ),
        name="hop",
    )(meta, part, place, *shards, *chunks, tele, inverse)


def finish_kernel(place, *rest):
    chunks, out = rest[:-1], rest[-1]
    per = chunks[0].shape[0]
    for j, chunk in enumerate(chunks):
        out[pl.ds(pl.multiple_of((place[0] ^ j) * per, 8), per), :] = chunk[...]


def finish(place, chunks):
    per, rows = chunks[0].shape
    topics = per * len(chunks)
    return pl.pallas_call(
        finish_kernel,
        in_specs=[pl.BlockSpec(memory_space=pltpu.SMEM)]
        + [pl.BlockSpec(memory_space=pltpu.VMEM)] * len(chunks),
        out_shape=jax.ShapeDtypeStruct((topics, rows), jnp.float32),
        compiler_params=pltpu.CompilerParams(vmem_limit_bytes=16 * MIB),
        name="finish",
    )(place, *chunks)


def spread(sent, axis):
    size = lax.axis_size(axis)
    held = {0: sent}
    for j in range(2, size, 2):
        held[j] = xor_send(sent, axis, j)
    held[1] = xor_send(sent, axis, 1)
    for j in range(2, size, 2):
        held[j + 1] = xor_send(held[j], axis, 1)
    return [held[j] for j in range(size)]


def body(docs, w_in, w_out, doc_host, tiles, dst_block, src_block, tile_count, teleport):
    hosts = teleport.shape[0]
    slots, block, _ = tiles.shape
    parts, split = lax.axis_size("hst"), lax.axis_size("doc")
    blocks = hosts // block
    part = lax.axis_index("hst").astype(jnp.int32).reshape(1)
    place = lax.axis_index("doc").astype(jnp.int32).reshape(1)
    labels = [label.reshape(1, -1) for label in (src_block, dst_block, tile_count)]

    near = xor_send(tiles, "doc", 1)
    cut = 5 * slots // 8
    early, late = take(tiles, cut)
    far = {j: [xor_send(early, "doc", j)] for j in range(2, split, 2)}
    degrees = column_sums(src_block, tile_count, tiles, parts, blocks)
    degrees = lax.all_to_all(degrees, "hst", split_axis=0, concat_axis=0, tiled=True)
    sums = documents(docs, w_in, w_out, doc_host, hosts, split, place, part, degrees, labels)
    sums = [sums[0]] + [xor_send(sums[j], "doc", j) for j in range(1, split)]
    for j in range(2, split, 2):
        far[j][0] = after(far[j][0], sums[1:])
        far[j + 1] = [xor_send(far[j][0], "doc", 1)]
    sent, tele, inverse, meta, late, near = start_values(teleport, sums, block, [late, near])
    for j in range(2, split, 2):
        far[j].append(xor_send(late, "doc", j))
    for step in range(HOPS):
        first, last = step == 0, step == HOPS - 1
        shards = spread(sent, "hst")
        if first:
            for j in range(2, split, 2):
                far[j][1] = after(far[j][1], shards[1:])
                far[j + 1].append(xor_send(far[j][1], "doc", 1))
            sets = [[tiles], [near]] + [far[j] for j in range(2, split)]
        outs = hop(first, last, meta, part, place, shards, sets, tele, inverse)
        sent = outs[0]
        if first:
            tele = outs[1]
    chunks = [outs[0]] + [xor_send(outs[j], "doc", j) for j in range(1, split)]
    return finish(place, chunks).T


def solution(mesh):
    placed = (
        P(("hst", "doc"), None),
        P(),
        P(),
        P(("hst", "doc")),
        P(("hst", "doc"), None, None),
        P(("hst", "doc")),
        P(("hst", "doc")),
        P(("hst", "doc")),
        P("hst"),
    )
    return jax.shard_map(
        body, mesh=mesh, in_specs=placed, out_specs=P(("hst", "doc"), None), check_vma=False
    )
```
